32 devices in a mesh: dp: 16 (over z, x, core), spk: 2 (over y).
Axes of the slice: x: 2, y: 2, z: 4, core: 2. Of those that a mesh axis runs over, the one named last changes fastest.
Arguments:
- spans: bfloat16 [512, 100, 64], P(('dp', 'spk')), may hold values from -6 to 6
- encoded: bfloat16 [25600, 64], P(('dp', 'spk')), may hold values from -6 to 6
- clip_lengths: int32 [16, 2, 3], P('dp'), may hold values from 1 to 12, 16 in all within a row
- clip_pads: int32 [16, 2, 3], P('dp'), may hold values from 0 to 49
- lstm_in: bfloat16 [2, 2, 2, 64, 512], replicated, may hold values from -0.75 to 0.75
- lstm_rec: bfloat16 [2, 2, 2, 128, 512], replicated, may hold values from -0.5 to 0.5
- lstm_bias: float32 [2, 2, 2, 512], replicated, may hold values from -3 to 3
- proj_weight: bfloat16 [2, 2, 256, 64], replicated, may hold values from -0.375 to 0.375
- proj_bias: float32 [2, 2, 64], replicated, may hold values from -3 to 3
- gln_gain: float32 [2, 2, 64], replicated, may hold values from 0.25 to 1.75
- gln_shift: float32 [2, 2, 64], replicated, may hold values from -3 to 3
- mask_weight: bfloat16 [2, 64, 64], P('spk'), may hold values from -0.75 to 0.75
- mask_bias: bfloat16 [2, 64], P('spk'), may hold values from -3 to 3
- dec_weight: bfloat16 [64, 16], replicated, may hold values from -0.75 to 0.75
- wave_grad: bfloat16 [2, 204800], P('spk', 'dp'), may hold values from -6 to 6
Outputs:
- waveforms: float32 [2, 204800], P('spk', 'dp')
- grad_spans: float32 [512, 100, 64], P(('dp', 'spk'))
- grad_lstm_in: float32 [2, 2, 2, 64, 512], replicated
- grad_lstm_rec: float32 [2, 2, 2, 128, 512], replicated
- grad_lstm_bias: float32 [2, 2, 2, 512], replicated
- grad_proj_weight: float32 [2, 2, 256, 64], replicated
- grad_proj_bias: float32 [2, 2, 64], replicated
- grad_gln_gain: float32 [2, 2, 64], replicated
- grad_gln_shift: float32 [2, 2, 64], replicated
- grad_mask_weight: float32 [2, 64, 64], P('spk')
- grad_mask_bias: float32 [2, 64], P('spk')
- grad_dec_weight: float32 [64, 16], replicated
The draws below stay inside these ranges and needn't reach their ends.
Inputs may be any that keep to these rules, and one draw needn't show every extreme that they name: `clip_lengths`: each device's 3 counts sum to 16, and on every device the longest is exactly 12.
All inputs are finite; a program needn't handle non-finite values.
Results may differ from the reference program's by a relative error of at most 0.013.
Values may be sent and summed in bfloat16 or wider, within the bound.
A program may use at most 192 MiB of HBM per device.

```python
import math
import jax
import jax.numpy as jnp
import numpy as np
from jax import lax

B = 64
N = 64
HID = 128
K = 100
KDEC = 16
SPK = 2
BLOCKS = 2
CLIPS = 3
CH_DEV = 16
HOP = 50
STRIDE = 8
LONGEST = 12
FR_DEV = 800
SPANS = 512
FRAMES = 25600
SAMPLES = 204800
N_DP = 16
N_SPK = 2


def with_ends(result, key, smallest, top_value):
    longest = result.shape.index(max(result.shape))
    spots = []
    for shift in (0, 1):
        where = [jax.random.randint(jax.random.fold_in(key, axis), (), 0, length) for axis, length in enumerate(result.shape)]
        where[longest] = (where[longest] + shift) % result.shape[longest]
        spots.append(tuple(where))
    return result.at[spots[0]].set(smallest).at[spots[1]].set(top_value)


def shard_levels(key, shape, cuts, smallest, largest):
    level, own = 1.0, jax.random.fold_in(key, 6)
    for position, parts in cuts:
        heights = jnp.exp(jax.random.uniform(jax.random.fold_in(own, position), (parts,), jnp.float32, smallest / len(cuts), largest / len(cuts)))
        level = level * jnp.repeat(heights, shape[position] // parts).reshape([-1 if axis == position else 1 for axis in range(len(shape))])
    return level


def profile(number_of, total, most, slope):
    weights = [(1 << 20) // math.isqrt(standing ** slope) + 1 for standing in range(2, number_of + 1)]
    spare, given = total - most - (number_of - 1), [1] * (number_of - 1)
    while spare > 0:
        candidates = [i for i in range(number_of - 1) if given[i] < most]
        mass, remaining = sum([weights[i] for i in candidates]), spare
        for i in candidates:
            extra = min(most - given[i], max(1, remaining * weights[i] // mass), spare)
            given[i] = given[i] + extra
            spare = spare - extra
    return np.array([most] + given)


def ragged_sizes(own_key, amount, total, most, skew):
    if amount == 2:
        one = jax.random.randint(own_key, (), max(1, total - most), min(most, total - 1) + 1)
        return jnp.stack([one, total - one])
    tallies = jnp.asarray(profile(amount, total, most, skew), jnp.int32)
    couples = (amount - 1) // 2
    giver, receiver = tallies[1:1 + 2 * couples:2], tallies[2:2 + 2 * couples:2]
    room = jnp.minimum(giver - 1, most - receiver)
    passed = jax.random.randint(jax.random.fold_in(own_key, 1), (couples,), 0, 1 << 20) % (room + 1)
    tallies = tallies.at[1:1 + 2 * couples:2].set(giver - passed).at[2:2 + 2 * couples:2].set(receiver + passed)
    return tallies[jax.random.permutation(jax.random.fold_in(own_key, 2), amount)]


def scatter_about(own_key, dims, spread, limit, shards=(), kind=jnp.bfloat16):
    drawn = spread * jax.random.normal(own_key, dims, jnp.float32)
    if shards:
        drawn = drawn * shard_levels(own_key, dims, shards, -0.22, 0.18)
    return jnp.clip(drawn, -limit, limit).astype(kind)


def setup_inputs(seed: int = 0) -> dict:
    streams_of = jax.random.split(jax.random.key(seed), 16)
    return {
        "spans": scatter_about(streams_of[0], (SPANS, K, B), 1.0, 6.0, ((0, 32),)),
        "encoded": scatter_about(streams_of[1], (FRAMES, N), 1.0, 6.0, ((0, 32),)),
        "clip_lengths": jax.vmap(lambda own: ragged_sizes(own, CLIPS, CH_DEV, LONGEST, 1))(jax.random.split(streams_of[2], N_DP * N_SPK)).reshape((N_DP, N_SPK, CLIPS)).astype(jnp.int32),
        "clip_pads": with_ends(jax.random.randint(streams_of[3], (N_DP, N_SPK, CLIPS), 0, HOP), jax.random.fold_in(streams_of[3], 1), 0, HOP - 1).astype(jnp.int32),
        "lstm_in": scatter_about(streams_of[4], (BLOCKS, 2, 2, B, 4 * HID), B ** -0.5, 0.75),
        "lstm_rec": scatter_about(streams_of[5], (BLOCKS, 2, 2, HID, 4 * HID), HID ** -0.5, 0.5),
        "lstm_bias": scatter_about(streams_of[6], (BLOCKS, 2, 2, 4 * HID), 0.5, 3.0, (), jnp.float32),
        "proj_weight": scatter_about(streams_of[7], (BLOCKS, 2, 2 * HID, B), (2 * HID) ** -0.5, 0.375),
        "proj_bias": scatter_about(streams_of[8], (BLOCKS, 2, B), 0.5, 3.0, (), jnp.float32),
        "gln_gain": jnp.clip(1.0 + 0.15 * jax.random.normal(streams_of[9], (BLOCKS, 2, B), jnp.float32), 0.25, 1.75),
        "gln_shift": scatter_about(streams_of[10], (BLOCKS, 2, B), 0.5, 3.0, (), jnp.float32),
        "mask_weight": scatter_about(streams_of[11], (SPK, B, N), B ** -0.5, 0.75, ((0, 2),)),
        "mask_bias": scatter_about(streams_of[12], (SPK, N), 0.5, 3.0, ((0, 2),)),
        "dec_weight": scatter_about(streams_of[13], (N, KDEC), N ** -0.5, 0.75),
        "wave_grad": scatter_about(streams_of[14], (SPK, SAMPLES), 1.0, 6.0, ((0, 2), (1, 16))),
    }


UPPER_BOUND = lax.Precision.HIGHEST

@jax.custom_vjp
def low(v):
    return lax.optimization_barrier(v.astype(jnp.bfloat16)).astype(jnp.float32)

@jax.custom_vjp
def lower_bound_back(v):
    return v

def low_keep(v):
    return (low(v), None)

def low_pass(kept, grad):
    return (grad,)

def back_keep(v):
    return (v, None)

def back_low(kept, grad):
    return (low(grad),)
low.defvjp(low_keep, low_pass)
lower_bound_back.defvjp(back_keep, back_low)

def clip_tables(lengths, pad_counts):
    clip_ends = jnp.cumsum(lengths, axis=-1).astype(jnp.int32)
    clip_starts = (clip_ends - lengths).astype(jnp.int32)
    positions = jnp.arange(CH_DEV, dtype=jnp.int32)
    clip_of = lax.optimization_barrier(jnp.sum((clip_ends[:, None, :] <= positions[None, :, None]).astype(jnp.int32), axis=-1))
    onehot = (clip_of[:, :, None] == jnp.arange(CLIPS, dtype=jnp.int32)[None, None, :]).astype(jnp.float32)
    is_first = lax.optimization_barrier(jnp.sum((clip_starts[:, None, :] == positions[None, :, None]).astype(jnp.float32), axis=-1))
    is_last = lax.optimization_barrier(jnp.sum((clip_ends[:, None, :] - 1 == positions[None, :, None]).astype(jnp.float32), axis=-1))
    tail_pad = lax.optimization_barrier(jnp.sum(onehot * pad_counts[:, None, :].astype(jnp.float32), axis=-1))
    offsets = jnp.arange(K).astype(jnp.float32)
    is_valid = 1.0 - is_last[:, :, None] * (offsets[None, None, :] >= K - tail_pad[:, :, None]).astype(jnp.float32)
    return (onehot, is_first, is_last, is_valid)

def lstm_run(sequence, keep_mask, w_in, w_rec, w_bias, reverse):
    driven = jnp.einsum('trb,bg->trg', sequence, w_in, precision=UPPER_BOUND)

    def lstm_step(state_pair, inputs):
        hidden, cell_state = state_pair
        drive_now, keep_now = inputs
        hidden = hidden * keep_now[:, None]
        cell_state = cell_state * keep_now[:, None]
        preact = lower_bound_back(drive_now + jnp.dot(hidden, w_rec, precision=UPPER_BOUND) + w_bias)
        in_gate, forget_gate, cand_gate, out_gate = jnp.split(preact, 4, axis=-1)
        cell_state = jax.nn.sigmoid(forget_gate) * cell_state + jax.nn.sigmoid(in_gate) * jnp.tanh(cand_gate)
        hidden = low(jax.nn.sigmoid(out_gate) * jnp.tanh(cell_state))
        return ((hidden, cell_state), hidden)
    zero_state = jnp.zeros((sequence.shape[1], HID), jnp.float32)
    unused, outputs = lax.scan(lstm_step, (zero_state, zero_state), (driven, keep_mask), reverse=reverse)
    return outputs

def global_norm(mixed_out, gain, shift, onehot, is_valid):
    counts = B * jnp.einsum('gj,gjc->gc', lax.optimization_barrier(jnp.sum(is_valid, axis=-1)), onehot, precision=UPPER_BOUND)
    totals = jnp.einsum('gj,gjc->gc', lax.optimization_barrier(jnp.sum(is_valid[..., None] * mixed_out, axis=(2, 3))), onehot, precision=UPPER_BOUND)
    clip_mean = jnp.einsum('gc,gjc->gj', totals / counts, onehot, precision=UPPER_BOUND)
    centered = mixed_out - clip_mean[:, :, None, None]
    spread_values = jnp.einsum('gj,gjc->gc', lax.optimization_barrier(jnp.sum(is_valid[..., None] * centered * centered, axis=(2, 3))), onehot, precision=UPPER_BOUND)
    inv_scale = lax.rsqrt(jnp.einsum('gc,gjc->gj', spread_values / counts, onehot, precision=UPPER_BOUND) + 1e-08)
    return is_valid[..., None] * (centered * inv_scale[:, :, None, None] * gain + shift)

def run_section(stream, weights, tables, across):
    w_in, w_rec, w_bias, w_proj, proj_bias, gain, shift = weights
    onehot, is_first, is_last, is_valid = tables
    groups = stream.shape[0]
    low_in = low(stream)
    runner = jax.checkpoint(lstm_run, static_argnums=(5,))
    if across:
        sequence = low_in.transpose(1, 0, 2, 3).reshape(CH_DEV, groups * K, B)
        keep_ahead = jnp.repeat((1.0 - is_first).T, K, axis=1)
        keep_behind = jnp.repeat((1.0 - is_last).T, K, axis=1)
    else:
        sequence = low_in.transpose(2, 0, 1, 3).reshape(K, groups * CH_DEV, B)
        keep_ahead = jnp.ones((K, groups * CH_DEV), jnp.float32)
        keep_behind = keep_ahead
    forward_run = runner(sequence, keep_ahead, w_in[0], w_rec[0], w_bias[0], False)
    backward_run = runner(sequence, keep_behind, w_in[1], w_rec[1], w_bias[1], True)
    joined = jnp.concatenate([forward_run, backward_run], axis=-1)
    mixed_out = lower_bound_back(jnp.einsum('trh,hb->trb', joined, w_proj, precision=UPPER_BOUND) + proj_bias)
    if across:
        mixed_out = mixed_out.reshape(CH_DEV, groups, K, B).transpose(1, 0, 2, 3)
    else:
        mixed_out = mixed_out.reshape(K, groups, CH_DEV, B).transpose(1, 2, 0, 3)
    return stream + global_norm(mixed_out, gain, shift, onehot, is_valid)

def run_head(stream, mask_all, mask_bias_all, decoder_weight, mixture, is_first):
    groups = stream.shape[0]
    features = low(jax.nn.silu(stream))
    preact = lower_bound_back(jnp.einsum('gjkb,sbn->gsjkn', features, mask_all, precision=UPPER_BOUND) + mask_bias_all[None, :, None, None, :])
    lead_half = preact[:, :, :, :HOP]
    tail_half = preact[:, :, :, HOP:]
    span_keep = (1.0 - is_first)[:, None, :, None, None]
    shifted = jnp.concatenate([jnp.zeros_like(tail_half[:, :, :1]), tail_half[:, :, :-1]], axis=2) * span_keep
    frames = (lead_half + shifted).reshape(groups, SPK, FR_DEV, N)
    masked_features = low(jax.nn.softplus(frames) * mixture[:, None])
    segment_frames = lower_bound_back(jnp.einsum('qyej,jc->qyec', masked_features, decoder_weight, precision=UPPER_BOUND))
    is_start = (jnp.arange(FR_DEV) % HOP == 0).astype(jnp.float32)
    frame_keep = 1.0 - is_start[None, :] * jnp.repeat(is_first, HOP, axis=1)
    lead_part = segment_frames[..., :STRIDE]
    tail_part = segment_frames[..., STRIDE:]
    carried = jnp.concatenate([jnp.zeros_like(tail_part[:, :, :1]), tail_part[:, :, :-1]], axis=2) * frame_keep[:, None, :, None]
    waveform = (lead_part + carried).reshape(groups, SPK, FR_DEV * STRIDE)
    return waveform.transpose(1, 0, 2).reshape(SPK, groups * FR_DEV * STRIDE)

def reference(spans, encoded, clip_lengths, clip_pads, lstm_in, lstm_rec, lstm_bias, proj_weight, proj_bias, gln_gain, gln_shift, mask_weight, mask_bias, dec_weight, wave_grad):
    groups = N_DP * N_SPK
    tables = clip_tables(clip_lengths.reshape(groups, CLIPS), clip_pads.reshape(groups, CLIPS))
    mixture = encoded.astype(jnp.float32).reshape(groups, FR_DEV, N)

    def forward(span_in, in_weights, rec_weights, bias_all, proj_all, proj_bias_all, every_gain, shift_all, mask_all, mask_bias_all, decoder_weight):
        stream = span_in.reshape(groups, CH_DEV, K, B) * tables[3][..., None]
        for block_index in range(BLOCKS):
            for section_index in range(2):
                weights = (in_weights[block_index, section_index], rec_weights[block_index, section_index], bias_all[block_index, section_index], proj_all[block_index, section_index], proj_bias_all[block_index, section_index], every_gain[block_index, section_index], shift_all[block_index, section_index])
                stream = run_section(stream, weights, tables, section_index == 1)
        return run_head(stream, mask_all, mask_bias_all, decoder_weight, mixture, tables[1])
    primals = (spans, lstm_in, lstm_rec, lstm_bias, proj_weight, proj_bias, gln_gain, gln_shift, mask_weight, mask_bias, dec_weight)
    primals = tuple((item.astype(jnp.float32) for item in primals))
    waveforms, pullback = jax.vjp(forward, *primals)
    grads = pullback(wave_grad.astype(jnp.float32))
    return (waveforms, grads[0], grads[1], grads[2], grads[3], grads[4], grads[5], grads[6], grads[7], grads[8], grads[9], grads[10])
```

```python
import functools

import jax
import jax.numpy as jnp
from jax import lax
from jax.experimental import pallas as pl
from jax.experimental.pallas import tpu as pltpu
from jax.sharding import PartitionSpec as P

F32 = jnp.float32
BF16 = jnp.bfloat16
LANES = 128


def dot(a, b):
    return jnp.dot(a, b, preferred_element_type=F32)


def dot_tn(a, b):
    return lax.dot_general(a, b, (((0,), (0,)), ((), ())), preferred_element_type=F32)


def dot_nt(a, b):
    return lax.dot_general(a, b, (((1,), (1,)), ((), ())), preferred_element_type=F32)


def chunks(total, size, body):
    assert total % size == 0

    def step(i, carry):
        body(pl.multiple_of(i * size, size))
        return carry

    lax.fori_loop(0, total // size, step, 0)


def local_kernel(
    sizes,
    lengths_ref,
    pads_ref,
    spans_ref,
    enc_ref,
    w_in_ref,
    w_rec_ref,
    w_bias_ref,
    w_proj_ref,
    proj_bias_ref,
    gain_ref,
    shift_ref,
    mask_ref,
    mask_bias_ref,
    dec_ref,
    dw_ref,
    wave_out,
    spans_out,
    in_out,
    rec_out,
    bias_out,
    proj_out,
    proj_bias_out,
    gain_out,
    shift_out,
    mask_out,
    mask_bias_out,
    dec_out,
    stream,
    valid,
    mx,
    xj,
    dz,
    dmj,
    normed,
    inv_all,
    u_a,
    u_e,
    hc_a,
    hc_e,
    sv_a,
    sv_e,
    gd,
    dh,
    dp,
    wis,
    wrs,
    wiu,
    wrt,
    pws,
    vec,
    enc_t,
    pre,
    masked,
    feats,
    dpre,
):
    R, K, C, H, clips, blocks, kp = sizes
    rows, rows_e = R * K, R * kp
    hop = K // 2
    frames = R * hop
    half = 8
    cr = 10 * R
    speaker = lax.axis_index("spk")

    jio = lax.broadcasted_iota(jnp.int32, (R, LANES), 0)
    lane = lax.broadcasted_iota(jnp.int32, (1, LANES), 1)
    ones_lane = (lane == C).astype(F32)

    lens = [lengths_ref[0, speaker, c] for c in range(clips)]
    pads = [pads_ref[0, speaker, c] for c in range(clips)]
    starts, ends, at = [], [], 0
    for c in range(clips):
        starts.append(at)
        at = at + lens[c]
        ends.append(at)

    def is_start(j):
        hit = j == starts[0]
        for c in range(1, clips):
            hit = jnp.logical_or(hit, j == starts[c])
        return hit

    def is_end(j):
        hit = j == ends[0] - 1
        for c in range(1, clips):
            hit = jnp.logical_or(hit, j == ends[c] - 1)
        return hit

    members, thr, inv_count = [], jnp.full((R, LANES), K, jnp.int32), jnp.zeros((R, LANES), F32)
    for c in range(clips):
        member = jnp.logical_and(jio >= starts[c], jio < ends[c]).astype(F32)
        members.append(member)
        thr = jnp.where(jio == ends[c] - 1, K - pads[c], thr)
        total = (C * (K * lens[c] - pads[c])).astype(F32)
        inv_count = inv_count + member / jnp.full((R, LANES), total, F32)
    not_first = 1.0 - is_start(jio).astype(F32)
    next_not_first = 1.0 - jnp.logical_or(is_start(jio + 1), jio == R - 1).astype(F32)

    def clip_sum(x):
        out = jnp.zeros((R, 1), F32)
        for member in members:
            out = out + member[:, :1] * jnp.sum(member * x, axis=(0, 1), keepdims=True)
        return out

    def fill_valid(r):
        k = lax.broadcasted_iota(jnp.int32, (cr // R, R, LANES), 0) + r // R
        low = lax.broadcasted_iota(jnp.int32, (cr // R, R, LANES), 2) < C
        ok = jnp.logical_and(k < thr[None], low).astype(F32)
        valid[pl.ds(r, cr)] = ok.reshape(cr, LANES)

    chunks(rows, cr, fill_valid)

    pws[...] = jnp.zeros_like(pws)
    wis[...] = jnp.zeros_like(wis)
    wiu[...] = jnp.zeros_like(wiu)
    vec[...] = jnp.zeros_like(vec)
    for b in range(blocks):
        for s in range(2):
            n = 2 * b + s
            pws[b, s, :, 0:C] = w_proj_ref[b, s]
            vec[n, 0:1, 0:C] = proj_bias_ref[b, s : s + 1]
            vec[n, 1:2, 0:C] = gain_ref[b, s : s + 1]
            vec[n, 2:3, 0:C] = shift_ref[b, s : s + 1]

    stream[...] = jnp.zeros_like(stream)
    for j in range(R):
        x = spans_ref[j].astype(F32)
        stream[pl.ds(j, K, stride=R), :] = jnp.concatenate([x, jnp.zeros_like(x)], axis=1)

    def start_stream(r):
        x = stream[pl.ds(r, cr)] * valid[pl.ds(r, cr)]
        stream[pl.ds(r, cr)] = jnp.where(lane == C, 1.0, x)

    chunks(rows, cr, start_stream)

    gate_scale = jnp.where(
        lax.broadcasted_iota(jnp.int32, (1, 4 * H), 1) // H == 2, 1.0, 0.5
    ).astype(F32)

    def lane_part(x, g):
        return x[:, g * H : (g + 1) * H]

    def gate_step(d, sv, b, r, n, p, c, keep_next):
        acts = [jnp.tanh(p[:, g * H : (g + 1) * H] + gd[d, pl.ds(r, n), g * H : (g + 1) * H]) for g in range(4)]
        ti, tf, g, to = acts
        i, f, o = 0.5 * ti + 0.5, 0.5 * tf + 0.5, 0.5 * to + 0.5
        cn = f * c + i * g
        tc = jnp.tanh(cn)
        h = o * tc
        parts = [
            g * (0.25 - 0.25 * ti * ti),
            c * (0.25 - 0.25 * tf * tf),
            i * (1.0 - g * g),
            tc * (0.25 - 0.25 * to * to),
            o * (1.0 - tc * tc),
            f,
        ]
        for m, part in enumerate(parts):
            sv[b, d, pl.ds(r, n), m * H : (m + 1) * H] = part.astype(BF16)
        if keep_next is None:
            return h.astype(BF16), h.astype(BF16), cn
        return h.astype(BF16), (h * keep_next).astype(BF16), cn * keep_next

    def run_forward(b, sec, u, hc, sv, n, steps, unroll):
        total = n * steps
        for d in range(2):
            w = w_in_ref[b, sec, d].astype(F32) * gate_scale
            wis[0:C, d * 4 * H : (d + 1) * 4 * H] = w.astype(BF16)
            wrs[d] = (w_rec_ref[b, sec, d].astype(F32) * gate_scale).astype(BF16)
        size = total // 4

        def drive(r):
            for d in range(2):
                bias = w_bias_ref[b, sec, d : d + 1] * gate_scale
                gd[d, pl.ds(r, size)] = (
                    dot(u[b, pl.ds(r, size)], wis[:, d * 4 * H : (d + 1) * 4 * H]) + bias
                )

        chunks(total, size, drive)

        def step(t, carry):
            hf, hb, cf, cb = carry
            back = steps - 1 - t
            rf = pl.multiple_of(t * n, n)
            rb = pl.multiple_of(back * n, n)
            kf = kb = None
            if sec == 1:
                kf = 1.0 - is_start(t + 1).astype(F32)
                kb = 1.0 - is_end(back - 1).astype(F32)
            pf = dot(hf, wrs[0])
            pb = dot(hb, wrs[1])
            out_f, hf, cf = gate_step(0, sv, b, rf, n, pf, cf, kf)
            out_b, hb, cb = gate_step(1, sv, b, rb, n, pb, cb, kb)
            hc[b, pl.ds(rf, n), 0:H] = out_f
            hc[b, pl.ds(rb, n), H : 2 * H] = out_b
            return hf, hb, cf, cb

        zh, zc = jnp.zeros((n, H), BF16), jnp.zeros((n, H), F32)
        lax.fori_loop(0, steps, step, (zh, zh, zc, zc), unroll=unroll)

    def norm_forward(b, sec):
        n = 2 * b + sec
        gain, shift = vec[n, 1:2], vec[n, 2:3]

        def fold(body):
            def step(i, acc):
                return acc + jnp.sum(body(pl.multiple_of(i * cr, cr)).reshape(cr // R, R, LANES), axis=0)

            return lax.fori_loop(0, rows // cr, step, jnp.zeros((R, LANES), F32))

        mean = clip_sum(fold(lambda r: valid[pl.ds(r, cr)] * mx[pl.ds(r, cr)])) * inv_count

        def spread(r):
            x = mx[pl.ds(r, cr)].reshape(cr // R, R, LANES) - mean[None]
            return valid[pl.ds(r, cr)] * (x * x).reshape(cr, LANES)

        inv = lax.rsqrt(clip_sum(fold(spread)) * inv_count + 1e-08)
        inv_all[n] = inv

        def apply(r):
            x = (mx[pl.ds(r, cr)].reshape(cr // R, R, LANES) - mean[None]) * inv[None]
            x = x.reshape(cr, LANES)
            normed[n, pl.ds(r, cr)] = x
            stream[pl.ds(r, cr)] += valid[pl.ds(r, cr)] * (x * gain + shift)

        chunks(rows, cr, apply)

    def forward_block(b, carry):
        def u_intra(r):
            u_a[b, pl.ds(r, cr)] = stream[pl.ds(r, cr)].astype(BF16)

        chunks(rows, cr, u_intra)
        run_forward(b, 0, u_a, hc_a, sv_a, R, K, 4)

        def mix_intra(r):
            mx[pl.ds(r, rows // 4)] = dot(hc_a[b, pl.ds(r, rows // 4)], pws[b, 0]) + vec[2 * b, 0:1]

        chunks(rows, rows // 4, mix_intra)
        norm_forward(b, 0)

        for j in range(R):
            u_e[b, pl.ds(j * kp, kp)] = stream[pl.ds(j, kp, stride=R), :].astype(BF16)
        run_forward(b, 1, u_e, hc_e, sv_e, kp, R, 2)

        def mix_inter(r):
            xj[pl.ds(r, rows_e // 4)] = (
                dot(hc_e[b, pl.ds(r, rows_e // 4)], pws[b, 1]) + vec[2 * b + 1, 0:1]
            )

        chunks(rows_e, rows_e // 4, mix_inter)
        for j in range(R):
            mx[pl.ds(j, kp, stride=R), :] = xj[pl.ds(j * kp, kp)]
        norm_forward(b, 1)
        return carry

    lax.fori_loop(0, blocks, forward_block, 0)

    for j in range(R):
        e = enc_ref[j * hop : (j + 1) * hop].astype(F32)
        enc_t[pl.ds(j, hop, stride=R), :] = jnp.concatenate([e, e], axis=1)
        xj[pl.ds(j, hop, stride=R), :] = dw_ref[j * hop : (j + 1) * hop]
    seg_a, seg_b = 2, 3

    def head_pre(r):
        x = stream[pl.ds(r, cr)]
        f = x * (0.5 * jnp.tanh(0.5 * x) + 0.5)
        f = jnp.where(lane == C, 1.0, f).astype(BF16)
        feats[pl.ds(r, cr)] = f
        pre[pl.ds(r, cr)] = dot(f[:, 0:C], mask_ref[...]) + mask_bias_ref[...]

    chunks(rows, cr, head_pre)

    hr = frames // 5
    del seg_a, seg_b

    def tile(v):
        return jnp.broadcast_to(v[None], (hr // R, R, LANES)).reshape(hr, LANES)

    for q in range(5):
        r = q * hr
        fr = pre[r : r + hr] + tile(not_first) * pre[frames + r - 1 : frames + r - 1 + hr]
        e = enc_t[r : r + hr]
        sp = jnp.maximum(fr, 0.0) + jnp.log1p(jnp.exp(-jnp.abs(fr)))
        masked[r : r + hr] = (sp * e).astype(BF16)
        pre[r : r + hr] = e * (0.5 * jnp.tanh(0.5 * fr) + 0.5)
    for q in range(5):
        r = q * hr
        gd[0, r : r + hr, 0 : 2 * LANES] = dot(masked[r : r + hr], dec_ref[...])
    gd[1, 0:R, 0:LANES] = (
        gd[0, 0:R, 0:LANES] + not_first * gd[0, frames - R - 1 : frames - 1, LANES : 2 * LANES]
    )
    gd[1, R:frames, 0:LANES] = gd[0, R:frames, 0:LANES] + gd[0, 0 : frames - R, LANES : 2 * LANES]
    xj[frames : 2 * frames] = gd[1, 0:frames, 0:LANES]
    for j in range(R):
        wave_out[j * hop : (j + 1) * hop] = xj[pl.ds(frames + j, hop, stride=R), :][:, 0 : 2 * half]

    gd[0, 0:frames, 0:LANES] = xj[0:frames]
    gd[0, 0 : frames - R, LANES : 2 * LANES] = xj[R:frames]
    gd[0, frames - R : frames, LANES : 2 * LANES] = next_not_first * xj[1 : R + 1]
    dp[0, 0:frames, 0 : 2 * LANES] = gd[0, 0:frames, 0 : 2 * LANES].astype(BF16)
    dec_out[...] = dot_tn(masked[...], dp[0, 0:frames, 0 : 2 * LANES])
    xj[frames : frames + 8] = jnp.zeros((8, LANES), F32)
    for q in range(5):
        r = q * hr
        dfr = dot_nt(dp[0, r : r + hr, 0 : 2 * LANES], dec_ref[...]) * pre[r : r + hr]
        xj[r : r + hr] = dfr
        dpre[r : r + hr] = dfr.astype(BF16)
    for q in range(5):
        r = q * hr
        dpre[frames + r : frames + r + hr] = (tile(next_not_first) * xj[r + 1 : r + 1 + hr]).astype(BF16)
    gm = dot_tn(feats[...], dpre[...])
    mask_out[...] = gm[0:C]
    mask_bias_out[...] = gm[C : C + 1]
    dz[...] = jnp.zeros_like(dz)

    def head_dz(r):
        x = stream[pl.ds(r, cr)]
        sg = 0.5 * jnp.tanh(0.5 * x) + 0.5
        df = dot_nt(dpre[pl.ds(r, cr)], mask_ref[...])
        df = jnp.concatenate([df, jnp.zeros_like(df)], axis=1)
        dz[pl.ds(r, cr)] = df * sg * (1.0 + x * (1.0 - sg))

    chunks(rows, cr, head_dz)

    def norm_backward(b, sec):
        n = 2 * b + sec
        gain = vec[n, 1:2]

        def sums(i, acc):
            r = pl.multiple_of(i * cr, cr)
            v = valid[pl.ds(r, cr)] * dz[pl.ds(r, cr)]
            w = v * normed[n, pl.ds(r, cr)]
            return (
                acc[0] + jnp.sum(v.reshape(cr // R, R, LANES), axis=0),
                acc[1] + jnp.sum(w.reshape(cr // R, R, LANES), axis=0),
            )

        zero = jnp.zeros((R, LANES), F32)
        s1, s2 = lax.fori_loop(0, rows // cr, sums, (zero, zero))
        shift_out[b, sec : sec + 1] = jnp.sum(s1, axis=0, keepdims=True)[:, 0:C]
        gain_out[b, sec : sec + 1] = jnp.sum(s2, axis=0, keepdims=True)[:, 0:C]
        m1 = clip_sum(s1 * gain) * inv_count
        m2 = clip_sum(s2 * gain) * inv_count
        inv = inv_all[n]

        def apply(i, acc):
            r = pl.multiple_of(i * cr, cr)
            d = (dz[pl.ds(r, cr)] * gain).reshape(cr // R, R, LANES)
            x = normed[n, pl.ds(r, cr)].reshape(cr // R, R, LANES)
            y = (d - m1[None] - x * m2[None]) * inv[None]
            y = (y.reshape(cr, LANES) * valid[pl.ds(r, cr)]).astype(BF16)
            if sec == 0:
                dmj[pl.ds(r, cr)] = y
            y = y.astype(F32)
            if sec == 1:
                mx[pl.ds(r, cr)] = y
            return acc + jnp.sum(y.reshape(cr // R, R, LANES), axis=0)

        acc = lax.fori_loop(0, rows // cr, apply, zero)
        proj_bias_out[b, sec : sec + 1] = jnp.sum(acc, axis=0, keepdims=True)[:, 0:C]

    def back_step(d, sv, b, r, n, dhn, dcn, keep):
        a = [sv[b, d, pl.ds(r, n), m * H : (m + 1) * H].astype(F32) for m in range(6)]
        g = dh[pl.ds(r, n), d * H : (d + 1) * H] + dhn
        dc = dcn + g * a[4]
        for m in range(4):
            dp[d, pl.ds(r, n), m * H : (m + 1) * H] = ((g if m == 3 else dc) * a[m]).astype(BF16)
        dhn = dot(dp[d, pl.ds(r, n)], wrt[d])
        dcn = dc * a[5]
        if keep is not None:
            dhn, dcn = dhn * keep, dcn * keep
        return dhn, dcn

    def run_backward(b, sec, u, hc, sv, n, steps, unroll):
        total = n * steps
        size = total // 4
        proj_out[b, sec] = dot_tn(dmj[0:total], hc[b]).T[:, 0:C]

        def joined(r):
            dh[pl.ds(r, size)] = dot_nt(dmj[pl.ds(r, size)], pws[b, sec])

        chunks(total, size, joined)
        for d in range(2):
            wrt[d] = w_rec_ref[b, sec, d].T
            wiu[0:C, d * 4 * H : (d + 1) * 4 * H] = w_in_ref[b, sec, d]

        def step(t, carry):
            hf, hb, cf, cb = carry
            back = steps - 1 - t
            rf = pl.multiple_of(back * n, n)
            rb = pl.multiple_of(t * n, n)
            kf = kb = None
            if sec == 1:
                kf = 1.0 - is_start(back).astype(F32)
                kb = 1.0 - is_end(t).astype(F32)
            hf, cf = back_step(0, sv, b, rf, n, hf, cf, kf)
            hb, cb = back_step(1, sv, b, rb, n, hb, cb, kb)
            return hf, hb, cf, cb

        z = jnp.zeros((n, H), F32)
        lax.fori_loop(0, steps, step, (z, z, z, z), unroll=unroll)
        if sec == 1:
            for j in range(1, steps):
                kf = (1.0 - is_start(j).astype(F32)).astype(BF16)
                at = slice((j - 1) * n, j * n)
                hc[b, at, 0:H] = hc[b, at, 0:H] * kf
                kb = (1.0 - is_end(j - 1).astype(F32)).astype(BF16)
                at = slice(j * n, (j + 1) * n)
                hc[b, at, H : 2 * H] = hc[b, at, H : 2 * H] * kb
        for d in range(2):
            g = dot_tn(u[b], dp[d, 0:total])
            in_out[b, sec, d] = g[0:C]
            bias_out[b, sec, d : d + 1] = g[C : C + 1]
        rec_out[b, sec, 0] = dot_tn(hc[b, 0 : total - n, 0:H], dp[0, n:total])
        rec_out[b, sec, 1] = dot_tn(hc[b, n:total, H : 2 * H], dp[1, 0 : total - n])

    def stream_grad(r, size):
        return dot_nt(dp[0, pl.ds(r, size)], wiu[:, 0 : 4 * H]) + dot_nt(
            dp[1, pl.ds(r, size)], wiu[:, 4 * H : 8 * H]
        )

    def backward_block(i, carry):
        b = blocks - 1 - i
        norm_backward(b, 1)
        mx[rows:rows_e] = jnp.zeros((rows_e - rows, LANES), F32)
        for j in range(R):
            dmj[pl.ds(j * kp, kp)] = mx[pl.ds(j, kp, stride=R), :].astype(BF16)
        run_backward(b, 1, u_e, hc_e, sv_e, kp, R, 2)

        def grad_inter(r):
            xj[pl.ds(r, rows_e // 4)] = stream_grad(r, rows_e // 4)

        chunks(rows_e, rows_e // 4, grad_inter)
        for j in range(R):
            dz[pl.ds(j, kp, stride=R), :] += xj[pl.ds(j * kp, kp)]

        norm_backward(b, 0)
        run_backward(b, 0, u_a, hc_a, sv_a, R, K, 4)

        def grad_intra(r):
            dz[pl.ds(r, rows // 4)] += stream_grad(r, rows // 4)

        chunks(rows, rows // 4, grad_intra)
        return carry

    lax.fori_loop(0, blocks, backward_block, 0)

    def finish(r):
        dz[pl.ds(r, cr)] = dz[pl.ds(r, cr)] * valid[pl.ds(r, cr)]

    chunks(rows, cr, finish)
    for j in range(R):
        spans_out[j] = dz[pl.ds(j, K, stride=R), :][:, 0:C]


def shards(
    spans,
    encoded,
    clip_lengths,
    clip_pads,
    lstm_in,
    lstm_rec,
    lstm_bias,
    proj_weight,
    proj_bias,
    gln_gain,
    gln_shift,
    mask_weight,
    mask_bias,
    dec_weight,
    wave_grad,
):
    speaker = lax.axis_index("spk")
    R, K, C = spans.shape
    H = lstm_rec.shape[3]
    blocks = lstm_in.shape[0]
    clips = clip_lengths.shape[2]
    frames = encoded.shape[0]
    half = dec_weight.shape[1] // 2
    samples = frames * half
    kp = -(-K // 16) * 16
    rows, rows_e = R * K, R * kp

    mine = lax.dynamic_slice_in_dim(wave_grad[0], speaker * samples, samples, 0)
    theirs = lax.dynamic_slice_in_dim(wave_grad[0], (1 - speaker) * samples, samples, 0)
    sent = jnp.concatenate([theirs, mask_weight.reshape(-1), mask_bias.reshape(-1)])
    got = lax.ppermute(sent, "spk", [(0, 1), (1, 0)])
    other_mask = got[samples : samples + C * C].reshape(C, C)
    other_bias = got[samples + C * C :].reshape(1, C)
    dw = jnp.concatenate([mine.reshape(frames, half), got[:samples].reshape(frames, half)], axis=1)
    dw = jnp.pad(dw.astype(F32), ((0, 0), (0, LANES - 2 * half)))
    masks = jnp.concatenate([mask_weight[0], other_mask], axis=1)
    mask_biases = jnp.concatenate([mask_bias, other_bias], axis=1).astype(F32)
    zero = jnp.zeros((C, half), BF16)
    pad = jnp.zeros((C, LANES - 2 * half), BF16)
    lead, tail = dec_weight[:, :half], dec_weight[:, half:]
    dec = jnp.concatenate(
        [
            jnp.concatenate([lead, zero, pad, tail, zero, pad], axis=1),
            jnp.concatenate([zero, lead, pad, zero, tail, pad], axis=1),
        ],
        axis=0,
    )

    sizes = (R, K, C, H, clips, blocks, kp)
    smem = pl.BlockSpec(memory_space=pltpu.SMEM)
    vmem = pl.BlockSpec(memory_space=pltpu.VMEM)
    shape = jax.ShapeDtypeStruct
    outs = pl.pallas_call(
        functools.partial(local_kernel, sizes),
        out_shape=(
            shape((frames, 2 * half), F32),
            shape((R, K, C), F32),
            shape((blocks, 2, 2, C, 4 * H), F32),
            shape((blocks, 2, 2, H, 4 * H), F32),
            shape((blocks, 2, 2, 4 * H), F32),
            shape((blocks, 2, 2 * H, C), F32),
            shape((blocks, 2, C), F32),
            shape((blocks, 2, C), F32),
            shape((blocks, 2, C), F32),
            shape((C, 2 * C), F32),
            shape((1, 2 * C), F32),
            shape((2 * C, 2 * LANES), F32),
        ),
        in_specs=[smem, smem] + [vmem] * 13,
        out_specs=tuple([vmem] * 12),
        scratch_shapes=[
            pltpu.VMEM((rows_e, LANES), F32),
            pltpu.VMEM((rows, LANES), F32),
            pltpu.VMEM((rows_e, LANES), F32),
            pltpu.VMEM((rows_e, LANES), F32),
            pltpu.VMEM((rows_e, LANES), F32),
            pltpu.VMEM((rows_e, LANES), BF16),
            pltpu.VMEM((2 * blocks, rows, LANES), F32),
            pltpu.VMEM((2 * blocks, R, LANES), F32),
            pltpu.VMEM((blocks, rows, LANES), BF16),
            pltpu.VMEM((blocks, rows_e, LANES), BF16),
            pltpu.VMEM((blocks, rows, 2 * H), BF16),
            pltpu.VMEM((blocks, rows_e, 2 * H), BF16),
            pltpu.VMEM((blocks, 2, rows, 6 * H), BF16),
            pltpu.VMEM((blocks, 2, rows_e, 6 * H), BF16),
            pltpu.VMEM((2, rows_e, 4 * H), F32),
            pltpu.VMEM((rows_e, 2 * H), F32),
            pltpu.VMEM((2, rows_e, 4 * H), BF16),
            pltpu.VMEM((LANES, 8 * H), BF16),
            pltpu.VMEM((2, H, 4 * H), BF16),
            pltpu.VMEM((LANES, 8 * H), BF16),
            pltpu.VMEM((2, 4 * H, H), BF16),
            pltpu.VMEM((blocks, 2, 2 * H, LANES), BF16),
            pltpu.VMEM((2 * blocks, 8, LANES), F32),
            pltpu.VMEM((frames, LANES), F32),
            pltpu.VMEM((rows, LANES), F32),
            pltpu.VMEM((frames, LANES), BF16),
            pltpu.VMEM((rows, LANES), BF16),
            pltpu.VMEM((rows, LANES), BF16),
        ],
        compiler_params=pltpu.CompilerParams(vmem_limit_bytes=62 * 1024 * 1024),
        name="dual_path",
    )(
        clip_lengths,
        clip_pads,
        spans,
        encoded,
        lstm_in,
        lstm_rec,
        lstm_bias,
        proj_weight,
        proj_bias,
        gln_gain,
        gln_shift,
        masks,
        mask_biases,
        dec,
        dw,
    )
    wave, grad_spans = outs[0], outs[1]
    own_wave = wave[:, :half].reshape(-1)
    far_wave = lax.ppermute(wave[:, half:].reshape(-1), "spk", [(0, 1), (1, 0)])
    first = speaker == 0
    waveforms = jnp.where(
        first,
        jnp.concatenate([own_wave, far_wave]),
        jnp.concatenate([far_wave, own_wave]),
    )[None]

    def by_speaker(x):
        a, b = x[:, :C], x[:, C:]
        return jnp.where(first, jnp.stack([a, b]), jnp.stack([b, a]))

    gd = outs[11]
    grad_dec = jnp.concatenate(
        [
            gd[:C, :half] + gd[C:, half : 2 * half],
            gd[:C, LANES : LANES + half] + gd[C:, LANES + half : LANES + 2 * half],
        ],
        axis=1,
    )
    summed = lax.psum(
        outs[2:9] + (by_speaker(outs[9]), by_speaker(outs[10])[:, 0], grad_dec), ("dp", "spk")
    )
    return (
        (waveforms, grad_spans)
        + summed[:7]
        + (
            lax.dynamic_slice_in_dim(summed[7], speaker, 1, 0),
            lax.dynamic_slice_in_dim(summed[8], speaker, 1, 0),
            summed[9],
        )
    )


def solution(mesh):
    return jax.shard_map(
        shards,
        mesh=mesh,
        in_specs=(
            P(("dp", "spk"), None, None),
            P(("dp", "spk"), None),
            P("dp", None, None),
            P("dp", None, None),
            P(),
            P(),
            P(),
            P(),
            P(),
            P(),
            P(),
            P("spk", None, None),
            P("spk", None),
            P(),
            P("spk", "dp"),
        ),
        out_specs=(
            P("spk", "dp"),
            P(("dp", "spk"), None, None),
            P(),
            P(),
            P(),
            P(),
            P(),
            P(),
            P(),
            P("spk", None, None),
            P("spk", None),
            P(),
        ),
        check_vma=False,
    )
```

```python
import functools

import jax
import jax.numpy as jnp
from jax import lax
from jax.experimental import pallas as pl
from jax.experimental.pallas import tpu as pltpu
from jax.sharding import PartitionSpec as P

F32 = jnp.float32
BF16 = jnp.bfloat16
LANES = 128
MESH = pl.DeviceIdType.MESH


def dot(a, b):
    return jnp.dot(a, b, preferred_element_type=F32)


def dot_tn(a, b):
    return lax.dot_general(a, b, (((0,), (0,)), ((), ())), preferred_element_type=F32)


def dot_nt(a, b):
    return lax.dot_general(a, b, (((1,), (1,)), ((), ())), preferred_element_type=F32)


def chunks(total, size, body):
    assert total % size == 0

    def step(i, carry):
        body(pl.multiple_of(i * size, size))
        return carry

    lax.fori_loop(0, total // size, step, 0)


def local_kernel(
    sizes,
    lengths_ref,
    pads_ref,
    spans_ref,
    enc_ref,
    w_in_ref,
    w_rec_ref,
    w_bias_ref,
    w_proj_ref,
    proj_bias_ref,
    gain_ref,
    shift_ref,
    mask_in_ref,
    mask_bias_in_ref,
    dec_in_ref,
    wave_grad_ref,
    wave_out,
    spans_out,
    in_out,
    rec_out,
    bias_out,
    proj_out,
    proj_bias_out,
    gain_out,
    shift_out,
    mask_out,
    mask_bias_out,
    dec_out,
    stream,
    valid,
    mx,
    xj,
    dz,
    dmj,
    normed,
    inv_all,
    u_a,
    u_e,
    hc_a,
    hc_e,
    sv_a,
    sv_e,
    gd,
    dh,
    dp,
    wis,
    wrs,
    wiu,
    wrt,
    pws,
    vec,
    enc_t,
    pre,
    masked,
    feats,
    dpre,
    mask_ref,
    dec_ref,
    send,
    own,
    got,
    wave_got,
    sems,
):
    R, K, C, H, clips, blocks, kp = sizes
    rows, rows_e = R * K, R * kp
    hop = K // 2
    frames = R * hop
    half = dec_in_ref.shape[0] // 2
    wr = frames * half // LANES
    group = LANES // half
    cr = 10 * R
    speaker = lax.axis_index("spk")
    partner = {"spk": 1 - speaker}

    barrier = pltpu.get_barrier_semaphore()
    pl.semaphore_signal(barrier, inc=1, device_id=partner, device_id_type=MESH)

    mask_row = -(-wr // 8) * 8
    for i in range(wr):
        at = pl.multiple_of(speaker * (wr * LANES) + i * LANES, LANES)
        own[i : i + 1] = wave_grad_ref[0:1, pl.ds(at, LANES)].astype(F32)
        at = pl.multiple_of((1 - speaker) * (wr * LANES) + i * LANES, LANES)
        send[i : i + 1] = wave_grad_ref[0:1, pl.ds(at, LANES)].astype(F32)
    mask_f = mask_in_ref[0].astype(F32)
    send[wr:mask_row] = jnp.zeros((mask_row - wr, LANES), F32)
    send[mask_row : mask_row + C] = jnp.concatenate([mask_f, mask_f], axis=1)
    bias_f = mask_bias_in_ref[0:1].astype(F32)
    bias_f = jnp.concatenate([bias_f, bias_f], axis=1)
    send[mask_row + C : mask_row + C + 8] = jnp.broadcast_to(bias_f, (8, LANES))
    pl.semaphore_wait(barrier, 1)
    swap = pltpu.make_async_remote_copy(
        src_ref=send, dst_ref=got, send_sem=sems.at[0], recv_sem=sems.at[1], device_id=partner, device_id_type=MESH
    )
    swap.start()

    jio = lax.broadcasted_iota(jnp.int32, (R, LANES), 0)
    lane = lax.broadcasted_iota(jnp.int32, (1, LANES), 1)
    ones_lane = (lane == C).astype(F32)

    lens = [lengths_ref[0, speaker, c] for c in range(clips)]
    pads = [pads_ref[0, speaker, c] for c in range(clips)]
    starts, ends, at = [], [], 0
    for c in range(clips):
        starts.append(at)
        at = at + lens[c]
        ends.append(at)

    def is_start(j):
        hit = j == starts[0]
        for c in range(1, clips):
            hit = jnp.logical_or(hit, j == starts[c])
        return hit

    def is_end(j):
        hit = j == ends[0] - 1
        for c in range(1, clips):
            hit = jnp.logical_or(hit, j == ends[c] - 1)
        return hit

    members, thr, inv_count = [], jnp.full((R, LANES), K, jnp.int32), jnp.zeros((R, LANES), F32)
    for c in range(clips):
        member = jnp.logical_and(jio >= starts[c], jio < ends[c]).astype(F32)
        members.append(member)
        thr = jnp.where(jio == ends[c] - 1, K - pads[c], thr)
        total = (C * (K * lens[c] - pads[c])).astype(F32)
        inv_count = inv_count + member / jnp.full((R, LANES), total, F32)
    not_first = 1.0 - is_start(jio).astype(F32)
    next_not_first = 1.0 - jnp.logical_or(is_start(jio + 1), jio == R - 1).astype(F32)

    def clip_sum(x):
        out = jnp.zeros((R, 1), F32)
        for member in members:
            out = out + member[:, :1] * jnp.sum(member * x, axis=(0, 1), keepdims=True)
        return out

    def fill_valid(r):
        k = lax.broadcasted_iota(jnp.int32, (cr // R, R, LANES), 0) + r // R
        low = lax.broadcasted_iota(jnp.int32, (cr // R, R, LANES), 2) < C
        ok = jnp.logical_and(k < thr[None], low).astype(F32)
        valid[pl.ds(r, cr)] = ok.reshape(cr, LANES)

    chunks(rows, cr, fill_valid)

    pws[...] = jnp.zeros_like(pws)
    wis[...] = jnp.zeros_like(wis)
    wiu[...] = jnp.zeros_like(wiu)
    vec[...] = jnp.zeros_like(vec)
    for b in range(blocks):
        for s in range(2):
            n = 2 * b + s
            pws[b, s, 0:C] = w_proj_ref[b, s]
            vec[n, 0:1, 0:C] = proj_bias_ref[b, s : s + 1]
            vec[n, 1:2, 0:C] = gain_ref[b, s : s + 1]
            vec[n, 2:3, 0:C] = shift_ref[b, s : s + 1]

    stream[...] = jnp.zeros_like(stream)
    for j in range(R):
        x = spans_ref[j].astype(F32)
        x = jnp.concatenate([x, jnp.zeros_like(x)], axis=0).T
        stream[pl.ds(j, K, stride=R), :] = x

    def start_stream(r):
        x = stream[pl.ds(r, cr)] * valid[pl.ds(r, cr)]
        stream[pl.ds(r, cr)] = jnp.where(lane == C, 1.0, x)

    chunks(rows, cr, start_stream)

    gate_scale = jnp.where(
        lax.broadcasted_iota(jnp.int32, (1, 4 * H), 1) // H == 2, 1.0, 0.5
    ).astype(F32)

    def lane_part(x, g):
        return x[:, g * H : (g + 1) * H]

    def gate_step(d, sv, b, r, n, p, c, keep_next):
        acts = [jnp.tanh(p[:, g * H : (g + 1) * H] + gd[d, pl.ds(r, n), g * H : (g + 1) * H]) for g in range(4)]
        ti, tf, g, to = acts
        i, f, o = 0.5 * ti + 0.5, 0.5 * tf + 0.5, 0.5 * to + 0.5
        cn = f * c + i * g
        tc = jnp.tanh(cn)
        h = o * tc
        parts = [
            g * (0.25 - 0.25 * ti * ti),
            c * (0.25 - 0.25 * tf * tf),
            i * (1.0 - g * g),
            tc * (0.25 - 0.25 * to * to),
            o * (1.0 - tc * tc),
            f,
        ]
        for m, part in enumerate(parts):
            sv[b, d, pl.ds(r, n), m * H : (m + 1) * H] = part.astype(BF16)
        if keep_next is None:
            return h.astype(BF16), h.astype(BF16), cn
        return h.astype(BF16), (h * keep_next).astype(BF16), cn * keep_next

    def run_forward(b, sec, u, hc, sv, n, steps, unroll):
        total = n * steps
        for d in range(2):
            w = w_in_ref[b, sec, d].astype(F32) * gate_scale
            wis[0:C, d * 4 * H : (d + 1) * 4 * H] = w.astype(BF16)
            wrs[d] = (w_rec_ref[b, sec, d].astype(F32) * gate_scale).astype(BF16)
        size = total // 4

        def drive(r):
            for d in range(2):
                bias = w_bias_ref[b, sec, d : d + 1] * gate_scale
                gd[d, pl.ds(r, size)] = (
                    dot(u[b, pl.ds(r, size)], wis[:, d * 4 * H : (d + 1) * 4 * H]) + bias
                )

        chunks(total, size, drive)

        def step(t, carry):
            hf, hb, cf, cb = carry
            back = steps - 1 - t
            rf = pl.multiple_of(t * n, n)
            rb = pl.multiple_of(back * n, n)
            kf = kb = None
            if sec == 1:
                kf = 1.0 - is_start(t + 1).astype(F32)
                kb = 1.0 - is_end(back - 1).astype(F32)
            pf = dot(hf, wrs[0])
            pb = dot(hb, wrs[1])
            out_f, hf, cf = gate_step(0, sv, b, rf, n, pf, cf, kf)
            out_b, hb, cb = gate_step(1, sv, b, rb, n, pb, cb, kb)
            hc[b, pl.ds(rf, n), 0:H] = out_f
            hc[b, pl.ds(rb, n), H : 2 * H] = out_b
            return hf, hb, cf, cb

        zh, zc = jnp.zeros((n, H), BF16), jnp.zeros((n, H), F32)
        lax.fori_loop(0, steps, step, (zh, zh, zc, zc), unroll=unroll)

    def norm_forward(b, sec):
        n = 2 * b + sec
        gain, shift = vec[n, 1:2], vec[n, 2:3]

        def fold(body):
            def step(i, acc):
                return acc + jnp.sum(body(pl.multiple_of(i * cr, cr)).reshape(cr // R, R, LANES), axis=0)

            return lax.fori_loop(0, rows // cr, step, jnp.zeros((R, LANES), F32))

        mean = clip_sum(fold(lambda r: valid[pl.ds(r, cr)] * mx[pl.ds(r, cr)])) * inv_count

        def spread(r):
            x = mx[pl.ds(r, cr)].reshape(cr // R, R, LANES) - mean[None]
            return valid[pl.ds(r, cr)] * (x * x).reshape(cr, LANES)

        inv = lax.rsqrt(clip_sum(fold(spread)) * inv_count + 1e-08)
        inv_all[n] = inv

        def apply(r):
            x = (mx[pl.ds(r, cr)].reshape(cr // R, R, LANES) - mean[None]) * inv[None]
            x = x.reshape(cr, LANES)
            normed[n, pl.ds(r, cr)] = x
            stream[pl.ds(r, cr)] += valid[pl.ds(r, cr)] * (x * gain + shift)

        chunks(rows, cr, apply)

    def forward_block(b, carry):
        def u_intra(r):
            u_a[b, pl.ds(r, cr)] = stream[pl.ds(r, cr)].astype(BF16)

        chunks(rows, cr, u_intra)
        run_forward(b, 0, u_a, hc_a, sv_a, R, K, 4)

        def mix_intra(r):
            mx[pl.ds(r, rows // 4)] = dot_nt(hc_a[b, pl.ds(r, rows // 4)], pws[b, 0]) + vec[2 * b, 0:1]

        chunks(rows, rows // 4, mix_intra)
        norm_forward(b, 0)

        for j in range(R):
            u_e[b, pl.ds(j * kp, kp)] = stream[pl.ds(j, kp, stride=R), :].astype(BF16)
        run_forward(b, 1, u_e, hc_e, sv_e, kp, R, 2)

        def mix_inter(r):
            xj[pl.ds(r, rows_e // 4)] = (
                dot_nt(hc_e[b, pl.ds(r, rows_e // 4)], pws[b, 1]) + vec[2 * b + 1, 0:1]
            )

        chunks(rows_e, rows_e // 4, mix_inter)
        for j in range(R):
            mx[pl.ds(j, kp, stride=R), :] = xj[pl.ds(j * kp, kp)]
        norm_forward(b, 1)
        return carry

    lax.fori_loop(0, blocks, forward_block, 0)

    e = enc_ref[...].astype(F32)
    xj[0:frames] = jnp.concatenate([e, e], axis=0).T
    for j in range(R):
        enc_t[pl.ds(j, hop, stride=R), :] = xj[j * hop : (j + 1) * hop]

    first_half = lane < half
    second_half = jnp.logical_and(lane >= half, lane < 2 * half)
    d = dec_in_ref[...].astype(F32)
    d = jnp.concatenate([d, jnp.zeros((LANES - 2 * half, C), F32)], axis=0).T
    dec_ref[0:C, 0:LANES] = jnp.where(first_half, d, 0.0).astype(BF16)
    dec_ref[C : 2 * C, 0:LANES] = jnp.where(second_half, pltpu.roll(d, half, 1), 0.0).astype(BF16)
    dec_ref[0:C, LANES : 2 * LANES] = jnp.where(first_half, pltpu.roll(d, LANES - half, 1), 0.0).astype(BF16)
    dec_ref[C : 2 * C, LANES : 2 * LANES] = jnp.where(second_half, d, 0.0).astype(BF16)

    swap.wait()
    mask_ref[...] = jnp.concatenate([mask_f, got[mask_row : mask_row + C, 0:C]], axis=1).astype(BF16)
    mask_bias = jnp.concatenate(
        [mask_bias_in_ref[0:1].astype(F32), got[mask_row + C : mask_row + C + 1, 0:C]], axis=1
    )
    for q in range(group):
        a = pltpu.roll(own[0:mask_row], LANES - q * half, 1) if q else own[0:mask_row]
        b = pltpu.roll(got[0:mask_row], (LANES - (q - 1) * half) % LANES, 1) if q != 1 else got[0:mask_row]
        w = jnp.where(first_half, a, jnp.where(second_half, b, 0.0))
        xj[pl.ds(q, wr, stride=group), :] = w[0:wr]
    for j in range(R):
        gd[1, j * hop : (j + 1) * hop, 0:LANES] = xj[j * hop : (j + 1) * hop]
    for j in range(R):
        xj[pl.ds(j, hop, stride=R), :] = gd[1, j * hop : (j + 1) * hop, 0:LANES]

    def head_pre(r):
        x = stream[pl.ds(r, cr)]
        f = x * (0.5 * jnp.tanh(0.5 * x) + 0.5)
        f = jnp.where(lane == C, 1.0, f).astype(BF16)
        feats[pl.ds(r, cr)] = f
        pre[pl.ds(r, cr)] = dot(f[:, 0:C], mask_ref[...]) + mask_bias

    chunks(rows, cr, head_pre)

    hr = frames // 5

    def tile(v):
        return jnp.broadcast_to(v[None], (hr // R, R, LANES)).reshape(hr, LANES)

    for q in range(5):
        r = q * hr
        fr = pre[r : r + hr] + tile(not_first) * pre[frames + r - 1 : frames + r - 1 + hr]
        e = enc_t[r : r + hr]
        sp = jnp.maximum(fr, 0.0) + jnp.log1p(jnp.exp(-jnp.abs(fr)))
        masked[r : r + hr] = (sp * e).astype(BF16)
        pre[r : r + hr] = e * (0.5 * jnp.tanh(0.5 * fr) + 0.5)
    for q in range(5):
        r = q * hr
        gd[0, r : r + hr, 0 : 2 * LANES] = dot(masked[r : r + hr], dec_ref[...])
    gd[1, 0:R, 0:LANES] = (
        gd[0, 0:R, 0:LANES] + not_first * gd[0, frames - R - 1 : frames - 1, LANES : 2 * LANES]
    )
    gd[1, R:frames, 0:LANES] = gd[0, R:frames, 0:LANES] + gd[0, 0 : frames - R, LANES : 2 * LANES]
    xj[frames : 2 * frames] = gd[1, 0:frames, 0:LANES]
    for j in range(R):
        gd[1, j * hop : (j + 1) * hop, 0:LANES] = xj[pl.ds(frames + j, hop, stride=R), :]
    xj[frames : 2 * frames] = gd[1, 0:frames, 0:LANES]
    zero = jnp.zeros((wr, LANES), F32)
    w_own, w_far = zero, zero
    for q in range(group):
        x = xj[pl.ds(frames + q, wr, stride=group), :]
        a = jnp.where(first_half, x, 0.0)
        b = jnp.where(second_half, x, 0.0)
        w_own = w_own + (pltpu.roll(a, q * half, 1) if q else a)
        w_far = w_far + (pltpu.roll(b, (q - 1) * half % LANES, 1) if q != 1 else b)
    own[0:wr] = w_own
    send[0:wr] = w_far
    wave_swap = pltpu.make_async_remote_copy(
        src_ref=send.at[0:mask_row],
        dst_ref=wave_got,
        send_sem=sems.at[2],
        recv_sem=sems.at[3],
        device_id=partner,
        device_id_type=MESH,
    )
    wave_swap.start()

    gd[0, 0:frames, 0:LANES] = xj[0:frames]
    gd[0, 0 : frames - R, LANES : 2 * LANES] = xj[R:frames]
    gd[0, frames - R : frames, LANES : 2 * LANES] = next_not_first * xj[1 : R + 1]
    dp[0, 0:frames, 0 : 2 * LANES] = gd[0, 0:frames, 0 : 2 * LANES].astype(BF16)
    g = dot_tn(masked[...], dp[0, 0:frames, 0 : 2 * LANES])
    g_lead = g[0:C, 0:LANES] + pltpu.roll(g[C : 2 * C, 0:LANES], LANES - half, 1)
    g_tail = pltpu.roll(g[0:C, LANES : 2 * LANES], half, 1) + g[C : 2 * C, LANES : 2 * LANES]
    g = jnp.where(first_half, g_lead, g_tail)
    dec_out[...] = jnp.concatenate([g, jnp.zeros_like(g)], axis=0).T[0 : 2 * half, 0:C]
    xj[frames : frames + 8] = jnp.zeros((8, LANES), F32)
    for q in range(5):
        r = q * hr
        dfr = dot_nt(dp[0, r : r + hr, 0 : 2 * LANES], dec_ref[...]) * pre[r : r + hr]
        xj[r : r + hr] = dfr
        dpre[r : r + hr] = dfr.astype(BF16)
    for q in range(5):
        r = q * hr
        dpre[frames + r : frames + r + hr] = (tile(next_not_first) * xj[r + 1 : r + 1 + hr]).astype(BF16)
    gm = dot_tn(feats[...], dpre[...])
    far = pltpu.roll(gm, C, 1)
    mask_out[speaker] = gm[0:C, 0:C]
    mask_out[1 - speaker] = far[0:C, 0:C]
    mask_bias_out[speaker] = gm[C : C + 1, 0:C]
    mask_bias_out[1 - speaker] = far[C : C + 1, 0:C]
    dz[...] = jnp.zeros_like(dz)

    def head_dz(r):
        x = stream[pl.ds(r, cr)]
        sg = 0.5 * jnp.tanh(0.5 * x) + 0.5
        df = dot_nt(dpre[pl.ds(r, cr)], mask_ref[...])
        df = jnp.concatenate([df, jnp.zeros_like(df)], axis=1)
        dz[pl.ds(r, cr)] = df * sg * (1.0 + x * (1.0 - sg))

    chunks(rows, cr, head_dz)

    def norm_backward(b, sec):
        n = 2 * b + sec
        gain = vec[n, 1:2]

        def sums(i, acc):
            r = pl.multiple_of(i * cr, cr)
            v = valid[pl.ds(r, cr)] * dz[pl.ds(r, cr)]
            w = v * normed[n, pl.ds(r, cr)]
            return (
                acc[0] + jnp.sum(v.reshape(cr // R, R, LANES), axis=0),
                acc[1] + jnp.sum(w.reshape(cr // R, R, LANES), axis=0),
            )

        zero = jnp.zeros((R, LANES), F32)
        s1, s2 = lax.fori_loop(0, rows // cr, sums, (zero, zero))
        shift_out[b, sec : sec + 1] = jnp.sum(s1, axis=0, keepdims=True)[:, 0:C]
        gain_out[b, sec : sec + 1] = jnp.sum(s2, axis=0, keepdims=True)[:, 0:C]
        m1 = clip_sum(s1 * gain) * inv_count
        m2 = clip_sum(s2 * gain) * inv_count
        inv = inv_all[n]

        def apply(i, acc):
            r = pl.multiple_of(i * cr, cr)
            d = (dz[pl.ds(r, cr)] * gain).reshape(cr // R, R, LANES)
            x = normed[n, pl.ds(r, cr)].reshape(cr // R, R, LANES)
            y = (d - m1[None] - x * m2[None]) * inv[None]
            y = (y.reshape(cr, LANES) * valid[pl.ds(r, cr)]).astype(BF16)
            if sec == 0:
                dmj[pl.ds(r, cr)] = y
            y = y.astype(F32)
            if sec == 1:
                mx[pl.ds(r, cr)] = y
            return acc + jnp.sum(y.reshape(cr // R, R, LANES), axis=0)

        acc = lax.fori_loop(0, rows // cr, apply, zero)
        proj_bias_out[b, sec : sec + 1] = jnp.sum(acc, axis=0, keepdims=True)[:, 0:C]

    def back_step(d, sv, b, r, n, dhn, dcn, keep):
        a = [sv[b, d, pl.ds(r, n), m * H : (m + 1) * H].astype(F32) for m in range(6)]
        g = dh[pl.ds(r, n), d * H : (d + 1) * H] + dhn
        dc = dcn + g * a[4]
        for m in range(4):
            dp[d, pl.ds(r, n), m * H : (m + 1) * H] = ((g if m == 3 else dc) * a[m]).astype(BF16)
        dhn = dot(dp[d, pl.ds(r, n)], wrt[d])
        dcn = dc * a[5]
        if keep is not None:
            dhn, dcn = dhn * keep, dcn * keep
        return dhn, dcn

    def run_backward(b, sec, u, hc, sv, n, steps, unroll):
        total = n * steps
        size = total // 4
        proj_out[b, sec] = dot_tn(dmj[0:total], hc[b])[0:C]

        def joined(r):
            dh[pl.ds(r, size)] = dot(dmj[pl.ds(r, size)], pws[b, sec])

        chunks(total, size, joined)
        for d in range(2):
            wrt[d] = w_rec_ref[b, sec, d].T
            wiu[0:C, d * 4 * H : (d + 1) * 4 * H] = w_in_ref[b, sec, d]

        def step(t, carry):
            hf, hb, cf, cb = carry
            back = steps - 1 - t
            rf = pl.multiple_of(back * n, n)
            rb = pl.multiple_of(t * n, n)
            kf = kb = None
            if sec == 1:
                kf = 1.0 - is_start(back).astype(F32)
                kb = 1.0 - is_end(t).astype(F32)
            hf, cf = back_step(0, sv, b, rf, n, hf, cf, kf)
            hb, cb = back_step(1, sv, b, rb, n, hb, cb, kb)
            return hf, hb, cf, cb

        z = jnp.zeros((n, H), F32)
        lax.fori_loop(0, steps, step, (z, z, z, z), unroll=unroll)
        if sec == 1:
            for j in range(1, steps):
                kf = (1.0 - is_start(j).astype(F32)).astype(BF16)
                at = slice((j - 1) * n, j * n)
                hc[b, at, 0:H] = hc[b, at, 0:H] * kf
                kb = (1.0 - is_end(j - 1).astype(F32)).astype(BF16)
                at = slice(j * n, (j + 1) * n)
                hc[b, at, H : 2 * H] = hc[b, at, H : 2 * H] * kb
        for d in range(2):
            g = dot_tn(u[b], dp[d, 0:total])
            in_out[b, sec, d] = g[0:C]
            bias_out[b, sec, d : d + 1] = g[C : C + 1]
        rec_out[b, sec, 0] = dot_tn(hc[b, 0 : total - n, 0:H], dp[0, n:total])
        rec_out[b, sec, 1] = dot_tn(hc[b, n:total, H : 2 * H], dp[1, 0 : total - n])

    def stream_grad(r, size):
        return dot_nt(dp[0, pl.ds(r, size)], wiu[:, 0 : 4 * H]) + dot_nt(
            dp[1, pl.ds(r, size)], wiu[:, 4 * H : 8 * H]
        )

    def backward_block(i, carry):
        b = blocks - 1 - i
        norm_backward(b, 1)
        mx[rows:rows_e] = jnp.zeros((rows_e - rows, LANES), F32)
        for j in range(R):
            dmj[pl.ds(j * kp, kp)] = mx[pl.ds(j, kp, stride=R), :].astype(BF16)
        run_backward(b, 1, u_e, hc_e, sv_e, kp, R, 2)

        def grad_inter(r):
            xj[pl.ds(r, rows_e // 4)] = stream_grad(r, rows_e // 4)

        chunks(rows_e, rows_e // 4, grad_inter)
        for j in range(R):
            dz[pl.ds(j, kp, stride=R), :] += xj[pl.ds(j * kp, kp)]

        norm_backward(b, 0)
        run_backward(b, 0, u_a, hc_a, sv_a, R, K, 4)

        def grad_intra(r):
            dz[pl.ds(r, rows // 4)] += stream_grad(r, rows // 4)

        chunks(rows, rows // 4, grad_intra)
        return carry

    lax.fori_loop(0, blocks, backward_block, 0)

    def finish(r):
        dz[pl.ds(r, cr)] = dz[pl.ds(r, cr)] * valid[pl.ds(r, cr)]

    chunks(rows, cr, finish)
    for j in range(R):
        spans_out[j] = dz[pl.ds(j, K, stride=R), :].T[0:C]
    wave_swap.wait()
    for i in range(wr):
        at = pl.multiple_of(speaker * (wr * LANES) + i * LANES, LANES)
        wave_out[0:1, pl.ds(at, LANES)] = own[i : i + 1]
        at = pl.multiple_of((1 - speaker) * (wr * LANES) + i * LANES, LANES)
        wave_out[0:1, pl.ds(at, LANES)] = wave_got[i : i + 1]


def shards(
    spans,
    encoded,
    clip_lengths,
    clip_pads,
    lstm_in,
    lstm_rec,
    lstm_bias,
    proj_weight,
    proj_bias,
    gln_gain,
    gln_shift,
    mask_weight,
    mask_bias,
    dec_weight,
    wave_grad,
):
    speaker = lax.axis_index("spk")
    R, K, C = spans.shape
    H = lstm_rec.shape[3]
    blocks = lstm_in.shape[0]
    clips = clip_lengths.shape[2]
    frames = encoded.shape[0]
    half = dec_weight.shape[1] // 2
    kp = -(-K // 16) * 16
    rows, rows_e = R * K, R * kp
    wr = frames * half // LANES
    mask_row = -(-wr // 8) * 8

    sizes = (R, K, C, H, clips, blocks, kp)
    smem = pl.BlockSpec(memory_space=pltpu.SMEM)
    vmem = pl.BlockSpec(memory_space=pltpu.VMEM)
    shape = jax.ShapeDtypeStruct
    outs = pl.pallas_call(
        functools.partial(local_kernel, sizes),
        out_shape=(
            shape((1, 2 * frames * half), F32),
            shape((R, C, K), F32),
            shape((blocks, 2, 2, C, 4 * H), F32),
            shape((blocks, 2, 2, H, 4 * H), F32),
            shape((blocks, 2, 2, 4 * H), F32),
            shape((blocks, 2, C, 2 * H), F32),
            shape((blocks, 2, C), F32),
            shape((blocks, 2, C), F32),
            shape((blocks, 2, C), F32),
            shape((2, C, C), F32),
            shape((2, 1, C), F32),
            shape((2 * half, C), F32),
        ),
        in_specs=[smem, smem] + [vmem] * 13,
        out_specs=tuple([vmem] * 12),
        scratch_shapes=[
            pltpu.VMEM((rows_e, LANES), F32),
            pltpu.VMEM((rows, LANES), F32),
            pltpu.VMEM((rows_e, LANES), F32),
            pltpu.VMEM((rows_e, LANES), F32),
            pltpu.VMEM((rows_e, LANES), F32),
            pltpu.VMEM((rows_e, LANES), BF16),
            pltpu.VMEM((2 * blocks, rows, LANES), F32),
            pltpu.VMEM((2 * blocks, R, LANES), F32),
            pltpu.VMEM((blocks, rows, LANES), BF16),
            pltpu.VMEM((blocks, rows_e, LANES), BF16),
            pltpu.VMEM((blocks, rows, 2 * H), BF16),
            pltpu.VMEM((blocks, rows_e, 2 * H), BF16),
            pltpu.VMEM((blocks, 2, rows, 6 * H), BF16),
            pltpu.VMEM((blocks, 2, rows_e, 6 * H), BF16),
            pltpu.VMEM((2, rows_e, 4 * H), F32),
            pltpu.VMEM((rows_e, 2 * H), F32),
            pltpu.VMEM((2, rows_e, 4 * H), BF16),
            pltpu.VMEM((LANES, 8 * H), BF16),
            pltpu.VMEM((2, H, 4 * H), BF16),
            pltpu.VMEM((LANES, 8 * H), BF16),
            pltpu.VMEM((2, 4 * H, H), BF16),
            pltpu.VMEM((blocks, 2, LANES, 2 * H), BF16),
            pltpu.VMEM((2 * blocks, 8, LANES), F32),
            pltpu.VMEM((frames, LANES), F32),
            pltpu.VMEM((rows, LANES), F32),
            pltpu.VMEM((frames, LANES), BF16),
            pltpu.VMEM((rows, LANES), BF16),
            pltpu.VMEM((rows, LANES), BF16),
            pltpu.VMEM((C, 2 * C), BF16),
            pltpu.VMEM((2 * C, 2 * LANES), BF16),
            pltpu.VMEM((mask_row + C + 8, LANES), F32),
            pltpu.VMEM((mask_row, LANES), F32),
            pltpu.VMEM((mask_row + C + 8, LANES), F32),
            pltpu.VMEM((mask_row, LANES), F32),
            pltpu.SemaphoreType.DMA((4,)),
        ],
        compiler_params=pltpu.CompilerParams(
            vmem_limit_bytes=62 * 1024 * 1024, collective_id=0, has_side_effects=True
        ),
        name="dual_path",
    )(
        clip_lengths,
        clip_pads,
        spans.transpose(0, 2, 1),
        encoded.T,
        lstm_in,
        lstm_rec,
        lstm_bias,
        proj_weight.transpose(0, 1, 3, 2),
        proj_bias,
        gln_gain,
        gln_shift,
        mask_weight,
        mask_bias,
        dec_weight.T,
        wave_grad,
    )
    summed = lax.psum(outs[2:], ("dp", "spk"))
    return (
        outs[0],
        outs[1].transpose(0, 2, 1),
        summed[0],
        summed[1],
        summed[2],
        summed[3].transpose(0, 1, 3, 2),
        summed[4],
        summed[5],
        summed[6],
        lax.dynamic_slice_in_dim(summed[7], speaker, 1, 0),
        lax.dynamic_slice_in_dim(summed[8][:, 0], speaker, 1, 0),
        summed[9].T,
    )


def solution(mesh):
    return jax.shard_map(
        shards,
        mesh=mesh,
        in_specs=(
            P(("dp", "spk"), None, None),
            P(("dp", "spk"), None),
            P("dp", None, None),
            P("dp", None, None),
            P(),
            P(),
            P(),
            P(),
            P(),
            P(),
            P(),
            P("spk", None, None),
            P("spk", None),
            P(),
            P("spk", "dp"),
        ),
        out_specs=(
            P("spk", "dp"),
            P(("dp", "spk"), None, None),
            P(),
            P(),
            P(),
            P(),
            P(),
            P(),
            P(),
            P("spk", None, None),
            P("spk", None),
            P(),
        ),
        check_vma=False,
    )
```

```python
import functools

import jax
import jax.numpy as jnp
from jax import lax
from jax.experimental import pallas as pl
from jax.experimental.pallas import tpu as pltpu
from jax.sharding import PartitionSpec as P

F32 = jnp.float32
BF16 = jnp.bfloat16
LANES = 128
PART = 16
MESH = pl.DeviceIdType.MESH


def dot(a, b):
    return jnp.dot(a, b, preferred_element_type=F32)


def dot_tn(a, b):
    return lax.dot_general(a, b, (((0,), (0,)), ((), ())), preferred_element_type=F32)


def dot_nt(a, b):
    return lax.dot_general(a, b, (((1,), (1,)), ((), ())), preferred_element_type=F32)


def chunks(total, size, body):
    assert total % size == 0

    def step(i, carry):
        body(pl.multiple_of(i * size, size))
        return carry

    lax.fori_loop(0, total // size, step, 0)


class Butterfly:
    def __init__(self, buf, recv, out, sems, hops):
        self.buf, self.recv, self.out, self.sems = buf, recv, out, sems
        self.steps = []
        size, off, at = buf.shape[0], 0, 0
        back = []
        for p, (bit, partner) in enumerate(hops):
            if size > PART:
                size //= 2
                keep, give = off + bit * size, off + (1 - bit) * size
                back.append((p, keep, size, partner))
            else:
                keep = give = off
            self.steps.append((self.give, self.take, (p, give, keep, at, size, partner)))
            off = keep
            at += size
        self.part = off, size
        self.last = len(self.steps)
        for p, keep, size, partner in reversed(back):
            self.steps.append((self.spread, None, (len(hops) + p, keep, size, partner)))
        self.pending = None
        self.done = 0

    def copy(self, p, src, dst, partner):
        return pltpu.make_async_remote_copy(
            src_ref=src,
            dst_ref=dst,
            send_sem=self.sems.at[p, 0],
            recv_sem=self.sems.at[p, 1],
            device_id=partner,
            device_id_type=MESH,
        )

    def give(self, p, give, keep, at, size, partner):
        rows = self.buf.at[pl.ds(pl.multiple_of(give, PART), size)]
        return self.copy(p, rows, self.recv.at[at : at + size], partner)

    def take(self, p, give, keep, at, size, partner):
        def add(i, carry):
            own = pl.ds(pl.multiple_of(keep + i * PART, PART), PART)
            new = self.recv[pl.ds(pl.multiple_of(at + i * PART, PART), PART)]
            self.buf[own] = (self.buf[own].astype(F32) + new.astype(F32)).astype(BF16)
            return carry

        lax.fori_loop(0, size // PART, add, 0)

    def spread(self, p, keep, size, partner):
        rows = self.out.at[pl.ds(pl.multiple_of(keep, PART), size)]
        return self.copy(p, rows, rows, partner)

    def advance(self):
        if self.pending is not None:
            copy, after, what = self.pending
            copy.wait()
            if after is not None:
                after(*what)
            self.pending = None
        if self.done == self.last:
            off, size = self.part
            rows = pl.ds(pl.multiple_of(off, PART), size)
            self.out[rows] = self.buf[rows]
        if self.done < len(self.steps):
            start, after, what = self.steps[self.done]
            copy = start(*what)
            copy.start()
            self.pending = (copy, after, what)
            self.done += 1

    def over(self):
        return self.pending is None and self.done == len(self.steps)


def hops_of(num_dp):
    dp, spk = lax.axis_index("dp"), lax.axis_index("spk")
    bits = num_dp.bit_length() - 1

    def bit(k):
        return dp // (1 << k) % 2

    def flip(k, amount=1):
        return dp + amount * (1 - 2 * bit(k)) * (1 << k)

    def along_dp(k):
        return bit(k), {"dp": flip(k), "spk": spk}

    hops = [along_dp(0)]
    first = 1 - bit(0)
    second = bit(0)
    for a, b in ((first, second), (second, first)):
        hops.append(
            (a * bit(1) + b * spk, {"dp": flip(1, a), "spk": spk + b * (1 - 2 * spk)})
        )
    return hops + [along_dp(k) for k in range(2, bits)]


def local_kernel(
    sizes,
    lengths_ref,
    pads_ref,
    spans_ref,
    enc_ref,
    w_in_ref,
    w_rec_ref,
    w_bias_ref,
    w_proj_ref,
    proj_bias_ref,
    gain_ref,
    shift_ref,
    mask_in_ref,
    mask_bias_in_ref,
    dec_in_ref,
    wave_grad_ref,
    wave_out,
    spans_out,
    all_sums,
    stream,
    valid,
    mx,
    xj,
    dz,
    dmj,
    normed,
    inv_all,
    u_a,
    u_e,
    hc_a,
    hc_e,
    sv_a,
    sv_e,
    gd,
    dh,
    dp,
    wis,
    wrs,
    wiu,
    wrt,
    pws,
    vec,
    enc_t,
    pre,
    masked,
    feats,
    dpre,
    mask_ref,
    dec_ref,
    send,
    own,
    got,
    wave_got,
    sems,
    sums,
    recv,
    small,
    sum_sems,
):
    R, K, C, H, clips, blocks, kp, num_dp = sizes
    rows, rows_e = R * K, R * kp
    hop = K // 2
    frames = R * hop
    half = dec_in_ref.shape[0] // 2
    wr = frames * half // LANES
    group = LANES // half
    cr = 10 * R
    speaker = lax.axis_index("spk")
    partner = {"spk": 1 - speaker}

    barrier = pltpu.get_barrier_semaphore()
    hops = hops_of(num_dp)
    for bit, device in hops:
        pl.semaphore_signal(barrier, inc=1, device_id=device, device_id_type=MESH)

    mask_row = -(-wr // 8) * 8
    for i in range(wr):
        at = pl.multiple_of(speaker * (wr * LANES) + i * LANES, LANES)
        own[i : i + 1] = wave_grad_ref[0:1, pl.ds(at, LANES)].astype(F32)
        at = pl.multiple_of((1 - speaker) * (wr * LANES) + i * LANES, LANES)
        send[i : i + 1] = wave_grad_ref[0:1, pl.ds(at, LANES)].astype(F32)
    mask_f = mask_in_ref[0].astype(F32)
    send[wr:mask_row] = jnp.zeros((mask_row - wr, LANES), F32)
    send[mask_row : mask_row + C] = jnp.concatenate([mask_f, mask_f], axis=1)
    bias_f = mask_bias_in_ref[0:1].astype(F32)
    bias_f = jnp.concatenate([bias_f, bias_f], axis=1)
    send[mask_row + C : mask_row + C + 8] = jnp.broadcast_to(bias_f, (8, LANES))
    pl.semaphore_wait(barrier, len(hops))
    swap = pltpu.make_async_remote_copy(
        src_ref=send, dst_ref=got, send_sem=sems.at[0], recv_sem=sems.at[1], device_id=partner, device_id_type=MESH
    )
    swap.start()

    jio = lax.broadcasted_iota(jnp.int32, (R, LANES), 0)
    lane = lax.broadcasted_iota(jnp.int32, (1, LANES), 1)
    ones_lane = (lane == C).astype(F32)

    lens = [lengths_ref[0, speaker, c] for c in range(clips)]
    pads = [pads_ref[0, speaker, c] for c in range(clips)]
    starts, ends, at = [], [], 0
    for c in range(clips):
        starts.append(at)
        at = at + lens[c]
        ends.append(at)

    def is_start(j):
        hit = j == starts[0]
        for c in range(1, clips):
            hit = jnp.logical_or(hit, j == starts[c])
        return hit

    def is_end(j):
        hit = j == ends[0] - 1
        for c in range(1, clips):
            hit = jnp.logical_or(hit, j == ends[c] - 1)
        return hit

    members, thr, inv_count = [], jnp.full((R, LANES), K, jnp.int32), jnp.zeros((R, LANES), F32)
    for c in range(clips):
        member = jnp.logical_and(jio >= starts[c], jio < ends[c]).astype(F32)
        members.append(member)
        thr = jnp.where(jio == ends[c] - 1, K - pads[c], thr)
        count = (C * (K * lens[c] - pads[c])).astype(F32)
        inv_count = inv_count + member / jnp.full((R, LANES), count, F32)
    not_first = 1.0 - is_start(jio).astype(F32)
    next_not_first = 1.0 - jnp.logical_or(is_start(jio + 1), jio == R - 1).astype(F32)

    def clip_sum(x):
        out = jnp.zeros((R, 1), F32)
        for member in members:
            out = out + member[:, :1] * jnp.sum(member * x, axis=(0, 1), keepdims=True)
        return out

    def fill_valid(r):
        k = lax.broadcasted_iota(jnp.int32, (cr // R, R, LANES), 0) + r // R
        low = lax.broadcasted_iota(jnp.int32, (cr // R, R, LANES), 2) < C
        ok = jnp.logical_and(k < thr[None], low).astype(F32)
        valid[pl.ds(r, cr)] = ok.reshape(cr, LANES)

    chunks(rows, cr, fill_valid)

    reduces = [Butterfly(sums.at[n], recv.at[n], all_sums.at[n], sum_sems.at[n], hops) for n in range(2 * blocks)]
    lay = sum_rows(C, H)
    active = []

    def point():
        for reduce in active:
            reduce.advance()

    for n in range(2 * blocks):
        sums[n, lay["head"] :] = jnp.zeros((sums.shape[1] - lay["head"], 4 * H), BF16)

    pws[...] = jnp.zeros_like(pws)
    wis[...] = jnp.zeros_like(wis)
    wiu[...] = jnp.zeros_like(wiu)
    vec[...] = jnp.zeros_like(vec)
    for b in range(blocks):
        for s in range(2):
            n = 2 * b + s
            pws[b, s, 0:C] = w_proj_ref[b, s]
            vec[n, 0:1, 0:C] = proj_bias_ref[b, s : s + 1]
            vec[n, 1:2, 0:C] = gain_ref[b, s : s + 1]
            vec[n, 2:3, 0:C] = shift_ref[b, s : s + 1]

    stream[...] = jnp.zeros_like(stream)
    for j in range(R):
        x = spans_ref[j].astype(F32)
        x = jnp.concatenate([x, jnp.zeros_like(x)], axis=0).T
        stream[pl.ds(j, K, stride=R), :] = x

    def start_stream(r):
        x = stream[pl.ds(r, cr)] * valid[pl.ds(r, cr)]
        stream[pl.ds(r, cr)] = jnp.where(lane == C, 1.0, x)

    chunks(rows, cr, start_stream)

    gate_scale = jnp.where(
        lax.broadcasted_iota(jnp.int32, (1, 4 * H), 1) // H == 2, 1.0, 0.5
    ).astype(F32)

    def lane_part(x, g):
        return x[:, g * H : (g + 1) * H]

    def gate_step(d, sv, b, r, n, p, c, keep_next):
        acts = [jnp.tanh(p[:, g * H : (g + 1) * H] + gd[d, pl.ds(r, n), g * H : (g + 1) * H]) for g in range(4)]
        ti, tf, g, to = acts
        i, f, o = 0.5 * ti + 0.5, 0.5 * tf + 0.5, 0.5 * to + 0.5
        cn = f * c + i * g
        tc = jnp.tanh(cn)
        h = o * tc
        parts = [
            g * (0.25 - 0.25 * ti * ti),
            c * (0.25 - 0.25 * tf * tf),
            i * (1.0 - g * g),
            tc * (0.25 - 0.25 * to * to),
            o * (1.0 - tc * tc),
            f,
        ]
        for m, part in enumerate(parts):
            sv[b, d, pl.ds(r, n), m * H : (m + 1) * H] = part.astype(BF16)
        if keep_next is None:
            return h.astype(BF16), h.astype(BF16), cn
        return h.astype(BF16), (h * keep_next).astype(BF16), cn * keep_next

    def run_forward(b, sec, u, hc, sv, n, steps, unroll):
        total = n * steps
        for d in range(2):
            w = w_in_ref[b, sec, d].astype(F32) * gate_scale
            wis[0:C, d * 4 * H : (d + 1) * 4 * H] = w.astype(BF16)
            wrs[d] = (w_rec_ref[b, sec, d].astype(F32) * gate_scale).astype(BF16)
        size = total // 4

        def drive(r):
            for d in range(2):
                bias = w_bias_ref[b, sec, d : d + 1] * gate_scale
                gd[d, pl.ds(r, size)] = (
                    dot(u[b, pl.ds(r, size)], wis[:, d * 4 * H : (d + 1) * 4 * H]) + bias
                )

        chunks(total, size, drive)

        def step(t, carry):
            hf, hb, cf, cb = carry
            back = steps - 1 - t
            rf = pl.multiple_of(t * n, n)
            rb = pl.multiple_of(back * n, n)
            kf = kb = None
            if sec == 1:
                kf = 1.0 - is_start(t + 1).astype(F32)
                kb = 1.0 - is_end(back - 1).astype(F32)
            pf = dot(hf, wrs[0])
            pb = dot(hb, wrs[1])
            out_f, hf, cf = gate_step(0, sv, b, rf, n, pf, cf, kf)
            out_b, hb, cb = gate_step(1, sv, b, rb, n, pb, cb, kb)
            hc[b, pl.ds(rf, n), 0:H] = out_f
            hc[b, pl.ds(rb, n), H : 2 * H] = out_b
            return hf, hb, cf, cb

        zh, zc = jnp.zeros((n, H), BF16), jnp.zeros((n, H), F32)
        lax.fori_loop(0, steps, step, (zh, zh, zc, zc), unroll=unroll)

    def norm_forward(b, sec):
        n = 2 * b + sec
        gain, shift = vec[n, 1:2], vec[n, 2:3]

        def fold(body):
            def step(i, acc):
                return acc + jnp.sum(body(pl.multiple_of(i * cr, cr)).reshape(cr // R, R, LANES), axis=0)

            return lax.fori_loop(0, rows // cr, step, jnp.zeros((R, LANES), F32))

        mean = clip_sum(fold(lambda r: valid[pl.ds(r, cr)] * mx[pl.ds(r, cr)])) * inv_count

        def spread(r):
            x = mx[pl.ds(r, cr)].reshape(cr // R, R, LANES) - mean[None]
            return valid[pl.ds(r, cr)] * (x * x).reshape(cr, LANES)

        inv = lax.rsqrt(clip_sum(fold(spread)) * inv_count + 1e-08)
        inv_all[n] = inv

        def apply(r):
            x = (mx[pl.ds(r, cr)].reshape(cr // R, R, LANES) - mean[None]) * inv[None]
            x = x.reshape(cr, LANES)
            normed[n, pl.ds(r, cr)] = x
            stream[pl.ds(r, cr)] += valid[pl.ds(r, cr)] * (x * gain + shift)

        chunks(rows, cr, apply)

    def forward_block(b, carry):
        def u_intra(r):
            u_a[b, pl.ds(r, cr)] = stream[pl.ds(r, cr)].astype(BF16)

        chunks(rows, cr, u_intra)
        run_forward(b, 0, u_a, hc_a, sv_a, R, K, 4)

        def mix_intra(r):
            mx[pl.ds(r, rows // 4)] = dot_nt(hc_a[b, pl.ds(r, rows // 4)], pws[b, 0]) + vec[2 * b, 0:1]

        chunks(rows, rows // 4, mix_intra)
        norm_forward(b, 0)

        for j in range(R):
            u_e[b, pl.ds(j * kp, kp)] = stream[pl.ds(j, kp, stride=R), :].astype(BF16)
        run_forward(b, 1, u_e, hc_e, sv_e, kp, R, 2)

        def mix_inter(r):
            xj[pl.ds(r, rows_e // 4)] = (
                dot_nt(hc_e[b, pl.ds(r, rows_e // 4)], pws[b, 1]) + vec[2 * b + 1, 0:1]
            )

        chunks(rows_e, rows_e // 4, mix_inter)
        for j in range(R):
            mx[pl.ds(j, kp, stride=R), :] = xj[pl.ds(j * kp, kp)]
        norm_forward(b, 1)
        return carry

    lax.fori_loop(0, blocks, forward_block, 0)

    e = enc_ref[...].astype(F32)
    xj[0:frames] = jnp.concatenate([e, e], axis=0).T
    for j in range(R):
        enc_t[pl.ds(j, hop, stride=R), :] = xj[j * hop : (j + 1) * hop]

    first_half = lane < half
    second_half = jnp.logical_and(lane >= half, lane < 2 * half)
    d = dec_in_ref[...].astype(F32)
    d = jnp.concatenate([d, jnp.zeros((LANES - 2 * half, C), F32)], axis=0).T
    dec_ref[0:C, 0:LANES] = jnp.where(first_half, d, 0.0).astype(BF16)
    dec_ref[C : 2 * C, 0:LANES] = jnp.where(second_half, pltpu.roll(d, half, 1), 0.0).astype(BF16)
    dec_ref[0:C, LANES : 2 * LANES] = jnp.where(first_half, pltpu.roll(d, LANES - half, 1), 0.0).astype(BF16)
    dec_ref[C : 2 * C, LANES : 2 * LANES] = jnp.where(second_half, d, 0.0).astype(BF16)

    swap.wait()
    mask_ref[...] = jnp.concatenate([mask_f, got[mask_row : mask_row + C, 0:C]], axis=1).astype(BF16)
    mask_bias = jnp.concatenate(
        [mask_bias_in_ref[0:1].astype(F32), got[mask_row + C : mask_row + C + 1, 0:C]], axis=1
    )
    for q in range(group):
        a = pltpu.roll(own[0:mask_row], LANES - q * half, 1) if q else own[0:mask_row]
        b = pltpu.roll(got[0:mask_row], (LANES - (q - 1) * half) % LANES, 1) if q != 1 else got[0:mask_row]
        w = jnp.where(first_half, a, jnp.where(second_half, b, 0.0))
        xj[pl.ds(q, wr, stride=group), :] = w[0:wr]
    for j in range(R):
        gd[1, j * hop : (j + 1) * hop, 0:LANES] = xj[j * hop : (j + 1) * hop]
    for j in range(R):
        xj[pl.ds(j, hop, stride=R), :] = gd[1, j * hop : (j + 1) * hop, 0:LANES]

    def head_pre(r):
        x = stream[pl.ds(r, cr)]
        f = x * (0.5 * jnp.tanh(0.5 * x) + 0.5)
        f = jnp.where(lane == C, 1.0, f).astype(BF16)
        feats[pl.ds(r, cr)] = f
        pre[pl.ds(r, cr)] = dot(f[:, 0:C], mask_ref[...]) + mask_bias

    chunks(rows, cr, head_pre)

    hr = frames // 5

    def tile(v):
        return jnp.broadcast_to(v[None], (hr // R, R, LANES)).reshape(hr, LANES)

    for q in range(5):
        r = q * hr
        fr = pre[r : r + hr] + tile(not_first) * pre[frames + r - 1 : frames + r - 1 + hr]
        e = enc_t[r : r + hr]
        sp = jnp.maximum(fr, 0.0) + jnp.log1p(jnp.exp(-jnp.abs(fr)))
        masked[r : r + hr] = (sp * e).astype(BF16)
        pre[r : r + hr] = e * (0.5 * jnp.tanh(0.5 * fr) + 0.5)
    for q in range(5):
        r = q * hr
        gd[0, r : r + hr, 0 : 2 * LANES] = dot(masked[r : r + hr], dec_ref[...])
    gd[1, 0:R, 0:LANES] = (
        gd[0, 0:R, 0:LANES] + not_first * gd[0, frames - R - 1 : frames - 1, LANES : 2 * LANES]
    )
    gd[1, R:frames, 0:LANES] = gd[0, R:frames, 0:LANES] + gd[0, 0 : frames - R, LANES : 2 * LANES]
    xj[frames : 2 * frames] = gd[1, 0:frames, 0:LANES]
    for j in range(R):
        gd[1, j * hop : (j + 1) * hop, 0:LANES] = xj[pl.ds(frames + j, hop, stride=R), :]
    xj[frames : 2 * frames] = gd[1, 0:frames, 0:LANES]
    zero = jnp.zeros((wr, LANES), F32)
    w_own, w_far = zero, zero
    for q in range(group):
        x = xj[pl.ds(frames + q, wr, stride=group), :]
        a = jnp.where(first_half, x, 0.0)
        b = jnp.where(second_half, x, 0.0)
        w_own = w_own + (pltpu.roll(a, q * half, 1) if q else a)
        w_far = w_far + (pltpu.roll(b, (q - 1) * half % LANES, 1) if q != 1 else b)
    own[0:wr] = w_own
    send[0:wr] = w_far
    wave_swap = pltpu.make_async_remote_copy(
        src_ref=send.at[0:mask_row],
        dst_ref=wave_got,
        send_sem=sems.at[2],
        recv_sem=sems.at[3],
        device_id=partner,
        device_id_type=MESH,
    )
    wave_swap.start()

    gd[0, 0:frames, 0:LANES] = xj[0:frames]
    gd[0, 0 : frames - R, LANES : 2 * LANES] = xj[R:frames]
    gd[0, frames - R : frames, LANES : 2 * LANES] = next_not_first * xj[1 : R + 1]
    dp[0, 0:frames, 0 : 2 * LANES] = gd[0, 0:frames, 0 : 2 * LANES].astype(BF16)
    g = dot_tn(masked[...], dp[0, 0:frames, 0 : 2 * LANES])
    g_lead = g[0:C, 0:LANES] + pltpu.roll(g[C : 2 * C, 0:LANES], LANES - half, 1)
    g_tail = pltpu.roll(g[0:C, LANES : 2 * LANES], half, 1) + g[C : 2 * C, LANES : 2 * LANES]
    g = jnp.where(first_half, g_lead, g_tail)
    g_dec = jnp.concatenate([g, jnp.zeros_like(g)], axis=0).T[0 : 2 * half]
    xj[frames : frames + 8] = jnp.zeros((8, LANES), F32)
    for q in range(5):
        r = q * hr
        dfr = dot_nt(dp[0, r : r + hr, 0 : 2 * LANES], dec_ref[...]) * pre[r : r + hr]
        xj[r : r + hr] = dfr
        dpre[r : r + hr] = dfr.astype(BF16)
    for q in range(5):
        r = q * hr
        dpre[frames + r : frames + r + hr] = (tile(next_not_first) * xj[r + 1 : r + 1 + hr]).astype(BF16)
    gm = dot_tn(feats[...], dpre[...])
    gm = jnp.where(speaker == 0, gm, pltpu.roll(gm, C, 1))
    n, at = 2 * blocks - 1, lay["head"]
    for q in range(4):
        sums[n, at : at + 16, q * LANES : (q + 1) * LANES] = gm[16 * q : 16 * q + 16].astype(BF16)
    sums[n, at + 16 : at + 32, 0:LANES] = jnp.where(lane < C, g_dec, 0.0).astype(BF16)
    sums[n, at + 16 : at + 32, LANES : 2 * LANES] = jnp.broadcast_to(gm[C : C + 1], (16, LANES)).astype(BF16)
    dz[...] = jnp.zeros_like(dz)

    def head_dz(r):
        x = stream[pl.ds(r, cr)]
        sg = 0.5 * jnp.tanh(0.5 * x) + 0.5
        df = dot_nt(dpre[pl.ds(r, cr)], mask_ref[...])
        df = jnp.concatenate([df, jnp.zeros_like(df)], axis=1)
        dz[pl.ds(r, cr)] = df * sg * (1.0 + x * (1.0 - sg))

    chunks(rows, cr, head_dz)

    def norm_backward(b, sec):
        n = 2 * b + sec
        gain = vec[n, 1:2]

        def sums(i, acc):
            r = pl.multiple_of(i * cr, cr)
            v = valid[pl.ds(r, cr)] * dz[pl.ds(r, cr)]
            w = v * normed[n, pl.ds(r, cr)]
            return (
                acc[0] + jnp.sum(v.reshape(cr // R, R, LANES), axis=0),
                acc[1] + jnp.sum(w.reshape(cr // R, R, LANES), axis=0),
            )

        zero = jnp.zeros((R, LANES), F32)
        s1, s2 = lax.fori_loop(0, rows // cr, sums, (zero, zero))
        small[2:3, LANES : 2 * LANES] = jnp.sum(s2, axis=0, keepdims=True)
        small[2:3, 2 * LANES : 3 * LANES] = jnp.sum(s1, axis=0, keepdims=True)
        m1 = clip_sum(s1 * gain) * inv_count
        m2 = clip_sum(s2 * gain) * inv_count
        inv = inv_all[n]

        def apply(i, acc):
            r = pl.multiple_of(i * cr, cr)
            d = (dz[pl.ds(r, cr)] * gain).reshape(cr // R, R, LANES)
            x = normed[n, pl.ds(r, cr)].reshape(cr // R, R, LANES)
            y = (d - m1[None] - x * m2[None]) * inv[None]
            y = (y.reshape(cr, LANES) * valid[pl.ds(r, cr)]).astype(BF16)
            if sec == 0:
                dmj[pl.ds(r, cr)] = y
            y = y.astype(F32)
            if sec == 1:
                mx[pl.ds(r, cr)] = y
            return acc + jnp.sum(y.reshape(cr // R, R, LANES), axis=0)

        acc = lax.fori_loop(0, rows // cr, apply, zero)
        small[2:3, 0:LANES] = jnp.sum(acc, axis=0, keepdims=True)

    def back_step(d, sv, b, r, n, dhn, dcn, keep):
        a = [sv[b, d, pl.ds(r, n), m * H : (m + 1) * H].astype(F32) for m in range(6)]
        g = dh[pl.ds(r, n), d * H : (d + 1) * H] + dhn
        dc = dcn + g * a[4]
        for m in range(4):
            dp[d, pl.ds(r, n), m * H : (m + 1) * H] = ((g if m == 3 else dc) * a[m]).astype(BF16)
        dhn = dot(dp[d, pl.ds(r, n)], wrt[d])
        dcn = dc * a[5]
        if keep is not None:
            dhn, dcn = dhn * keep, dcn * keep
        return dhn, dcn

    def run_backward(b, sec, u, hc, sv, n, steps, unroll, parts):
        total = n * steps
        size = total // 4
        out = sums.at[2 * b + sec]
        g = dot_tn(dmj[0:total], hc[b])[0:C].astype(BF16)
        at = lay["proj"]
        out[at : at + C // 2, 0 : 2 * H] = g[0 : C // 2]
        out[at : at + C // 2, 2 * H : 4 * H] = g[C // 2 : C]
        point()

        def joined(r):
            dh[pl.ds(r, size)] = dot(dmj[pl.ds(r, size)], pws[b, sec])

        chunks(total, size, joined)
        for d in range(2):
            wrt[d] = w_rec_ref[b, sec, d].T
            wiu[0:C, d * 4 * H : (d + 1) * 4 * H] = w_in_ref[b, sec, d]

        def step(t, carry):
            hf, hb, cf, cb = carry
            back = steps - 1 - t
            rf = pl.multiple_of(back * n, n)
            rb = pl.multiple_of(t * n, n)
            kf = kb = None
            if sec == 1:
                kf = 1.0 - is_start(back).astype(F32)
                kb = 1.0 - is_end(t).astype(F32)
            hf, cf = back_step(0, sv, b, rf, n, hf, cf, kf)
            hb, cb = back_step(1, sv, b, rb, n, hb, cb, kb)
            return hf, hb, cf, cb

        z = jnp.zeros((n, H), F32)
        carry = (z, z, z, z)
        point()
        for p in range(parts):
            carry = lax.fori_loop(p * steps // parts, (p + 1) * steps // parts, step, carry, unroll=unroll)
            point()
        if sec == 1:
            for j in range(1, steps):
                kf = (1.0 - is_start(j).astype(F32)).astype(BF16)
                at = slice((j - 1) * n, j * n)
                hc[b, at, 0:H] = hc[b, at, 0:H] * kf
                kb = (1.0 - is_end(j - 1).astype(F32)).astype(BF16)
                at = slice(j * n, (j + 1) * n)
                hc[b, at, H : 2 * H] = hc[b, at, H : 2 * H] * kb
        for d in range(2):
            g = dot_tn(u[b], dp[d, 0:total])
            out[lay["in"] + d * C : lay["in"] + (d + 1) * C] = g[0:C].astype(BF16)
            small[d : d + 1] = g[C : C + 1]
        at = lay["rec"]
        out[at : at + H] = dot_tn(hc[b, 0 : total - n, 0:H], dp[0, n:total]).astype(BF16)
        out[at + H : at + 2 * H] = dot_tn(hc[b, n:total, H : 2 * H], dp[1, 0 : total - n]).astype(BF16)
        out[lay["small"] : lay["small"] + 16] = small[...].astype(BF16)
        active.append(reduces[2 * b + sec])
        point()

    def stream_grad(r, size):
        return dot_nt(dp[0, pl.ds(r, size)], wiu[:, 0 : 4 * H]) + dot_nt(
            dp[1, pl.ds(r, size)], wiu[:, 4 * H : 8 * H]
        )

    small[...] = jnp.zeros_like(small)
    for b in reversed(range(blocks)):
        norm_backward(b, 1)
        mx[rows:rows_e] = jnp.zeros((rows_e - rows, LANES), F32)
        for j in range(R):
            dmj[pl.ds(j * kp, kp)] = mx[pl.ds(j, kp, stride=R), :].astype(BF16)
        run_backward(b, 1, u_e, hc_e, sv_e, kp, R, 2, 2)

        def grad_inter(r):
            xj[pl.ds(r, rows_e // 4)] = stream_grad(r, rows_e // 4)

        chunks(rows_e, rows_e // 4, grad_inter)
        for j in range(R):
            dz[pl.ds(j, kp, stride=R), :] += xj[pl.ds(j * kp, kp)]

        norm_backward(b, 0)
        run_backward(b, 0, u_a, hc_a, sv_a, R, K, 5, 4)

        def grad_intra(r):
            dz[pl.ds(r, rows // 4)] += stream_grad(r, rows // 4)

        chunks(rows, rows // 4, grad_intra)

    def finish(r):
        dz[pl.ds(r, cr)] = dz[pl.ds(r, cr)] * valid[pl.ds(r, cr)]

    chunks(rows, cr, finish)
    for j in range(R):
        spans_out[j] = dz[pl.ds(j, K, stride=R), :].T[0:C]
    while not all(reduce.over() for reduce in active):
        point()
    wave_swap.wait()
    for i in range(wr):
        at = pl.multiple_of(speaker * (wr * LANES) + i * LANES, LANES)
        wave_out[0:1, pl.ds(at, LANES)] = own[i : i + 1]
        at = pl.multiple_of((1 - speaker) * (wr * LANES) + i * LANES, LANES)
        wave_out[0:1, pl.ds(at, LANES)] = wave_got[i : i + 1]


def unpack_kernel(
    sizes,
    sums,
    wave_in,
    spans_in,
    wave_out,
    spans_out,
    in_out,
    rec_out,
    bias_out,
    proj_out,
    proj_bias_out,
    gain_out,
    shift_out,
    mask_out,
    mask_bias_out,
    dec_out,
):
    C, H = sizes
    lay = sum_rows(C, H)
    n = pl.program_id(0)
    b, sec = n // 2, n % 2
    speaker = lax.axis_index("spk")
    spans_out[...] = spans_in[...]
    for d in range(2):
        in_out[d] = sums[lay["in"] + d * C : lay["in"] + (d + 1) * C].astype(F32)
        rec_out[d] = sums[lay["rec"] + d * H : lay["rec"] + (d + 1) * H].astype(F32)
    at = lay["proj"]
    proj_out[0 : C // 2] = sums[at : at + C // 2, 0 : 2 * H].astype(F32)
    proj_out[C // 2 : C] = sums[at : at + C // 2, 2 * H : 4 * H].astype(F32)
    small = sums[lay["small"] : lay["small"] + 16].astype(F32)
    bias_out[...] = small[0:2]
    for m, out in enumerate((proj_bias_out, gain_out, shift_out)):
        out[b, pl.ds(sec, 1)] = small[2:3, m * LANES : m * LANES + C]

    @pl.when(n == 0)
    def _():
        wave_out[...] = wave_in[...]

    @pl.when(n == pl.num_programs(0) - 1)
    def _():
        at = lay["head"]

        def own(x):
            return jnp.where(speaker == 0, x, pltpu.roll(x, C, 1))[:, 0:C]

        for q in range(4):
            x = sums[at : at + 16, q * LANES : (q + 1) * LANES].astype(F32)
            mask_out[0, 16 * q : 16 * q + 16] = own(x)
        x = sums[at + 16 : at + 32, 0 : 2 * LANES].astype(F32)
        mask_bias_out[...] = own(x[:, LANES : 2 * LANES])[0:1]
        dec_out[...] = x[:, 0:C]


def sum_rows(C, H):
    lay, at = {}, 0
    for name, rows in (("in", 2 * C), ("rec", 2 * H), ("proj", C // 2), ("small", 16), ("head", 32)):
        lay[name] = at
        at += rows
    lay["total"] = -(-at // (32 * PART)) * 32 * PART
    return lay


def shards(
    num_dp,
    spans,
    encoded,
    clip_lengths,
    clip_pads,
    lstm_in,
    lstm_rec,
    lstm_bias,
    proj_weight,
    proj_bias,
    gln_gain,
    gln_shift,
    mask_weight,
    mask_bias,
    dec_weight,
    wave_grad,
):
    R, K, C = spans.shape
    H = lstm_rec.shape[3]
    blocks = lstm_in.shape[0]
    clips = clip_lengths.shape[2]
    frames = encoded.shape[0]
    half = dec_weight.shape[1] // 2
    kp = -(-K // 16) * 16
    rows, rows_e = R * K, R * kp
    wr = frames * half // LANES
    mask_row = -(-wr // 8) * 8

    sizes = (R, K, C, H, clips, blocks, kp, num_dp)
    lay = sum_rows(C, H)
    num_hops = num_dp.bit_length()
    smem = pl.BlockSpec(memory_space=pltpu.SMEM)
    vmem = pl.BlockSpec(memory_space=pltpu.VMEM)
    shape = jax.ShapeDtypeStruct
    outs = pl.pallas_call(
        functools.partial(local_kernel, sizes),
        out_shape=(
            shape((1, 2 * frames * half), F32),
            shape((R, C, K), F32),
            shape((2 * blocks, lay["total"], 4 * H), BF16),
        ),
        in_specs=[smem, smem] + [vmem] * 13,
        out_specs=tuple([vmem] * 3),
        scratch_shapes=[
            pltpu.VMEM((rows_e, LANES), F32),
            pltpu.VMEM((rows, LANES), F32),
            pltpu.VMEM((rows_e, LANES), F32),
            pltpu.VMEM((rows_e, LANES), F32),
            pltpu.VMEM((rows_e, LANES), F32),
            pltpu.VMEM((rows_e, LANES), BF16),
            pltpu.VMEM((2 * blocks, rows, LANES), F32),
            pltpu.VMEM((2 * blocks, R, LANES), F32),
            pltpu.VMEM((blocks, rows, LANES), BF16),
            pltpu.VMEM((blocks, rows_e, LANES), BF16),
            pltpu.VMEM((blocks, rows, 2 * H), BF16),
            pltpu.VMEM((blocks, rows_e, 2 * H), BF16),
            pltpu.VMEM((blocks, 2, rows, 6 * H), BF16),
            pltpu.VMEM((blocks, 2, rows_e, 6 * H), BF16),
            pltpu.VMEM((2, rows_e, 4 * H), F32),
            pltpu.VMEM((rows_e, 2 * H), F32),
            pltpu.VMEM((2, rows_e, 4 * H), BF16),
            pltpu.VMEM((LANES, 8 * H), BF16),
            pltpu.VMEM((2, H, 4 * H), BF16),
            pltpu.VMEM((LANES, 8 * H), BF16),
            pltpu.VMEM((2, 4 * H, H), BF16),
            pltpu.VMEM((blocks, 2, LANES, 2 * H), BF16),
            pltpu.VMEM((2 * blocks, 8, LANES), F32),
            pltpu.VMEM((frames, LANES), F32),
            pltpu.VMEM((rows, LANES), F32),
            pltpu.VMEM((frames, LANES), BF16),
            pltpu.VMEM((rows, LANES), BF16),
            pltpu.VMEM((rows, LANES), BF16),
            pltpu.VMEM((C, 2 * C), BF16),
            pltpu.VMEM((2 * C, 2 * LANES), BF16),
            pltpu.VMEM((mask_row + C + 8, LANES), F32),
            pltpu.VMEM((mask_row, LANES), F32),
            pltpu.VMEM((mask_row + C + 8, LANES), F32),
            pltpu.VMEM((mask_row, LANES), F32),
            pltpu.SemaphoreType.DMA((4,)),
            pltpu.VMEM((2 * blocks, lay["total"], 4 * H), BF16),
            pltpu.VMEM((2 * blocks, lay["total"] + PART * max(num_hops - 5, 0), 4 * H), BF16),
            pltpu.VMEM((16, 4 * H), F32),
            pltpu.SemaphoreType.DMA((2 * blocks, 2 * num_hops, 2)),
        ],
        compiler_params=pltpu.CompilerParams(
            vmem_limit_bytes=62 * 1024 * 1024, collective_id=0, has_side_effects=True
        ),
        name="dual_path",
    )(
        clip_lengths,
        clip_pads,
        spans.transpose(0, 2, 1),
        encoded.T,
        lstm_in,
        lstm_rec,
        lstm_bias,
        proj_weight.transpose(0, 1, 3, 2),
        proj_bias,
        gln_gain,
        gln_shift,
        mask_weight,
        mask_bias,
        dec_weight.T,
        wave_grad,
    )
    half = dec_weight.shape[1] // 2
    per_section = pl.BlockSpec((None, lay["total"], 4 * H), lambda n: (n, 0, 0))

    def whole(*dims):
        return pl.BlockSpec(dims, lambda n: (0,) * len(dims))

    def section(*dims):
        return pl.BlockSpec((None, None) + dims, lambda n: (n // 2, n % 2) + (0,) * len(dims))

    finals = pl.pallas_call(
        functools.partial(unpack_kernel, (C, H)),
        grid=(2 * blocks,),
        out_shape=(
            shape((1, 2 * frames * half), F32),
            shape((R, C, K), F32),
            shape((blocks, 2, 2, C, 4 * H), F32),
            shape((blocks, 2, 2, H, 4 * H), F32),
            shape((blocks, 2, 2, 4 * H), F32),
            shape((blocks, 2, C, 2 * H), F32),
            shape((blocks, 2, C), F32),
            shape((blocks, 2, C), F32),
            shape((blocks, 2, C), F32),
            shape((1, C, C), F32),
            shape((1, C), F32),
            shape((2 * half, C), F32),
        ),
        in_specs=[
            per_section,
            whole(1, 2 * frames * half),
            pl.BlockSpec((R // (2 * blocks), C, K), lambda n: (n, 0, 0)),
        ],
        out_specs=(
            whole(1, 2 * frames * half),
            pl.BlockSpec((R // (2 * blocks), C, K), lambda n: (n, 0, 0)),
            section(2, C, 4 * H),
            section(2, H, 4 * H),
            section(2, 4 * H),
            section(C, 2 * H),
            whole(blocks, 2, C),
            whole(blocks, 2, C),
            whole(blocks, 2, C),
            whole(1, C, C),
            whole(1, C),
            whole(2 * half, C),
        ),
        compiler_params=pltpu.CompilerParams(vmem_limit_bytes=32 * 1024 * 1024),
        name="unpack",
    )(outs[2], outs[0], outs[1])
    return (
        finals[0],
        finals[1].transpose(0, 2, 1),
        finals[2],
        finals[3],
        finals[4],
        finals[5].transpose(0, 1, 3, 2),
        finals[6],
        finals[7],
        finals[8],
        finals[9],
        finals[10],
        finals[11].T,
    )


def solution(mesh):
    return jax.shard_map(
        functools.partial(shards, mesh.shape["dp"]),
        mesh=mesh,
        in_specs=(
            P(("dp", "spk"), None, None),
            P(("dp", "spk"), None),
            P("dp", None, None),
            P("dp", None, None),
            P(),
            P(),
            P(),
            P(),
            P(),
            P(),
            P(),
            P("spk", None, None),
            P("spk", None),
            P(),
            P("spk", "dp"),
        ),
        out_specs=(
            P("spk", "dp"),
            P(("dp", "spk"), None, None),
            P(),
            P(),
            P(),
            P(),
            P(),
            P(),
            P(),
            P("spk", None, None),
            P("spk", None),
            P(),
        ),
        check_vma=False,
    )
```

```python
import functools

import jax
import jax.numpy as jnp
from jax import lax
from jax.experimental import pallas as pl
from jax.experimental.pallas import tpu as pltpu
from jax.sharding import PartitionSpec as P

F32 = jnp.float32
BF16 = jnp.bfloat16
LANES = 128
PART = 16
PAIR = 2 * PART
MESH = pl.DeviceIdType.MESH


def dot(a, b):
    return jnp.dot(a, b, preferred_element_type=F32)


def dot_tn(a, b):
    return lax.dot_general(a, b, (((0,), (0,)), ((), ())), preferred_element_type=F32)


def dot_nt(a, b):
    return lax.dot_general(a, b, (((1,), (1,)), ((), ())), preferred_element_type=F32)


def chunks(total, size, body):
    assert total % size == 0

    def step(i, carry):
        body(pl.multiple_of(i * size, size))
        return carry

    lax.fori_loop(0, total // size, step, 0)


class Place:
    def __init__(self, num_dp):
        self.dp, self.spk = lax.axis_index("dp"), lax.axis_index("spk")
        self.bits = num_dp.bit_length()

    def bit(self, k):
        if k == 1:
            return self.spk
        return self.dp // (1 << max(k - 1, 0)) % 2

    def device(self, mask):
        dp, spk = self.dp, self.spk
        for k in range(self.bits):
            if mask >> k & 1:
                if k == 1:
                    spk = 1 - spk
                else:
                    dp = dp + (1 - 2 * self.bit(k)) * (1 << max(k - 1, 0))
        return {"dp": dp, "spk": spk}

    def index(self, bits, mask=0):
        number = 0
        for i, k in enumerate(bits):
            one = 1 - self.bit(k) if mask >> k & 1 else self.bit(k)
            number = number + one * (1 << i)
        return number

    def masks(self, bits):
        found = []
        for m in range((1 << len(bits)) - 1, 0, -1):
            found.append(sum((m >> i & 1) << k for i, k in enumerate(bits)))
        return found


class Reduction:
    def __init__(self, buf, recv, out, sems, place, stages, outer, times):
        self.buf, self.recv, self.out, self.sems, self.place = buf, recv, out, sems, place
        self.steps, back = [], []
        off, size, at, sem = 0, buf.shape[0], 0, 0
        for i, bits in enumerate(stages):
            masks = place.masks(bits)
            part = size // (len(masks) + 1)
            own = off + place.index(bits) * part
            last = i == len(stages) - 1
            self.steps.append(
                (
                    functools.partial(self.scatter, sem, masks, bits, off, part, at),
                    functools.partial(self.add, len(masks), own, part, at, out if last else buf),
                    times[len(bits)],
                )
            )
            back.append((masks, own, part, times[len(bits)]))
            off, size = own, part
            at += len(masks) * part
            sem += 1
        for k in outer:
            self.steps.append(
                (
                    functools.partial(self.double, sem, k, off, size, at),
                    functools.partial(self.add_double, off, size, at),
                    times[1],
                )
            )
            at += size
            sem += 1
        for masks, own, part, time in reversed(back):
            self.steps.append((functools.partial(self.gather, sem, masks, own, part), None, time))
            sem += 1
        self.first = self.steps[0][1]
        self.pending, self.after, self.due = None, None, 0.0

    def copy(self, sem, src, dst, device):
        return pltpu.make_async_remote_copy(
            src_ref=src,
            dst_ref=dst,
            send_sem=self.sems.at[sem, 0],
            recv_sem=self.sems.at[sem, 1],
            device_id=device,
            device_id_type=MESH,
        )

    def rows(self, ref, off, size):
        return ref.at[pl.ds(pl.multiple_of(off, PART), size)]

    def all_of(self, sem, masks, part):
        rows = self.recv.at[0 : len(masks) * part]
        return self.copy(sem, rows, rows, self.place.device(masks[0]))

    def scatter(self, sem, masks, bits, off, part, at):
        for i, mask in enumerate(masks):
            src = self.rows(self.buf, off + self.place.index(bits, mask) * part, part)
            dst = self.recv.at[at + i * part : at + (i + 1) * part]
            self.copy(sem, src, dst, self.place.device(mask)).start()
        return self.all_of(sem, masks, part)

    def add(self, number, own, part, at, target):
        def body(i, carry):
            rows = pl.ds(pl.multiple_of(own + i * PART, PART), PART)
            total = self.buf[rows].astype(F32)
            for q in range(number):
                total = total + self.recv[pl.ds(pl.multiple_of(at + q * part + i * PART, PART), PART)].astype(F32)
            target[rows] = total.astype(BF16)
            return carry

        lax.fori_loop(0, part // PART, body, 0)

    def double(self, sem, k, off, size, at):
        copy = self.copy(sem, self.rows(self.out, off, size), self.recv.at[at : at + size], self.place.device(1 << k))
        copy.start()
        return copy

    def add_double(self, off, size, at):
        rows = pl.ds(pl.multiple_of(off, PART), size)
        self.out[rows] = (self.out[rows].astype(F32) + self.recv[at : at + size].astype(F32)).astype(BF16)

    def gather(self, sem, masks, own, part):
        rows = self.rows(self.out, own, part)
        for mask in masks:
            self.copy(sem, rows, rows, self.place.device(mask)).start()
        return self.all_of(sem, masks, part)

    def advance(self, now):
        if self.pending is not None:
            self.pending.wait()
            if self.after is not None:
                self.after()
            self.pending = None
        if self.steps:
            start, self.after, time = self.steps.pop(0)
            self.pending = start()
            self.due = now + time

    def over(self):
        return self.pending is None and not self.steps


def local_kernel(
    sizes,
    lengths_ref,
    pads_ref,
    spans_ref,
    enc_ref,
    w_in_ref,
    w_rec_ref,
    w_bias_ref,
    w_proj_ref,
    proj_bias_ref,
    gain_ref,
    shift_ref,
    mask_in_ref,
    mask_bias_in_ref,
    dec_in_ref,
    wave_grad_ref,
    wave_out,
    spans_out,
    all_sums,
    stream,
    valid,
    mx,
    xj,
    dz,
    dmj,
    normed,
    inv_all,
    u_a,
    u_e,
    hc_a,
    hc_e,
    sv_a,
    sv_e,
    gd,
    dh,
    dp,
    wcat,
    wiu,
    wrt,
    pws,
    vec,
    enc_t,
    pre,
    masked,
    feats,
    dpre,
    mask_ref,
    dec_ref,
    send,
    own,
    got,
    wave_got,
    sems,
    sums,
    recv,
    small,
    sum_sems,
):
    R, K, C, H, clips, blocks, kp, num_dp = sizes
    rows, rows_e = R * K, R * kp
    hop = K // 2
    frames = R * hop
    half = dec_in_ref.shape[0] // 2
    wr = frames * half // LANES
    group = LANES // half
    cr = rows
    speaker = lax.axis_index("spk")
    partner = {"spk": 1 - speaker}

    barrier = pltpu.get_barrier_semaphore()
    place = Place(num_dp)
    everyone = place.masks(range(1, min(place.bits, 5))) + [1 << k for k in [0, *range(5, place.bits)]]
    for mask in everyone:
        pl.semaphore_signal(barrier, inc=1, device_id=place.device(mask), device_id_type=MESH)

    mask_row = -(-wr // 8) * 8
    for i in range(wr):
        at = pl.multiple_of(speaker * (wr * LANES) + i * LANES, LANES)
        own[i : i + 1] = wave_grad_ref[0:1, pl.ds(at, LANES)].astype(F32)
        at = pl.multiple_of((1 - speaker) * (wr * LANES) + i * LANES, LANES)
        send[i : i + 1] = wave_grad_ref[0:1, pl.ds(at, LANES)].astype(F32)
    mask_f = mask_in_ref[0].astype(F32)
    send[wr:mask_row] = jnp.zeros((mask_row - wr, LANES), F32)
    send[mask_row : mask_row + C] = jnp.concatenate([mask_f, mask_f], axis=1)
    bias_f = mask_bias_in_ref[0:1].astype(F32)
    bias_f = jnp.concatenate([bias_f, bias_f], axis=1)
    send[mask_row + C : mask_row + C + 8] = jnp.broadcast_to(bias_f, (8, LANES))
    pl.semaphore_wait(barrier, len(everyone))
    swap = pltpu.make_async_remote_copy(
        src_ref=send, dst_ref=got, send_sem=sems.at[0], recv_sem=sems.at[1], device_id=partner, device_id_type=MESH
    )
    swap.start()

    jio = lax.broadcasted_iota(jnp.int32, (R, LANES), 0)
    lane = lax.broadcasted_iota(jnp.int32, (1, LANES), 1)
    ones_lanes = jnp.logical_and(lane >= C, lane < C + 3)

    lens = [lengths_ref[0, speaker, c] for c in range(clips)]
    pads = [pads_ref[0, speaker, c] for c in range(clips)]
    starts, ends, at = [], [], 0
    for c in range(clips):
        starts.append(at)
        at = at + lens[c]
        ends.append(at)

    def is_start(j):
        hit = j == starts[0]
        for c in range(1, clips):
            hit = jnp.logical_or(hit, j == starts[c])
        return hit

    def is_end(j):
        hit = j == ends[0] - 1
        for c in range(1, clips):
            hit = jnp.logical_or(hit, j == ends[c] - 1)
        return hit

    members, thr, inv_count = [], jnp.full((R, LANES), K, jnp.int32), jnp.zeros((R, LANES), F32)
    for c in range(clips):
        member = jnp.logical_and(jio >= starts[c], jio < ends[c]).astype(F32)
        members.append(member)
        thr = jnp.where(jio == ends[c] - 1, K - pads[c], thr)
        count = (C * (K * lens[c] - pads[c])).astype(F32)
        inv_count = inv_count + member / jnp.full((R, LANES), count, F32)
    not_first = 1.0 - is_start(jio).astype(F32)
    next_not_first = 1.0 - jnp.logical_or(is_start(jio + 1), jio == R - 1).astype(F32)

    def clip_sum(x):
        out = jnp.zeros((R, 1), F32)
        for member in members:
            out = out + member[:, :1] * jnp.sum(member * x, axis=(0, 1), keepdims=True)
        return out

    def fill_valid(r):
        k = lax.broadcasted_iota(jnp.int32, (cr // R, R, LANES), 0) + r // R
        low = lax.broadcasted_iota(jnp.int32, (cr // R, R, LANES), 2) < C
        ok = jnp.logical_and(k < thr[None], low).astype(F32)
        valid[pl.ds(r, cr)] = ok.reshape(cr, LANES)

    chunks(rows, cr, fill_valid)

    near, far = list(range(1, min(place.bits, 3))), list(range(3, min(place.bits, 5)))
    outer = range(5, place.bits)
    times = {1: 2.0, 2: 4.5, 4: 7.0}

    def reduction(n, stages):
        return Reduction(sums.at[n], recv.at[n], all_sums.at[n], sum_sems.at[n], place, stages, outer, times)

    lay = sum_rows(C, H)
    active = []
    clock = [0.0]

    def point(passed):
        clock[0] += passed
        for reduce in active:
            if not reduce.over() and reduce.due <= clock[0]:
                reduce.advance(clock[0])

    for n in range(2 * blocks):
        for at in (lay["proj"], lay["head"]):
            sums[n, at : at + PAIR] = jnp.zeros((PAIR, 4 * H), BF16)

    pws[...] = jnp.zeros_like(pws)
    wiu[...] = jnp.zeros_like(wiu)
    vec[...] = jnp.zeros_like(vec)
    for b in range(blocks):
        for s in range(2):
            n = 2 * b + s
            pws[b, s, 0:C] = w_proj_ref[b, s]
            vec[n, 0:1, 0:C] = proj_bias_ref[b, s : s + 1]
            vec[n, 1:2, 0:C] = gain_ref[b, s : s + 1]
            vec[n, 2:3, 0:C] = shift_ref[b, s : s + 1]

    stream[...] = jnp.zeros_like(stream)
    for j in range(R):
        x = spans_ref[j].astype(F32)
        x = jnp.concatenate([x, jnp.zeros_like(x)], axis=0).T
        stream[pl.ds(j, K, stride=R), :] = x

    def start_stream(r):
        x = stream[pl.ds(r, cr)] * valid[pl.ds(r, cr)]
        stream[pl.ds(r, cr)] = jnp.where(ones_lanes, 1.0, x)

    chunks(rows, cr, start_stream)

    gate_scale = jnp.where(
        lax.broadcasted_iota(jnp.int32, (1, 4 * H), 1) // H == 2, 1.0, 0.5
    ).astype(F32)

    def lane_part(x, g):
        return x[:, g * H : (g + 1) * H]

    def gate_step(d, sv, b, r, n, p, c, keep_next):
        acts = [jnp.tanh(p[:, g * H : (g + 1) * H]) for g in range(4)]
        ti, tf, g, to = acts
        i, f, o = 0.5 * ti + 0.5, 0.5 * tf + 0.5, 0.5 * to + 0.5
        cn = f * c + i * g
        tc = jnp.tanh(cn)
        h = o * tc
        parts = [
            g * (0.25 - 0.25 * ti * ti),
            c * (0.25 - 0.25 * tf * tf),
            i * (1.0 - g * g),
            tc * (0.25 - 0.25 * to * to),
            o * (1.0 - tc * tc),
            f,
        ]
        for m, part in enumerate(parts):
            sv[b, d, pl.ds(r, n), m * H : (m + 1) * H] = part.astype(BF16)
        if keep_next is None:
            return h.astype(BF16), h.astype(BF16), cn
        return h.astype(BF16), (h * keep_next).astype(BF16), cn * keep_next

    def run_forward(b, sec, u, hc, sv, n, steps, unroll):
        total = n * steps
        for d in range(2):
            wcat[d, 0:H] = (w_rec_ref[b, sec, d].astype(F32) * gate_scale).astype(BF16)
            wcat[d, H : H + C] = (w_in_ref[b, sec, d].astype(F32) * gate_scale).astype(BF16)
            bias = w_bias_ref[b, sec, d : d + 1] * gate_scale
            terms = []
            for _ in range(3):
                terms.append(bias.astype(BF16).astype(F32))
                bias = bias - terms[-1]
            row = lax.broadcasted_iota(jnp.int32, (H - C, 4 * H), 0)
            block = jnp.zeros((H - C, 4 * H), F32)
            for m, term in enumerate(terms):
                block = jnp.where(row == m, jnp.broadcast_to(term, block.shape), block)
            wcat[d, H + C : 2 * H] = block.astype(BF16)

        def step(t, carry):
            hf, hb, cf, cb = carry
            back = steps - 1 - t
            rf = pl.multiple_of(t * n, n)
            rb = pl.multiple_of(back * n, n)
            kf = kb = None
            if sec == 1:
                kf = 1.0 - is_start(t + 1).astype(F32)
                kb = 1.0 - is_end(back - 1).astype(F32)
            pf = dot(jnp.concatenate([hf, u[b, pl.ds(rf, n)]], axis=1), wcat[0])
            pb = dot(jnp.concatenate([hb, u[b, pl.ds(rb, n)]], axis=1), wcat[1])
            out_f, hf, cf = gate_step(0, sv, b, rf, n, pf, cf, kf)
            out_b, hb, cb = gate_step(1, sv, b, rb, n, pb, cb, kb)
            hc[b, pl.ds(rf, n), 0:H] = out_f
            hc[b, pl.ds(rb, n), H : 2 * H] = out_b
            return hf, hb, cf, cb

        zh, zc = jnp.zeros((n, H), BF16), jnp.zeros((n, H), F32)
        lax.fori_loop(0, steps, step, (zh, zh, zc, zc), unroll=unroll)

    def norm_forward(b, sec):
        n = 2 * b + sec
        gain, shift = vec[n, 1:2], vec[n, 2:3]

        def fold(body):
            def step(i, acc):
                return acc + jnp.sum(body(pl.multiple_of(i * cr, cr)).reshape(cr // R, R, LANES), axis=0)

            return lax.fori_loop(0, rows // cr, step, jnp.zeros((R, LANES), F32))

        mean = clip_sum(fold(lambda r: valid[pl.ds(r, cr)] * mx[pl.ds(r, cr)])) * inv_count

        def spread(r):
            x = mx[pl.ds(r, cr)].reshape(cr // R, R, LANES) - mean[None]
            return valid[pl.ds(r, cr)] * (x * x).reshape(cr, LANES)

        inv = lax.rsqrt(clip_sum(fold(spread)) * inv_count + 1e-08)
        inv_all[n] = inv

        def apply(r):
            x = (mx[pl.ds(r, cr)].reshape(cr // R, R, LANES) - mean[None]) * inv[None]
            x = x.reshape(cr, LANES)
            normed[n, pl.ds(r, cr)] = x
            stream[pl.ds(r, cr)] += valid[pl.ds(r, cr)] * (x * gain + shift)

        chunks(rows, cr, apply)

    def forward_block(b, carry):
        def u_intra(r):
            u_a[b, pl.ds(r, cr)] = stream[pl.ds(r, cr)].astype(BF16)

        chunks(rows, cr, u_intra)
        run_forward(b, 0, u_a, hc_a, sv_a, R, K, 10)

        mx[0:rows] = dot_nt(hc_a[b], pws[b, 0]) + vec[2 * b, 0:1]
        norm_forward(b, 0)

        for j in range(R):
            u_e[b, pl.ds(j * kp, kp)] = stream[pl.ds(j, kp, stride=R), :].astype(BF16)
        run_forward(b, 1, u_e, hc_e, sv_e, kp, R, R)

        xj[...] = dot_nt(hc_e[b], pws[b, 1]) + vec[2 * b + 1, 0:1]
        for j in range(R):
            mx[pl.ds(j, kp, stride=R), :] = xj[pl.ds(j * kp, kp)]
        norm_forward(b, 1)
        return carry

    lax.fori_loop(0, blocks, forward_block, 0)

    e = enc_ref[...].astype(F32)
    xj[0:frames] = jnp.concatenate([e, e], axis=0).T
    for j in range(R):
        enc_t[pl.ds(j, hop, stride=R), :] = xj[j * hop : (j + 1) * hop]

    first_half = lane < half
    second_half = jnp.logical_and(lane >= half, lane < 2 * half)
    d = dec_in_ref[...].astype(F32)
    d = jnp.concatenate([d, jnp.zeros((LANES - 2 * half, C), F32)], axis=0).T
    dec_ref[0:C, 0:LANES] = jnp.where(first_half, d, 0.0).astype(BF16)
    dec_ref[C : 2 * C, 0:LANES] = jnp.where(second_half, pltpu.roll(d, half, 1), 0.0).astype(BF16)
    dec_ref[0:C, LANES : 2 * LANES] = jnp.where(first_half, pltpu.roll(d, LANES - half, 1), 0.0).astype(BF16)
    dec_ref[C : 2 * C, LANES : 2 * LANES] = jnp.where(second_half, d, 0.0).astype(BF16)

    swap.wait()
    mask_ref[...] = jnp.concatenate([mask_f, got[mask_row : mask_row + C, 0:C]], axis=1).astype(BF16)
    mask_bias = jnp.concatenate(
        [mask_bias_in_ref[0:1].astype(F32), got[mask_row + C : mask_row + C + 1, 0:C]], axis=1
    )
    for q in range(group):
        a = pltpu.roll(own[0:mask_row], LANES - q * half, 1) if q else own[0:mask_row]
        b = pltpu.roll(got[0:mask_row], (LANES - (q - 1) * half) % LANES, 1) if q != 1 else got[0:mask_row]
        w = jnp.where(first_half, a, jnp.where(second_half, b, 0.0))
        xj[pl.ds(q, wr, stride=group), :] = w[0:wr]
    for j in range(R):
        gd[1, j * hop : (j + 1) * hop, 0:LANES] = xj[j * hop : (j + 1) * hop]
    for j in range(R):
        xj[pl.ds(j, hop, stride=R), :] = gd[1, j * hop : (j + 1) * hop, 0:LANES]

    def head_pre(r):
        x = stream[pl.ds(r, cr)]
        f = x * (0.5 * jnp.tanh(0.5 * x) + 0.5)
        f = jnp.where(lane == C, 1.0, f).astype(BF16)
        feats[pl.ds(r, cr)] = f
        pre[pl.ds(r, cr)] = dot(f[:, 0:C], mask_ref[...]) + mask_bias

    chunks(rows, cr, head_pre)

    hr = frames // 5

    def tile(v):
        return jnp.broadcast_to(v[None], (hr // R, R, LANES)).reshape(hr, LANES)

    for q in range(5):
        r = q * hr
        fr = pre[r : r + hr] + tile(not_first) * pre[frames + r - 1 : frames + r - 1 + hr]
        e = enc_t[r : r + hr]
        sp = jnp.maximum(fr, 0.0) + jnp.log1p(jnp.exp(-jnp.abs(fr)))
        masked[r : r + hr] = (sp * e).astype(BF16)
        pre[r : r + hr] = e * (0.5 * jnp.tanh(0.5 * fr) + 0.5)
    for q in range(5):
        r = q * hr
        gd[0, r : r + hr, 0 : 2 * LANES] = dot(masked[r : r + hr], dec_ref[...])
    gd[1, 0:R, 0:LANES] = (
        gd[0, 0:R, 0:LANES] + not_first * gd[0, frames - R - 1 : frames - 1, LANES : 2 * LANES]
    )
    gd[1, R:frames, 0:LANES] = gd[0, R:frames, 0:LANES] + gd[0, 0 : frames - R, LANES : 2 * LANES]
    xj[frames : 2 * frames] = gd[1, 0:frames, 0:LANES]
    for j in range(R):
        gd[1, j * hop : (j + 1) * hop, 0:LANES] = xj[pl.ds(frames + j, hop, stride=R), :]
    xj[frames : 2 * frames] = gd[1, 0:frames, 0:LANES]
    zero = jnp.zeros((wr, LANES), F32)
    w_own, w_far = zero, zero
    for q in range(group):
        x = xj[pl.ds(frames + q, wr, stride=group), :]
        a = jnp.where(first_half, x, 0.0)
        b = jnp.where(second_half, x, 0.0)
        w_own = w_own + (pltpu.roll(a, q * half, 1) if q else a)
        w_far = w_far + (pltpu.roll(b, (q - 1) * half % LANES, 1) if q != 1 else b)
    own[0:wr] = w_own
    send[0:wr] = w_far
    wave_swap = pltpu.make_async_remote_copy(
        src_ref=send.at[0:mask_row],
        dst_ref=wave_got,
        send_sem=sems.at[2],
        recv_sem=sems.at[3],
        device_id=partner,
        device_id_type=MESH,
    )
    wave_swap.start()

    gd[0, 0:frames, 0:LANES] = xj[0:frames]
    gd[0, 0 : frames - R, LANES : 2 * LANES] = xj[R:frames]
    gd[0, frames - R : frames, LANES : 2 * LANES] = next_not_first * xj[1 : R + 1]
    dp[0, 0:frames, 0 : 2 * LANES] = gd[0, 0:frames, 0 : 2 * LANES].astype(BF16)
    g = dot_tn(masked[...], dp[0, 0:frames, 0 : 2 * LANES])
    g_lead = g[0:C, 0:LANES] + pltpu.roll(g[C : 2 * C, 0:LANES], LANES - half, 1)
    g_tail = pltpu.roll(g[0:C, LANES : 2 * LANES], half, 1) + g[C : 2 * C, LANES : 2 * LANES]
    g = jnp.where(first_half, g_lead, g_tail)
    g_dec = jnp.concatenate([g, jnp.zeros_like(g)], axis=0).T[0 : 2 * half]
    xj[frames : frames + 8] = jnp.zeros((8, LANES), F32)
    for q in range(5):
        r = q * hr
        dfr = dot_nt(dp[0, r : r + hr, 0 : 2 * LANES], dec_ref[...]) * pre[r : r + hr]
        xj[r : r + hr] = dfr
        dpre[r : r + hr] = dfr.astype(BF16)
    for q in range(5):
        r = q * hr
        dpre[frames + r : frames + r + hr] = (tile(next_not_first) * xj[r + 1 : r + 1 + hr]).astype(BF16)
    gm = dot_tn(feats[...], dpre[...])
    gm = jnp.where(speaker == 0, gm, pltpu.roll(gm, C, 1))
    n, at = 2 * blocks - 1, lay["head"]
    for q in range(4):
        sums[n, at : at + 16, q * LANES : (q + 1) * LANES] = gm[16 * q : 16 * q + 16].astype(BF16)
    sums[n, at + 16 : at + 32, 0:LANES] = jnp.where(lane < C, g_dec, 0.0).astype(BF16)
    sums[n, at + 16 : at + 32, LANES : 2 * LANES] = jnp.broadcast_to(gm[C : C + 1], (16, LANES)).astype(BF16)
    dz[...] = jnp.zeros_like(dz)

    def head_dz(r):
        x = stream[pl.ds(r, cr)]
        sg = 0.5 * jnp.tanh(0.5 * x) + 0.5
        df = dot_nt(dpre[pl.ds(r, cr)], mask_ref[...])
        df = jnp.concatenate([df, jnp.zeros_like(df)], axis=1)
        dz[pl.ds(r, cr)] = df * sg * (1.0 + x * (1.0 - sg))

    chunks(rows, cr, head_dz)

    def norm_backward(b, sec):
        n = 2 * b + sec
        gain = vec[n, 1:2]

        def sums(i, acc):
            r = pl.multiple_of(i * cr, cr)
            v = valid[pl.ds(r, cr)] * dz[pl.ds(r, cr)]
            w = v * normed[n, pl.ds(r, cr)]
            return (
                acc[0] + jnp.sum(v.reshape(cr // R, R, LANES), axis=0),
                acc[1] + jnp.sum(w.reshape(cr // R, R, LANES), axis=0),
            )

        zero = jnp.zeros((R, LANES), F32)
        s1, s2 = lax.fori_loop(0, rows // cr, sums, (zero, zero))
        small[1:2, LANES : 2 * LANES] = jnp.sum(s2, axis=0, keepdims=True)
        small[1:2, 2 * LANES : 3 * LANES] = jnp.sum(s1, axis=0, keepdims=True)
        m1 = clip_sum(s1 * gain) * inv_count
        m2 = clip_sum(s2 * gain) * inv_count
        inv = inv_all[n]

        def apply(i, acc):
            r = pl.multiple_of(i * cr, cr)
            d = (dz[pl.ds(r, cr)] * gain).reshape(cr // R, R, LANES)
            x = normed[n, pl.ds(r, cr)].reshape(cr // R, R, LANES)
            y = (d - m1[None] - x * m2[None]) * inv[None]
            y = (y.reshape(cr, LANES) * valid[pl.ds(r, cr)]).astype(BF16)
            if sec == 0:
                dmj[pl.ds(r, cr)] = y
            y = y.astype(F32)
            if sec == 1:
                mx[pl.ds(r, cr)] = y
            return acc + jnp.sum(y.reshape(cr // R, R, LANES), axis=0)

        acc = lax.fori_loop(0, rows // cr, apply, zero)
        small[1:2, 0:LANES] = jnp.sum(acc, axis=0, keepdims=True)

    def back_step(d, sv, b, r, n, dhn, dcn, keep):
        a = [sv[b, d, pl.ds(r, n), m * H : (m + 1) * H].astype(F32) for m in range(6)]
        g = dh[pl.ds(r, n), d * H : (d + 1) * H] + dhn
        dc = dcn + g * a[4]
        for m in range(4):
            dp[d, pl.ds(r, n), m * H : (m + 1) * H] = ((g if m == 3 else dc) * a[m]).astype(BF16)
        dhn = dot(dp[d, pl.ds(r, n)], wrt[d])
        dcn = dc * a[5]
        if keep is not None:
            dhn, dcn = dhn * keep, dcn * keep
        return dhn, dcn

    def run_backward(b, sec, u, hc, sv, n, steps, unroll, parts):
        total = n * steps
        out = sums.at[2 * b + sec]
        g = dot_tn(dmj[0:total], hc[b])[0:C].astype(BF16)
        at = lay["proj"]
        out[at : at + C // 2, 0 : 2 * H] = g[0 : C // 2]
        out[at : at + C // 2, 2 * H : 4 * H] = g[C // 2 : C]

        dh[0:total] = dot(dmj[0:total], pws[b, sec])
        for d in range(2):
            wrt[d] = w_rec_ref[b, sec, d].T
            wiu[0:C, d * 4 * H : (d + 1) * 4 * H] = w_in_ref[b, sec, d]

        def step(t, carry):
            hf, hb, cf, cb = carry
            back = steps - 1 - t
            rf = pl.multiple_of(back * n, n)
            rb = pl.multiple_of(t * n, n)
            kf = kb = None
            if sec == 1:
                kf = 1.0 - is_start(back).astype(F32)
                kb = 1.0 - is_end(t).astype(F32)
            hf, cf = back_step(0, sv, b, rf, n, hf, cf, kf)
            hb, cb = back_step(1, sv, b, rb, n, hb, cb, kb)
            return hf, hb, cf, cb

        z = jnp.zeros((n, H), F32)
        carry = (z, z, z, z)
        point(2.5)
        for p in range(parts):
            carry = lax.fori_loop(p * steps // parts, (p + 1) * steps // parts, step, carry, unroll=unroll)
            point(steps * 0.125 / parts)
        if sec == 1:
            for j in range(1, steps):
                kf = (1.0 - is_start(j).astype(F32)).astype(BF16)
                at = slice((j - 1) * n, j * n)
                hc[b, at, 0:H] = hc[b, at, 0:H] * kf
                kb = (1.0 - is_end(j - 1).astype(F32)).astype(BF16)
                at = slice(j * n, (j + 1) * n)
                hc[b, at, H : 2 * H] = hc[b, at, H : 2 * H] * kb
        last = (b, sec) == (0, 0)
        core = place.bit(0)
        reduce = reduction(2 * b + sec, [[0], near + far] if last else [[0], near, far])
        for d in (1 - core, core):
            g = dot_tn(u[b], dp[d, 0:total])
            base = d * lay["half"]
            out[pl.ds(pl.multiple_of(base + lay["in"], PART), C)] = g[0:C].astype(BF16)
            small[0:1] = g[C : C + 1]
            out[pl.ds(pl.multiple_of(base + lay["small"], PART), 16)] = small[...].astype(BF16)
            h_prev = hc[b, pl.ds(pl.multiple_of(d * n, n), total - n), pl.ds(pl.multiple_of(d * H, H), H)]
            g = dot_tn(h_prev, dp[d, pl.ds(pl.multiple_of((1 - d) * n, n), total - n)])
            out[pl.ds(pl.multiple_of(base + lay["rec"], PART), H)] = g.astype(BF16)
            if d is core:
                point(0.6)
            else:
                reduce.advance(clock[0] + 0.6)
                active.append(reduce)

    def stream_grad(total):
        return dot_nt(dp[0, 0:total], wiu[:, 0 : 4 * H]) + dot_nt(dp[1, 0:total], wiu[:, 4 * H : 8 * H])

    small[...] = jnp.zeros_like(small)
    for b in reversed(range(blocks)):
        norm_backward(b, 1)
        mx[rows:rows_e] = jnp.zeros((rows_e - rows, LANES), F32)
        for j in range(R):
            dmj[pl.ds(j * kp, kp)] = mx[pl.ds(j, kp, stride=R), :].astype(BF16)
        run_backward(b, 1, u_e, hc_e, sv_e, kp, R, R, 1)

        xj[...] = stream_grad(rows_e)
        for j in range(R):
            dz[pl.ds(j, kp, stride=R), :] += xj[pl.ds(j * kp, kp)]
        point(1.5)

        norm_backward(b, 0)
        run_backward(b, 0, u_a, hc_a, sv_a, R, K, 10, 5)

        dz[0:rows] += stream_grad(rows)
        point(1.5)

    def finish(r):
        dz[pl.ds(r, cr)] = dz[pl.ds(r, cr)] * valid[pl.ds(r, cr)]

    chunks(rows, cr, finish)
    for j in range(R):
        spans_out[j] = dz[pl.ds(j, K, stride=R), :].T[0:C]
    while not all(reduce.over() for reduce in active):
        nearest = min((reduce for reduce in active if not reduce.over()), key=lambda reduce: reduce.due)
        clock[0] = max(clock[0], nearest.due)
        nearest.advance(clock[0])
    wave_swap.wait()
    for i in range(wr):
        at = pl.multiple_of(speaker * (wr * LANES) + i * LANES, LANES)
        wave_out[0:1, pl.ds(at, LANES)] = own[i : i + 1]
        at = pl.multiple_of((1 - speaker) * (wr * LANES) + i * LANES, LANES)
        wave_out[0:1, pl.ds(at, LANES)] = wave_got[i : i + 1]


def unpack_kernel(
    sizes,
    sums,
    wave_in,
    spans_in,
    wave_out,
    spans_out,
    in_out,
    rec_out,
    bias_out,
    proj_out,
    proj_bias_out,
    gain_out,
    shift_out,
    mask_out,
    mask_bias_out,
    dec_out,
):
    C, H = sizes
    lay = sum_rows(C, H)
    n = pl.program_id(0)
    b, sec = n // 2, n % 2
    speaker = lax.axis_index("spk")
    spans_out[...] = spans_in[...]
    for d in range(2):
        base = d * lay["half"]
        in_out[d] = sums[base + lay["in"] : base + lay["in"] + C].astype(F32)
        rec_out[d] = sums[base + lay["rec"] : base + lay["rec"] + H].astype(F32)
        small = sums[base + lay["small"] : base + lay["small"] + 16].astype(F32)
        bias_out[d : d + 1] = small[0:1]
        if d == 0:
            for m, out in enumerate((proj_bias_out, gain_out, shift_out)):
                out[b, pl.ds(sec, 1)] = small[1:2, m * LANES : m * LANES + C]
    at = lay["proj"]
    proj_out[0 : C // 2] = sums[at : at + C // 2, 0 : 2 * H].astype(F32)
    proj_out[C // 2 : C] = sums[at : at + C // 2, 2 * H : 4 * H].astype(F32)

    @pl.when(n == 0)
    def _():
        wave_out[...] = wave_in[...]

    @pl.when(n == pl.num_programs(0) - 1)
    def _():
        at = lay["head"]

        def own(x):
            return jnp.where(speaker == 0, x, pltpu.roll(x, C, 1))[:, 0:C]

        for q in range(4):
            x = sums[at : at + 16, q * LANES : (q + 1) * LANES].astype(F32)
            mask_out[0, 16 * q : 16 * q + 16] = own(x)
        x = sums[at + 16 : at + 32, 0 : 2 * LANES].astype(F32)
        mask_bias_out[...] = own(x[:, LANES : 2 * LANES])[0:1]
        dec_out[...] = x[:, 0:C]


def sum_rows(C, H):
    lay, at = {}, 0
    for name, rows in (("in", C), ("rec", H), ("small", 16), ("proj", C // 2)):
        lay[name] = at
        at += rows
    lay["half"] = -(-at // (16 * PART)) * 16 * PART
    lay["head"] = lay["half"] + lay["proj"]
    lay["total"] = 2 * lay["half"]
    return lay


def shards(
    num_dp,
    spans,
    encoded,
    clip_lengths,
    clip_pads,
    lstm_in,
    lstm_rec,
    lstm_bias,
    proj_weight,
    proj_bias,
    gln_gain,
    gln_shift,
    mask_weight,
    mask_bias,
    dec_weight,
    wave_grad,
):
    R, K, C = spans.shape
    H = lstm_rec.shape[3]
    blocks = lstm_in.shape[0]
    clips = clip_lengths.shape[2]
    frames = encoded.shape[0]
    half = dec_weight.shape[1] // 2
    kp = -(-K // 16) * 16
    rows, rows_e = R * K, R * kp
    wr = frames * half // LANES
    mask_row = -(-wr // 8) * 8

    sizes = (R, K, C, H, clips, blocks, kp, num_dp)
    lay = sum_rows(C, H)
    outer = max(num_dp.bit_length() - 5, 0)
    smem = pl.BlockSpec(memory_space=pltpu.SMEM)
    vmem = pl.BlockSpec(memory_space=pltpu.VMEM)
    shape = jax.ShapeDtypeStruct
    outs = pl.pallas_call(
        functools.partial(local_kernel, sizes),
        out_shape=(
            shape((1, 2 * frames * half), F32),
            shape((R, C, K), F32),
            shape((2 * blocks, lay["total"], 4 * H), BF16),
        ),
        in_specs=[smem, smem] + [vmem] * 13,
        out_specs=tuple([vmem] * 3),
        scratch_shapes=[
            pltpu.VMEM((rows_e, LANES), F32),
            pltpu.VMEM((rows, LANES), F32),
            pltpu.VMEM((rows_e, LANES), F32),
            pltpu.VMEM((rows_e, LANES), F32),
            pltpu.VMEM((rows_e, LANES), F32),
            pltpu.VMEM((rows_e, LANES), BF16),
            pltpu.VMEM((2 * blocks, rows, LANES), F32),
            pltpu.VMEM((2 * blocks, R, LANES), F32),
            pltpu.VMEM((blocks, rows, LANES), BF16),
            pltpu.VMEM((blocks, rows_e, LANES), BF16),
            pltpu.VMEM((blocks, rows, 2 * H), BF16),
            pltpu.VMEM((blocks, rows_e, 2 * H), BF16),
            pltpu.VMEM((blocks, 2, rows, 6 * H), BF16),
            pltpu.VMEM((blocks, 2, rows_e, 6 * H), BF16),
            pltpu.VMEM((2, frames, 2 * LANES), F32),
            pltpu.VMEM((rows_e, 2 * H), F32),
            pltpu.VMEM((2, rows_e, 4 * H), BF16),
            pltpu.VMEM((2, 2 * H, 4 * H), BF16),
            pltpu.VMEM((LANES, 8 * H), BF16),
            pltpu.VMEM((2, 4 * H, H), BF16),
            pltpu.VMEM((blocks, 2, LANES, 2 * H), BF16),
            pltpu.VMEM((2 * blocks, 8, LANES), F32),
            pltpu.VMEM((frames, LANES), F32),
            pltpu.VMEM((rows, LANES), F32),
            pltpu.VMEM((frames, LANES), BF16),
            pltpu.VMEM((rows, LANES), BF16),
            pltpu.VMEM((rows, LANES), BF16),
            pltpu.VMEM((C, 2 * C), BF16),
            pltpu.VMEM((2 * C, 2 * LANES), BF16),
            pltpu.VMEM((mask_row + C + 8, LANES), F32),
            pltpu.VMEM((mask_row, LANES), F32),
            pltpu.VMEM((mask_row + C + 8, LANES), F32),
            pltpu.VMEM((mask_row, LANES), F32),
            pltpu.SemaphoreType.DMA((4,)),
            pltpu.VMEM((2 * blocks, lay["total"], 4 * H), BF16),
            pltpu.VMEM((2 * blocks, lay["total"] + PART * outer, 4 * H), BF16),
            pltpu.VMEM((16, 4 * H), F32),
            pltpu.SemaphoreType.DMA((2 * blocks, 6 + outer, 2)),
        ],
        compiler_params=pltpu.CompilerParams(
            vmem_limit_bytes=62 * 1024 * 1024, collective_id=0, has_side_effects=True
        ),
        name="dual_path",
    )(
        clip_lengths,
        clip_pads,
        spans.transpose(0, 2, 1),
        encoded.T,
        lstm_in,
        lstm_rec,
        lstm_bias,
        proj_weight.transpose(0, 1, 3, 2),
        proj_bias,
        gln_gain,
        gln_shift,
        mask_weight,
        mask_bias,
        dec_weight.T,
        wave_grad,
    )
    half = dec_weight.shape[1] // 2
    per_section = pl.BlockSpec((None, lay["total"], 4 * H), lambda n: (n, 0, 0))

    def whole(*dims):
        return pl.BlockSpec(dims, lambda n: (0,) * len(dims))

    def section(*dims):
        return pl.BlockSpec((None, None) + dims, lambda n: (n // 2, n % 2) + (0,) * len(dims))

    finals = pl.pallas_call(
        functools.partial(unpack_kernel, (C, H)),
        grid=(2 * blocks,),
        out_shape=(
            shape((1, 2 * frames * half), F32),
            shape((R, C, K), F32),
            shape((blocks, 2, 2, C, 4 * H), F32),
            shape((blocks, 2, 2, H, 4 * H), F32),
            shape((blocks, 2, 2, 4 * H), F32),
            shape((blocks, 2, C, 2 * H), F32),
            shape((blocks, 2, C), F32),
            shape((blocks, 2, C), F32),
            shape((blocks, 2, C), F32),
            shape((1, C, C), F32),
            shape((1, C), F32),
            shape((2 * half, C), F32),
        ),
        in_specs=[
            per_section,
            whole(1, 2 * frames * half),
            pl.BlockSpec((R // (2 * blocks), C, K), lambda n: (n, 0, 0)),
        ],
        out_specs=(
            whole(1, 2 * frames * half),
            pl.BlockSpec((R // (2 * blocks), C, K), lambda n: (n, 0, 0)),
            section(2, C, 4 * H),
            section(2, H, 4 * H),
            section(2, 4 * H),
            section(C, 2 * H),
            whole(blocks, 2, C),
            whole(blocks, 2, C),
            whole(blocks, 2, C),
            whole(1, C, C),
            whole(1, C),
            whole(2 * half, C),
        ),
        compiler_params=pltpu.CompilerParams(vmem_limit_bytes=60 * 1024 * 1024),
        name="unpack",
    )(outs[2], outs[0], outs[1])
    return (
        finals[0],
        finals[1].transpose(0, 2, 1),
        finals[2],
        finals[3],
        finals[4],
        finals[5].transpose(0, 1, 3, 2),
        finals[6],
        finals[7],
        finals[8],
        finals[9],
        finals[10],
        finals[11].T,
    )


def solution(mesh):
    return jax.shard_map(
        functools.partial(shards, mesh.shape["dp"]),
        mesh=mesh,
        in_specs=(
            P(("dp", "spk"), None, None),
            P(("dp", "spk"), None),
            P("dp", None, None),
            P("dp", None, None),
            P(),
            P(),
            P(),
            P(),
            P(),
            P(),
            P(),
            P("spk", None, None),
            P("spk", None),
            P(),
            P("spk", "dp"),
        ),
        out_specs=(
            P("spk", "dp"),
            P(("dp", "spk"), None, None),
            P(),
            P(),
            P(),
            P(),
            P(),
            P(),
            P(),
            P("spk", None, None),
            P("spk", None),
            P(),
        ),
        check_vma=False,
    )
```

```python
import functools

import jax
import jax.numpy as jnp
from jax import lax
from jax.experimental import pallas as pl
from jax.experimental.pallas import tpu as pltpu
from jax.sharding import PartitionSpec as P

F32 = jnp.float32
BF16 = jnp.bfloat16
LANES = 128
PART = 16
PAIR = 2 * PART
MESH = pl.DeviceIdType.MESH


def dot(a, b):
    return jnp.dot(a, b, preferred_element_type=F32)


def dot_tn(a, b):
    return lax.dot_general(a, b, (((0,), (0,)), ((), ())), preferred_element_type=F32)


def dot_nt(a, b):
    return lax.dot_general(a, b, (((1,), (1,)), ((), ())), preferred_element_type=F32)


def chunks(total, size, body):
    assert total % size == 0

    def step(i, carry):
        body(pl.multiple_of(i * size, size))
        return carry

    lax.fori_loop(0, total // size, step, 0)


class Place:
    def __init__(self, num_dp):
        self.dp, self.spk = lax.axis_index("dp"), lax.axis_index("spk")
        self.bits = num_dp.bit_length()

    def bit(self, k):
        if k == 1:
            return self.spk
        return self.dp // (1 << max(k - 1, 0)) % 2

    def device(self, mask):
        dp, spk = self.dp, self.spk
        for k in range(self.bits):
            if mask >> k & 1:
                if k == 1:
                    spk = 1 - spk
                else:
                    dp = dp + (1 - 2 * self.bit(k)) * (1 << max(k - 1, 0))
        return {"dp": dp, "spk": spk}

    def index(self, bits, mask=0):
        number = 0
        for i, k in enumerate(bits):
            one = 1 - self.bit(k) if mask >> k & 1 else self.bit(k)
            number = number + one * (1 << i)
        return number

    def masks(self, bits):
        found = []
        for m in range((1 << len(bits)) - 1, 0, -1):
            found.append(sum((m >> i & 1) << k for i, k in enumerate(bits)))
        return found


class Reduction:
    def __init__(self, buf, recv, out, sems, place, stages, outer, times):
        self.buf, self.recv, self.out, self.sems, self.place = buf, recv, out, sems, place
        self.steps, back = [], []
        off, size, at, sem = 0, buf.shape[0], 0, 0
        for i, bits in enumerate(stages):
            masks = place.masks(bits)
            part = size // (len(masks) + 1)
            own = off + place.index(bits) * part
            last = i == len(stages) - 1
            self.steps.append(
                (
                    functools.partial(self.scatter, sem, masks, bits, off, part, at),
                    functools.partial(self.add, len(masks), own, part, at, out if last else buf),
                    times[len(bits)],
                )
            )
            back.append((masks, own, part, times[len(bits)]))
            off, size = own, part
            at += len(masks) * part
            sem += 1
        for k in outer:
            self.steps.append(
                (
                    functools.partial(self.double, sem, k, off, size, at),
                    functools.partial(self.add_double, off, size, at),
                    times[1],
                )
            )
            at += size
            sem += 1
        for masks, own, part, time in reversed(back):
            self.steps.append((functools.partial(self.gather, sem, masks, own, part), None, time))
            sem += 1
        self.pending, self.after, self.due = None, None, 0.0

    def copy(self, sem, src, dst, device):
        return pltpu.make_async_remote_copy(
            src_ref=src,
            dst_ref=dst,
            send_sem=self.sems.at[sem, 0],
            recv_sem=self.sems.at[sem, 1],
            device_id=device,
            device_id_type=MESH,
        )

    def rows(self, ref, off, size):
        return ref.at[pl.ds(pl.multiple_of(off, PART), size)]

    def all_of(self, sem, masks, part):
        rows = self.recv.at[0 : len(masks) * part]
        return self.copy(sem, rows, rows, self.place.device(masks[0]))

    def scatter(self, sem, masks, bits, off, part, at):
        for i, mask in enumerate(masks):
            src = self.rows(self.buf, off + self.place.index(bits, mask) * part, part)
            dst = self.recv.at[at + i * part : at + (i + 1) * part]
            self.copy(sem, src, dst, self.place.device(mask)).start()
        return self.all_of(sem, masks, part)

    def add(self, number, own, part, at, target):
        def body(i, carry):
            rows = pl.ds(pl.multiple_of(own + i * PART, PART), PART)
            for lanes in [slice(x, x + LANES) for x in range(0, self.buf.shape[1], LANES)]:
                total = self.buf[rows, lanes].astype(F32)
                for q in range(number):
                    new = pl.ds(pl.multiple_of(at + q * part + i * PART, PART), PART)
                    total = total + self.recv[new, lanes].astype(F32)
                target[rows, lanes] = total.astype(BF16)
            return carry

        lax.fori_loop(0, part // PART, body, 0)

    def double(self, sem, k, off, size, at):
        copy = self.copy(sem, self.rows(self.out, off, size), self.recv.at[at : at + size], self.place.device(1 << k))
        copy.start()
        return copy

    def add_double(self, off, size, at):
        rows = pl.ds(pl.multiple_of(off, PART), size)
        self.out[rows] = (self.out[rows].astype(F32) + self.recv[at : at + size].astype(F32)).astype(BF16)

    def gather(self, sem, masks, own, part):
        rows = self.rows(self.out, own, part)
        for mask in masks:
            self.copy(sem, rows, rows, self.place.device(mask)).start()
        return self.all_of(sem, masks, part)

    def advance(self, now):
        if self.pending is not None:
            self.pending.wait()
            if self.after is not None:
                self.after()
            self.pending = None
        if self.steps:
            start, self.after, time = self.steps.pop(0)
            self.pending = start()
            self.due = now + time

    def over(self):
        return self.pending is None and not self.steps


def local_kernel(
    sizes,
    lengths_ref,
    pads_ref,
    spans_ref,
    enc_ref,
    w_in_ref,
    w_rec_ref,
    w_bias_ref,
    w_proj_ref,
    proj_bias_ref,
    gain_ref,
    shift_ref,
    mask_in_ref,
    mask_bias_in_ref,
    dec_in_ref,
    wave_grad_ref,
    wave_out,
    spans_out,
    sums_out,
    stream,
    valid,
    mx,
    xj,
    dz,
    dmj,
    normed,
    inv_all,
    u_a,
    u_e,
    hc_a,
    hc_e,
    sv_a,
    sv_e,
    gd,
    dh,
    dp,
    wcat,
    wit,
    wrt,
    pws,
    vec,
    enc_t,
    pre,
    masked,
    feats,
    dpre,
    mask_ref,
    dec_ref,
    send,
    own,
    got,
    wave_got,
    sems,
    sums,
    recv,
    small,
    sum_sems,
    all_sums,
    grad_spans,
    out_sems,
):
    R, K, C, H, clips, blocks, kp, num_dp = sizes
    rows, rows_e = R * K, R * kp
    hop = K // 2
    frames = R * hop
    half = dec_in_ref.shape[0] // 2
    wr = frames * half // LANES
    group = LANES // half
    cr = rows
    speaker = lax.axis_index("spk")
    partner = {"spk": 1 - speaker}

    barrier = pltpu.get_barrier_semaphore()
    place = Place(num_dp)
    everyone = place.masks(range(1, min(place.bits, 5))) + [1 << k for k in [0, *range(5, place.bits)]]
    for mask in everyone:
        pl.semaphore_signal(barrier, inc=1, device_id=place.device(mask), device_id_type=MESH)

    mask_row = -(-wr // 8) * 8
    for i in range(wr):
        at = pl.multiple_of(speaker * (wr * LANES) + i * LANES, LANES)
        own[i : i + 1] = wave_grad_ref[0:1, pl.ds(at, LANES)].astype(F32)
        at = pl.multiple_of((1 - speaker) * (wr * LANES) + i * LANES, LANES)
        send[i : i + 1] = wave_grad_ref[0:1, pl.ds(at, LANES)].astype(F32)
    mask_f = mask_in_ref[0].astype(F32)
    send[wr:mask_row] = jnp.zeros((mask_row - wr, LANES), F32)
    send[mask_row : mask_row + C] = jnp.concatenate([mask_f, mask_f], axis=1)
    bias_f = mask_bias_in_ref[0:1].astype(F32)
    bias_f = jnp.concatenate([bias_f, bias_f], axis=1)
    send[mask_row + C : mask_row + C + 8] = jnp.broadcast_to(bias_f, (8, LANES))

    jio = lax.broadcasted_iota(jnp.int32, (R, LANES), 0)
    lane = lax.broadcasted_iota(jnp.int32, (1, LANES), 1)
    ones_lanes = jnp.logical_and(lane >= C, lane < C + 3)

    lens = [lengths_ref[0, speaker, c] for c in range(clips)]
    pads = [pads_ref[0, speaker, c] for c in range(clips)]
    starts, ends, at = [], [], 0
    for c in range(clips):
        starts.append(at)
        at = at + lens[c]
        ends.append(at)

    def is_start(j):
        hit = j == starts[0]
        for c in range(1, clips):
            hit = jnp.logical_or(hit, j == starts[c])
        return hit

    def is_end(j):
        hit = j == ends[0] - 1
        for c in range(1, clips):
            hit = jnp.logical_or(hit, j == ends[c] - 1)
        return hit

    members, thr, inv_count = [], jnp.full((R, LANES), K, jnp.int32), jnp.zeros((R, LANES), F32)
    for c in range(clips):
        member = jnp.logical_and(jio >= starts[c], jio < ends[c]).astype(F32)
        members.append(member)
        thr = jnp.where(jio == ends[c] - 1, K - pads[c], thr)
        count = (C * (K * lens[c] - pads[c])).astype(F32)
        inv_count = inv_count + member / jnp.full((R, LANES), count, F32)
    not_first = 1.0 - is_start(jio).astype(F32)
    next_not_first = 1.0 - jnp.logical_or(is_start(jio + 1), jio == R - 1).astype(F32)

    def clip_sum(x):
        out = jnp.zeros((R, 1), F32)
        for member in members:
            out = out + member[:, :1] * jnp.sum(member * x, axis=(0, 1), keepdims=True)
        return out

    def fill_valid(r):
        k = lax.broadcasted_iota(jnp.int32, (cr // R, R, LANES), 0) + r // R
        low = lax.broadcasted_iota(jnp.int32, (cr // R, R, LANES), 2) < C
        ok = jnp.logical_and(k < thr[None], low).astype(F32)
        valid[pl.ds(r, cr)] = ok.reshape(cr, LANES)

    chunks(rows, cr, fill_valid)

    near, far = list(range(1, min(place.bits, 3))), list(range(3, min(place.bits, 5)))
    outer = range(5, place.bits)
    times = {1: 1.7, 2: 4.2, 4: 6.8}

    def reduction(n, stages):
        reduce = Reduction(sums.at[n], recv.at[n], all_sums.at[n], sum_sems.at[n], place, stages, outer, times)
        reduce.number = n
        return reduce

    lay = sum_rows(C, H)
    active = []
    clock = [0.0]

    def point(passed):
        clock[0] += passed
        for reduce in active:
            if not reduce.over() and reduce.due <= clock[0]:
                reduce.advance(clock[0])

    for n in range(2 * blocks):
        for at in (lay["proj"], lay["head"]):
            sums[n, at : at + PAIR] = jnp.zeros((PAIR, 4 * H), BF16)

    pws[...] = jnp.zeros_like(pws)
    wit[...] = jnp.zeros_like(wit)
    vec[...] = jnp.zeros_like(vec)
    for b in range(blocks):
        for s in range(2):
            n = 2 * b + s
            pws[b, s, 0:C] = w_proj_ref[b, s]
            vec[n, 0:1, 0:C] = proj_bias_ref[b, s : s + 1]
            vec[n, 1:2, 0:C] = gain_ref[b, s : s + 1]
            vec[n, 2:3, 0:C] = shift_ref[b, s : s + 1]

    stream[...] = jnp.zeros_like(stream)
    for j in range(R):
        x = spans_ref[j].astype(F32)
        x = jnp.concatenate([x, jnp.zeros_like(x)], axis=0).T
        stream[pl.ds(j, K, stride=R), :] = x

    def start_stream(r):
        x = stream[pl.ds(r, cr)] * valid[pl.ds(r, cr)]
        stream[pl.ds(r, cr)] = jnp.where(ones_lanes, 1.0, x)

    chunks(rows, cr, start_stream)

    gate_scale = jnp.where(
        lax.broadcasted_iota(jnp.int32, (1, 4 * H), 1) // H == 2, 1.0, 0.5
    ).astype(F32)

    def lane_part(x, g):
        return x[:, g * H : (g + 1) * H]

    def gate_step(d, sv, b, r, n, p, c, keep_next):
        acts = [jnp.tanh(p[:, g * H : (g + 1) * H]) for g in range(4)]
        ti, tf, g, to = acts
        i, f, o = 0.5 * ti + 0.5, 0.5 * tf + 0.5, 0.5 * to + 0.5
        cn = f * c + i * g
        tc = jnp.tanh(cn)
        h = o * tc
        parts = [
            g * (0.25 - 0.25 * ti * ti),
            c * (0.25 - 0.25 * tf * tf),
            i * (1.0 - g * g),
            tc * (0.25 - 0.25 * to * to),
            o * (1.0 - tc * tc),
            f,
        ]
        for m, part in enumerate(parts):
            sv[b, d, pl.ds(r, n), m * H : (m + 1) * H] = part.astype(BF16)
        if keep_next is None:
            return h.astype(BF16), h.astype(BF16), cn
        return h.astype(BF16), (h * keep_next).astype(BF16), cn * keep_next

    def run_forward(b, sec, u, hc, sv, n, steps, unroll):
        total = n * steps
        for d in range(2):
            wcat[d, 0:H] = (w_rec_ref[b, sec, d].astype(F32) * gate_scale).astype(BF16)
            wcat[d, H : H + C] = (w_in_ref[b, sec, d].astype(F32) * gate_scale).astype(BF16)
            bias = w_bias_ref[b, sec, d : d + 1] * gate_scale
            terms = []
            for _ in range(3):
                terms.append(bias.astype(BF16).astype(F32))
                bias = bias - terms[-1]
            row = lax.broadcasted_iota(jnp.int32, (H - C, 4 * H), 0)
            block = jnp.zeros((H - C, 4 * H), F32)
            for m, term in enumerate(terms):
                block = jnp.where(row == m, jnp.broadcast_to(term, block.shape), block)
            wcat[d, H + C : 2 * H] = block.astype(BF16)

        def step(t, carry):
            hf, hb, cf, cb = carry
            back = steps - 1 - t
            rf, rb = t * n, back * n
            if sec == 0:
                rf, rb = pl.multiple_of(rf, n), pl.multiple_of(rb, n)
            kf = kb = None
            if sec == 1:
                kf = 1.0 - is_start(t + 1).astype(F32)
                kb = 1.0 - is_end(back - 1).astype(F32)
            if sec == 1 and t < steps // 2:
                uf = stream[pl.ds(t, n, stride=R), :].astype(BF16)
                ub = stream[pl.ds(back, n, stride=R), :].astype(BF16)
                u[b, rf : rf + n] = uf
                u[b, rb : rb + n] = ub
            else:
                uf, ub = u[b, pl.ds(rf, n)], u[b, pl.ds(rb, n)]
            pf = dot(jnp.concatenate([hf, uf], axis=1), wcat[0])
            pb = dot(jnp.concatenate([hb, ub], axis=1), wcat[1])
            out_f, hf, cf = gate_step(0, sv, b, rf, n, pf, cf, kf)
            out_b, hb, cb = gate_step(1, sv, b, rb, n, pb, cb, kb)
            hc[b, pl.ds(rf, n), 0:H] = out_f
            hc[b, pl.ds(rb, n), H : 2 * H] = out_b
            return hf, hb, cf, cb

        zh, zc = jnp.zeros((n, H), BF16), jnp.zeros((n, H), F32)
        carry = (zh, zh, zc, zc)
        if sec == 1:
            for t in range(steps):
                carry = step(t, carry)
        else:
            lax.fori_loop(0, steps, step, carry, unroll=unroll)

    def norm_forward(b, sec):
        n = 2 * b + sec
        gain, shift = vec[n, 1:2], vec[n, 2:3]

        def fold(body):
            def step(i, acc):
                return acc + jnp.sum(body(pl.multiple_of(i * cr, cr)).reshape(cr // R, R, LANES), axis=0)

            return lax.fori_loop(0, rows // cr, step, jnp.zeros((R, LANES), F32))

        mean = clip_sum(fold(lambda r: valid[pl.ds(r, cr)] * mx[pl.ds(r, cr)])) * inv_count

        def spread(r):
            x = mx[pl.ds(r, cr)].reshape(cr // R, R, LANES) - mean[None]
            return valid[pl.ds(r, cr)] * (x * x).reshape(cr, LANES)

        inv = lax.rsqrt(clip_sum(fold(spread)) * inv_count + 1e-08)
        inv_all[n] = inv

        def apply(r):
            x = (mx[pl.ds(r, cr)].reshape(cr // R, R, LANES) - mean[None]) * inv[None]
            x = x.reshape(cr, LANES)
            normed[n, pl.ds(r, cr)] = x
            stream[pl.ds(r, cr)] += valid[pl.ds(r, cr)] * (x * gain + shift)

        chunks(rows, cr, apply)

    def forward_block(b, carry):
        def u_intra(r):
            u_a[b, pl.ds(r, cr)] = stream[pl.ds(r, cr)].astype(BF16)

        chunks(rows, cr, u_intra)
        run_forward(b, 0, u_a, hc_a, sv_a, R, K, 10)

        mx[0:rows] = dot_nt(hc_a[b], pws[b, 0]) + vec[2 * b, 0:1]
        norm_forward(b, 0)

        run_forward(b, 1, u_e, hc_e, sv_e, kp, R, R)

        xj[...] = dot_nt(hc_e[b], pws[b, 1]) + vec[2 * b + 1, 0:1]
        for k in range(K):
            mx[k * R : (k + 1) * R] = xj[pl.ds(k, R, stride=kp), :]
        norm_forward(b, 1)
        return carry

    forward_block(0, 0)
    pl.semaphore_wait(barrier, len(everyone))
    swap = pltpu.make_async_remote_copy(
        src_ref=send, dst_ref=got, send_sem=sems.at[0], recv_sem=sems.at[1], device_id=partner, device_id_type=MESH
    )
    swap.start()
    lax.fori_loop(1, blocks, forward_block, 0)

    e = enc_ref[...].astype(F32)
    xj[0:frames] = jnp.concatenate([e, e], axis=0).T
    for j in range(R):
        enc_t[pl.ds(j, hop, stride=R), :] = xj[j * hop : (j + 1) * hop]

    first_half = lane < half
    second_half = jnp.logical_and(lane >= half, lane < 2 * half)
    d = dec_in_ref[...].astype(F32)
    d = jnp.concatenate([d, jnp.zeros((LANES - 2 * half, C), F32)], axis=0).T
    dec_ref[0:C, 0:LANES] = jnp.where(first_half, d, 0.0).astype(BF16)
    dec_ref[C : 2 * C, 0:LANES] = jnp.where(second_half, pltpu.roll(d, half, 1), 0.0).astype(BF16)
    dec_ref[0:C, LANES : 2 * LANES] = jnp.where(first_half, pltpu.roll(d, LANES - half, 1), 0.0).astype(BF16)
    dec_ref[C : 2 * C, LANES : 2 * LANES] = jnp.where(second_half, d, 0.0).astype(BF16)

    swap.wait()
    mask_ref[...] = jnp.concatenate([mask_f, got[mask_row : mask_row + C, 0:C]], axis=1).astype(BF16)
    mask_bias = jnp.concatenate(
        [mask_bias_in_ref[0:1].astype(F32), got[mask_row + C : mask_row + C + 1, 0:C]], axis=1
    )
    for q in range(group):
        a = pltpu.roll(own[0:mask_row], LANES - q * half, 1) if q else own[0:mask_row]
        b = pltpu.roll(got[0:mask_row], (LANES - (q - 1) * half) % LANES, 1) if q != 1 else got[0:mask_row]
        w = jnp.where(first_half, a, jnp.where(second_half, b, 0.0))
        xj[pl.ds(q, wr, stride=group), :] = w[0:wr]
    for j in range(R):
        gd[1, j * hop : (j + 1) * hop, 0:LANES] = xj[j * hop : (j + 1) * hop]
    for j in range(R):
        xj[pl.ds(j, hop, stride=R), :] = gd[1, j * hop : (j + 1) * hop, 0:LANES]

    def head_pre(r):
        x = stream[pl.ds(r, cr)]
        f = x * (0.5 * jnp.tanh(0.5 * x) + 0.5)
        f = jnp.where(lane == C, 1.0, f).astype(BF16)
        feats[pl.ds(r, cr)] = f
        pre[pl.ds(r, cr)] = dot(f[:, 0:C], mask_ref[...]) + mask_bias

    chunks(rows, cr, head_pre)

    hr = frames // 5

    def tile(v):
        return jnp.broadcast_to(v[None], (hr // R, R, LANES)).reshape(hr, LANES)

    for q in range(5):
        r = q * hr
        fr = pre[r : r + hr] + tile(not_first) * pre[frames + r - 1 : frames + r - 1 + hr]
        e = enc_t[r : r + hr]
        sp = jnp.maximum(fr, 0.0) + jnp.log1p(jnp.exp(-jnp.abs(fr)))
        masked[r : r + hr] = (sp * e).astype(BF16)
        pre[r : r + hr] = e * (0.5 * jnp.tanh(0.5 * fr) + 0.5)
    for q in range(5):
        r = q * hr
        gd[0, r : r + hr, 0 : 2 * LANES] = dot(masked[r : r + hr], dec_ref[...])
    gd[1, 0:R, 0:LANES] = (
        gd[0, 0:R, 0:LANES] + not_first * gd[0, frames - R - 1 : frames - 1, LANES : 2 * LANES]
    )
    gd[1, R:frames, 0:LANES] = gd[0, R:frames, 0:LANES] + gd[0, 0 : frames - R, LANES : 2 * LANES]
    xj[frames : 2 * frames] = gd[1, 0:frames, 0:LANES]
    for j in range(R):
        gd[1, j * hop : (j + 1) * hop, 0:LANES] = xj[pl.ds(frames + j, hop, stride=R), :]
    xj[frames : 2 * frames] = gd[1, 0:frames, 0:LANES]
    zero = jnp.zeros((wr, LANES), F32)
    w_own, w_far = zero, zero
    for q in range(group):
        x = xj[pl.ds(frames + q, wr, stride=group), :]
        a = jnp.where(first_half, x, 0.0)
        b = jnp.where(second_half, x, 0.0)
        w_own = w_own + (pltpu.roll(a, q * half, 1) if q else a)
        w_far = w_far + (pltpu.roll(b, (q - 1) * half % LANES, 1) if q != 1 else b)
    own[0:wr] = w_own
    send[0:wr] = w_far
    wave_swap = pltpu.make_async_remote_copy(
        src_ref=send.at[0:mask_row],
        dst_ref=wave_got,
        send_sem=sems.at[2],
        recv_sem=sems.at[3],
        device_id=partner,
        device_id_type=MESH,
    )
    wave_swap.start()

    gd[0, 0:frames, 0:LANES] = xj[0:frames]
    gd[0, 0 : frames - R, LANES : 2 * LANES] = xj[R:frames]
    gd[0, frames - R : frames, LANES : 2 * LANES] = next_not_first * xj[1 : R + 1]
    dp[0:frames, 0 : 2 * LANES] = gd[0, 0:frames, 0 : 2 * LANES].astype(BF16)
    g = dot_tn(masked[...], dp[0:frames, 0 : 2 * LANES])
    g_lead = g[0:C, 0:LANES] + pltpu.roll(g[C : 2 * C, 0:LANES], LANES - half, 1)
    g_tail = pltpu.roll(g[0:C, LANES : 2 * LANES], half, 1) + g[C : 2 * C, LANES : 2 * LANES]
    g = jnp.where(first_half, g_lead, g_tail)
    g_dec = jnp.concatenate([g, jnp.zeros_like(g)], axis=0).T[0 : 2 * half]
    xj[frames : frames + 8] = jnp.zeros((8, LANES), F32)
    for q in range(5):
        r = q * hr
        dfr = dot_nt(dp[r : r + hr, 0 : 2 * LANES], dec_ref[...]) * pre[r : r + hr]
        xj[r : r + hr] = dfr
        dpre[r : r + hr] = dfr.astype(BF16)
    for q in range(5):
        r = q * hr
        dpre[frames + r : frames + r + hr] = (tile(next_not_first) * xj[r + 1 : r + 1 + hr]).astype(BF16)
    gm = dot_tn(feats[...], dpre[...])
    gm = jnp.where(speaker == 0, gm, pltpu.roll(gm, C, 1))
    n, at = 2 * blocks - 1, lay["head"]
    for q in range(4):
        sums[n, at : at + 16, q * LANES : (q + 1) * LANES] = gm[16 * q : 16 * q + 16].astype(BF16)
    sums[n, at + 16 : at + 32, 0:LANES] = jnp.where(lane < C, g_dec, 0.0).astype(BF16)
    sums[n, at + 16 : at + 32, LANES : 2 * LANES] = jnp.broadcast_to(gm[C : C + 1], (16, LANES)).astype(BF16)
    dz[...] = jnp.zeros_like(dz)

    def head_dz(r):
        x = stream[pl.ds(r, cr)]
        sg = 0.5 * jnp.tanh(0.5 * x) + 0.5
        df = dot_nt(dpre[pl.ds(r, cr)], mask_ref[...])
        df = jnp.concatenate([df, jnp.zeros_like(df)], axis=1)
        dz[pl.ds(r, cr)] = df * sg * (1.0 + x * (1.0 - sg))

    chunks(rows, cr, head_dz)

    def norm_backward(b, sec):
        n = 2 * b + sec
        gain = vec[n, 1:2]

        def sums(i, acc):
            r = pl.multiple_of(i * cr, cr)
            v = valid[pl.ds(r, cr)] * dz[pl.ds(r, cr)]
            w = v * normed[n, pl.ds(r, cr)]
            return (
                acc[0] + jnp.sum(v.reshape(cr // R, R, LANES), axis=0),
                acc[1] + jnp.sum(w.reshape(cr // R, R, LANES), axis=0),
            )

        zero = jnp.zeros((R, LANES), F32)
        s1, s2 = lax.fori_loop(0, rows // cr, sums, (zero, zero))
        small[1:2, LANES : 2 * LANES] = jnp.sum(s2, axis=0, keepdims=True)
        small[1:2, 2 * LANES : 3 * LANES] = jnp.sum(s1, axis=0, keepdims=True)
        m1 = clip_sum(s1 * gain) * inv_count
        m2 = clip_sum(s2 * gain) * inv_count
        inv = inv_all[n]

        def apply(i, acc):
            r = pl.multiple_of(i * cr, cr)
            d = (dz[pl.ds(r, cr)] * gain).reshape(cr // R, R, LANES)
            x = normed[n, pl.ds(r, cr)].reshape(cr // R, R, LANES)
            y = (d - m1[None] - x * m2[None]) * inv[None]
            y = (y.reshape(cr, LANES) * valid[pl.ds(r, cr)]).astype(BF16)
            if sec == 0:
                dmj[pl.ds(r, cr)] = y
            y = y.astype(F32)
            if sec == 1:
                mx[pl.ds(r, cr)] = y
            return acc + jnp.sum(y.reshape(cr // R, R, LANES), axis=0)

        acc = lax.fori_loop(0, rows // cr, apply, zero)
        small[1:2, 0:LANES] = jnp.sum(acc, axis=0, keepdims=True)

    def back_step(d, sv, b, r, n, dhn, dcn, keep):
        a = [sv[b, d, pl.ds(r, n), m * H : (m + 1) * H].astype(F32) for m in range(6)]
        g = dh[pl.ds(r, n), d * H : (d + 1) * H] + dhn
        dc = dcn + g * a[4]
        for m in range(4):
            dp[pl.ds(r, n), (4 * d + m) * H : (4 * d + m + 1) * H] = ((g if m == 3 else dc) * a[m]).astype(BF16)
        dhn = dot(dp[pl.ds(r, n), 4 * d * H : 4 * (d + 1) * H], wrt[d])
        dcn = dc * a[5]
        if keep is not None:
            dhn, dcn = dhn * keep, dcn * keep
        return dhn, dcn

    def run_backward(b, sec, u, hc, sv, n, steps, unroll, parts):
        total = n * steps
        out = sums.at[2 * b + sec]
        g = dot_tn(dmj[0:total], hc[b])[0:C].astype(BF16)
        at = lay["proj"]
        out[at : at + C // 2, 0 : 2 * H] = g[0 : C // 2]
        out[at : at + C // 2, 2 * H : 4 * H] = g[C // 2 : C]

        dh[0:total] = dot(dmj[0:total], pws[b, sec])
        for d in range(2):
            wrt[d] = w_rec_ref[b, sec, d].T
            wit[d * 4 * H : (d + 1) * 4 * H, 0:C] = w_in_ref[b, sec, d].T

        def step(t, carry):
            hf, hb, cf, cb = carry
            back = steps - 1 - t
            rf = pl.multiple_of(back * n, n)
            rb = pl.multiple_of(t * n, n)
            kf = kb = None
            if sec == 1:
                kf = 1.0 - is_start(back).astype(F32)
                kb = 1.0 - is_end(t).astype(F32)
            hf, cf = back_step(0, sv, b, rf, n, hf, cf, kf)
            hb, cb = back_step(1, sv, b, rb, n, hb, cb, kb)
            return hf, hb, cf, cb

        z = jnp.zeros((n, H), F32)
        carry = (z, z, z, z)
        point(2.5)
        for p in range(parts):
            carry = lax.fori_loop(p * steps // parts, (p + 1) * steps // parts, step, carry, unroll=unroll)
            point(steps * 0.125 / parts)
        if sec == 1:
            for j in range(1, steps):
                kf = (1.0 - is_start(j).astype(F32)).astype(BF16)
                at = slice((j - 1) * n, j * n)
                hc[b, at, 0:H] = hc[b, at, 0:H] * kf
                kb = (1.0 - is_end(j - 1).astype(F32)).astype(BF16)
                at = slice(j * n, (j + 1) * n)
                hc[b, at, H : 2 * H] = hc[b, at, H : 2 * H] * kb
        last = (b, sec) == (0, 0)
        core = place.bit(0)
        reduce = reduction(2 * b + sec, [[0], near + far] if b == 0 else [[0], near, far])
        for d in (1 - core, core):
            gates = pl.ds(pl.multiple_of(4 * d * H, H), 4 * H)
            g = dot_tn(u[b], dp[0:total, gates])
            base = d * lay["half"]
            out[pl.ds(pl.multiple_of(base + lay["in"], PART), C)] = g[0:C].astype(BF16)
            small[0:1] = g[C : C + 1]
            out[pl.ds(pl.multiple_of(base + lay["small"], PART), 16)] = small[...].astype(BF16)
            h_prev = hc[b, pl.ds(pl.multiple_of(d * n, n), total - n), pl.ds(pl.multiple_of(d * H, H), H)]
            g = dot_tn(h_prev, dp[pl.ds(pl.multiple_of((1 - d) * n, n), total - n), gates])
            out[pl.ds(pl.multiple_of(base + lay["rec"], PART), H)] = g.astype(BF16)
            if d is core:
                point(0.6)
            else:
                reduce.advance(clock[0] + 0.6)
                active.append(reduce)

    def stream_grad(total):
        return dot(dp[0:total], wit[...])

    small[...] = jnp.zeros_like(small)
    for b in reversed(range(blocks)):
        norm_backward(b, 1)
        mx[rows:rows_e] = jnp.zeros((rows_e - rows, LANES), F32)
        for j in range(R):
            dmj[pl.ds(j * kp, kp)] = mx[pl.ds(j, kp, stride=R), :].astype(BF16)
        run_backward(b, 1, u_e, hc_e, sv_e, kp, R, R, 1)

        xj[...] = stream_grad(rows_e)
        for k in range(K):
            dz[k * R : (k + 1) * R] += xj[pl.ds(k, R, stride=kp), :]
        point(1.5)

        norm_backward(b, 0)
        run_backward(b, 0, u_a, hc_a, sv_a, R, K, 10, 5)

        dz[0:rows] += stream_grad(rows)
        point(1.5)

    def finish(r):
        dz[pl.ds(r, cr)] = dz[pl.ds(r, cr)] * valid[pl.ds(r, cr)]

    chunks(rows, cr, finish)
    for j in range(R):
        grad_spans[j] = dz[pl.ds(j, K, stride=R), :].T[0:C]
    exits = [pltpu.make_async_copy(grad_spans, spans_out, out_sems.at[2 * blocks])]
    exits[0].start()
    wave_swap.wait()
    for i in range(wr):
        at = pl.multiple_of(speaker * (wr * LANES) + i * LANES, LANES)
        wave_out[0:1, pl.ds(at, LANES)] = own[i : i + 1]
        at = pl.multiple_of((1 - speaker) * (wr * LANES) + i * LANES, LANES)
        wave_out[0:1, pl.ds(at, LANES)] = wave_got[i : i + 1]

    left = list(active)
    while left:
        for reduce in [reduce for reduce in left if reduce.over()]:
            n = reduce.number
            exits.append(pltpu.make_async_copy(all_sums.at[n], sums_out.at[n], out_sems.at[n]))
            exits[-1].start()
            left.remove(reduce)
        if left:
            nearest = min(left, key=lambda reduce: reduce.due)
            clock[0] = max(clock[0], nearest.due)
            nearest.advance(clock[0])
    for copy in exits:
        copy.wait()


def unpack_kernel(
    sizes,
    sums,
    wave_in,
    spans_in,
    wave_out,
    spans_out,
    in_out,
    rec_out,
    bias_out,
    proj_out,
    proj_bias_out,
    gain_out,
    shift_out,
    mask_out,
    mask_bias_out,
    dec_out,
):
    C, H = sizes
    lay = sum_rows(C, H)
    n = pl.program_id(0)
    b, sec = n // 2, n % 2
    speaker = lax.axis_index("spk")
    spans_out[...] = spans_in[...]
    for d in range(2):
        base = d * lay["half"]
        in_out[d] = sums[base + lay["in"] : base + lay["in"] + C].astype(F32)
        rec_out[d] = sums[base + lay["rec"] : base + lay["rec"] + H].astype(F32)
        small = sums[base + lay["small"] : base + lay["small"] + 16].astype(F32)
        bias_out[d : d + 1] = small[0:1]
        if d == 0:
            for m, out in enumerate((proj_bias_out, gain_out, shift_out)):
                out[b, pl.ds(sec, 1)] = small[1:2, m * LANES : m * LANES + C]
    at = lay["proj"]
    proj_out[0 : C // 2] = sums[at : at + C // 2, 0 : 2 * H].astype(F32)
    proj_out[C // 2 : C] = sums[at : at + C // 2, 2 * H : 4 * H].astype(F32)

    @pl.when(n == 0)
    def _():
        wave_out[...] = wave_in[...]

    @pl.when(n == pl.num_programs(0) - 1)
    def _():
        at = lay["head"]

        def own(x):
            return jnp.where(speaker == 0, x, pltpu.roll(x, C, 1))[:, 0:C]

        for q in range(4):
            x = sums[at : at + 16, q * LANES : (q + 1) * LANES].astype(F32)
            mask_out[0, 16 * q : 16 * q + 16] = own(x)
        x = sums[at + 16 : at + 32, 0 : 2 * LANES].astype(F32)
        mask_bias_out[...] = own(x[:, LANES : 2 * LANES])[0:1]
        dec_out[...] = x[:, 0:C]


def sum_rows(C, H):
    lay, at = {}, 0
    for name, rows in (("in", C), ("rec", H), ("small", 16), ("proj", C // 2)):
        lay[name] = at
        at += rows
    lay["half"] = -(-at // (16 * PART)) * 16 * PART
    lay["head"] = lay["half"] + lay["proj"]
    lay["total"] = 2 * lay["half"]
    return lay


def shards(
    num_dp,
    spans,
    encoded,
    clip_lengths,
    clip_pads,
    lstm_in,
    lstm_rec,
    lstm_bias,
    proj_weight,
    proj_bias,
    gln_gain,
    gln_shift,
    mask_weight,
    mask_bias,
    dec_weight,
    wave_grad,
):
    R, K, C = spans.shape
    H = lstm_rec.shape[3]
    blocks = lstm_in.shape[0]
    clips = clip_lengths.shape[2]
    frames = encoded.shape[0]
    half = dec_weight.shape[1] // 2
    kp = -(-K // 16) * 16
    rows, rows_e = R * K, R * kp
    wr = frames * half // LANES
    mask_row = -(-wr // 8) * 8

    sizes = (R, K, C, H, clips, blocks, kp, num_dp)
    lay = sum_rows(C, H)
    outer = max(num_dp.bit_length() - 5, 0)
    smem = pl.BlockSpec(memory_space=pltpu.SMEM)
    vmem = pl.BlockSpec(memory_space=pltpu.VMEM)
    shape = jax.ShapeDtypeStruct
    outs = pl.pallas_call(
        functools.partial(local_kernel, sizes),
        out_shape=(
            shape((1, 2 * frames * half), F32),
            shape((R, C, K), F32),
            shape((2 * blocks, lay["total"], 4 * H), BF16),
        ),
        in_specs=[smem, smem] + [vmem] * 13,
        out_specs=(vmem, pl.BlockSpec(memory_space=pl.ANY), pl.BlockSpec(memory_space=pl.ANY)),
        scratch_shapes=[
            pltpu.VMEM((rows_e, LANES), F32),
            pltpu.VMEM((rows, LANES), F32),
            pltpu.VMEM((rows_e, LANES), F32),
            pltpu.VMEM((rows_e, LANES), F32),
            pltpu.VMEM((rows_e, LANES), F32),
            pltpu.VMEM((rows_e, LANES), BF16),
            pltpu.VMEM((2 * blocks, rows, LANES), F32),
            pltpu.VMEM((2 * blocks, R, LANES), F32),
            pltpu.VMEM((blocks, rows, LANES), BF16),
            pltpu.VMEM((blocks, rows_e, LANES), BF16),
            pltpu.VMEM((blocks, rows, 2 * H), BF16),
            pltpu.VMEM((blocks, rows_e, 2 * H), BF16),
            pltpu.VMEM((blocks, 2, rows, 6 * H), BF16),
            pltpu.VMEM((blocks, 2, rows_e, 6 * H), BF16),
            pltpu.VMEM((2, frames, 2 * LANES), F32),
            pltpu.VMEM((rows_e, 2 * H), F32),
            pltpu.VMEM((rows_e, 8 * H), BF16),
            pltpu.VMEM((2, 2 * H, 4 * H), BF16),
            pltpu.VMEM((8 * H, LANES), BF16),
            pltpu.VMEM((2, 4 * H, H), BF16),
            pltpu.VMEM((blocks, 2, LANES, 2 * H), BF16),
            pltpu.VMEM((2 * blocks, 8, LANES), F32),
            pltpu.VMEM((frames, LANES), F32),
            pltpu.VMEM((rows, LANES), F32),
            pltpu.VMEM((frames, LANES), BF16),
            pltpu.VMEM((rows, LANES), BF16),
            pltpu.VMEM((rows, LANES), BF16),
            pltpu.VMEM((C, 2 * C), BF16),
            pltpu.VMEM((2 * C, 2 * LANES), BF16),
            pltpu.VMEM((mask_row + C + 8, LANES), F32),
            pltpu.VMEM((mask_row, LANES), F32),
            pltpu.VMEM((mask_row + C + 8, LANES), F32),
            pltpu.VMEM((mask_row, LANES), F32),
            pltpu.SemaphoreType.DMA((4,)),
            pltpu.VMEM((2 * blocks, lay["total"], 4 * H), BF16),
            pltpu.VMEM((2 * blocks, lay["total"] + PART * outer, 4 * H), BF16),
            pltpu.VMEM((16, 4 * H), F32),
            pltpu.SemaphoreType.DMA((2 * blocks, 6 + outer, 2)),
            pltpu.VMEM((2 * blocks, lay["total"], 4 * H), BF16),
            pltpu.VMEM((R, C, K), F32),
            pltpu.SemaphoreType.DMA((2 * blocks + 1,)),
        ],
        compiler_params=pltpu.CompilerParams(
            vmem_limit_bytes=62 * 1024 * 1024, collective_id=0, has_side_effects=True
        ),
        name="dual_path",
    )(
        clip_lengths,
        clip_pads,
        spans.transpose(0, 2, 1),
        encoded.T,
        lstm_in,
        lstm_rec,
        lstm_bias,
        proj_weight.transpose(0, 1, 3, 2),
        proj_bias,
        gln_gain,
        gln_shift,
        mask_weight,
        mask_bias,
        dec_weight.T,
        wave_grad,
    )
    half = dec_weight.shape[1] // 2
    per_section = pl.BlockSpec((None, lay["total"], 4 * H), lambda n: (n, 0, 0))

    def whole(*dims):
        return pl.BlockSpec(dims, lambda n: (0,) * len(dims))

    def section(*dims):
        return pl.BlockSpec((None, None) + dims, lambda n: (n // 2, n % 2) + (0,) * len(dims))

    finals = pl.pallas_call(
        functools.partial(unpack_kernel, (C, H)),
        grid=(2 * blocks,),
        out_shape=(
            shape((1, 2 * frames * half), F32),
            shape((R, C, K), F32),
            shape((blocks, 2, 2, C, 4 * H), F32),
            shape((blocks, 2, 2, H, 4 * H), F32),
            shape((blocks, 2, 2, 4 * H), F32),
            shape((blocks, 2, C, 2 * H), F32),
            shape((blocks, 2, C), F32),
            shape((blocks, 2, C), F32),
            shape((blocks, 2, C), F32),
            shape((1, C, C), F32),
            shape((1, C), F32),
            shape((2 * half, C), F32),
        ),
        in_specs=[
            per_section,
            whole(1, 2 * frames * half),
            pl.BlockSpec((R // (2 * blocks), C, K), lambda n: (n, 0, 0)),
        ],
        out_specs=(
            whole(1, 2 * frames * half),
            pl.BlockSpec((R // (2 * blocks), C, K), lambda n: (n, 0, 0)),
            section(2, C, 4 * H),
            section(2, H, 4 * H),
            section(2, 4 * H),
            section(C, 2 * H),
            whole(blocks, 2, C),
            whole(blocks, 2, C),
            whole(blocks, 2, C),
            whole(1, C, C),
            whole(1, C),
            whole(2 * half, C),
        ),
        compiler_params=pltpu.CompilerParams(vmem_limit_bytes=60 * 1024 * 1024),
        name="unpack",
    )(outs[2], outs[0], outs[1])
    return (
        finals[0],
        finals[1].transpose(0, 2, 1),
        finals[2],
        finals[3],
        finals[4],
        finals[5].transpose(0, 1, 3, 2),
        finals[6],
        finals[7],
        finals[8],
        finals[9],
        finals[10],
        finals[11].T,
    )


def solution(mesh):
    return jax.shard_map(
        functools.partial(shards, mesh.shape["dp"]),
        mesh=mesh,
        in_specs=(
            P(("dp", "spk"), None, None),
            P(("dp", "spk"), None),
            P("dp", None, None),
            P("dp", None, None),
            P(),
            P(),
            P(),
            P(),
            P(),
            P(),
            P(),
            P("spk", None, None),
            P("spk", None),
            P(),
            P("spk", "dp"),
        ),
        out_specs=(
            P("spk", "dp"),
            P(("dp", "spk"), None, None),
            P(),
            P(),
            P(),
            P(),
            P(),
            P(),
            P(),
            P("spk", None, None),
            P("spk", None),
            P(),
        ),
        check_vma=False,
    )
```

```python
import functools

import jax
import jax.numpy as jnp
from jax import lax
from jax.experimental import pallas as pl
from jax.experimental.pallas import tpu as pltpu
from jax.sharding import PartitionSpec as P

F32 = jnp.float32
BF16 = jnp.bfloat16
LANES = 128
PART = 16
PAIR = 2 * PART
MESH = pl.DeviceIdType.MESH


def dot(a, b):
    return jnp.dot(a, b, preferred_element_type=F32)


def dot_tn(a, b):
    return lax.dot_general(a, b, (((0,), (0,)), ((), ())), preferred_element_type=F32)


def dot_nt(a, b):
    return lax.dot_general(a, b, (((1,), (1,)), ((), ())), preferred_element_type=F32)


def chunks(total, size, body):
    assert total % size == 0

    def step(i, carry):
        body(pl.multiple_of(i * size, size))
        return carry

    lax.fori_loop(0, total // size, step, 0)


class Place:
    def __init__(self, num_dp):
        self.dp, self.spk = lax.axis_index("dp"), lax.axis_index("spk")
        self.bits = num_dp.bit_length()

    def bit(self, k):
        if k == 1:
            return self.spk
        return self.dp // (1 << max(k - 1, 0)) % 2

    def device(self, mask):
        dp, spk = self.dp, self.spk
        for k in range(self.bits):
            if mask >> k & 1:
                if k == 1:
                    spk = 1 - spk
                else:
                    dp = dp + (1 - 2 * self.bit(k)) * (1 << max(k - 1, 0))
        return {"dp": dp, "spk": spk}

    def index(self, bits, mask=0):
        number = 0
        for i, k in enumerate(bits):
            one = 1 - self.bit(k) if mask >> k & 1 else self.bit(k)
            number = number + one * (1 << i)
        return number

    def masks(self, bits):
        found = []
        for m in range((1 << len(bits)) - 1, 0, -1):
            found.append(sum((m >> i & 1) << k for i, k in enumerate(bits)))
        return found


class Reduction:
    def __init__(self, buf, recv, out, sems, place, stages, outer, times):
        self.buf, self.recv, self.out, self.sems, self.place = buf, recv, out, sems, place
        self.steps, back = [], []
        off, size, at, sem = 0, buf.shape[0], 0, 0
        for i, bits in enumerate(stages):
            masks = place.masks(bits)
            part = size // (len(masks) + 1)
            own = off + place.index(bits) * part
            last = i == len(stages) - 1
            self.steps.append(
                (
                    functools.partial(self.scatter, sem, masks, bits, off, part, at),
                    functools.partial(self.add, len(masks), own, part, at, out if last else buf),
                    times[len(bits)],
                )
            )
            back.append((masks, own, part, times[len(bits)]))
            off, size = own, part
            at += len(masks) * part
            sem += 1
        for k in outer:
            self.steps.append(
                (
                    functools.partial(self.double, sem, k, off, size, at),
                    functools.partial(self.add_double, off, size, at),
                    times[1],
                )
            )
            at += size
            sem += 1
        for masks, own, part, time in reversed(back):
            self.steps.append((functools.partial(self.gather, sem, masks, own, part), None, time))
            sem += 1
        self.pending, self.after, self.due = None, None, 0.0

    def copy(self, sem, src, dst, device):
        return pltpu.make_async_remote_copy(
            src_ref=src,
            dst_ref=dst,
            send_sem=self.sems.at[sem, 0],
            recv_sem=self.sems.at[sem, 1],
            device_id=device,
            device_id_type=MESH,
        )

    def rows(self, ref, off, size):
        return ref.at[pl.ds(pl.multiple_of(off, PART), size)]

    def all_of(self, sem, masks, part):
        rows = self.recv.at[0 : len(masks) * part]
        return self.copy(sem, rows, rows, self.place.device(masks[0]))

    def scatter(self, sem, masks, bits, off, part, at):
        for i, mask in enumerate(masks):
            src = self.rows(self.buf, off + self.place.index(bits, mask) * part, part)
            dst = self.recv.at[at + i * part : at + (i + 1) * part]
            self.copy(sem, src, dst, self.place.device(mask)).start()
        return self.all_of(sem, masks, part)

    def add(self, number, own, part, at, target):
        def body(i, carry):
            rows = pl.ds(pl.multiple_of(own + i * PART, PART), PART)
            for lanes in [slice(x, x + LANES) for x in range(0, self.buf.shape[1], LANES)]:
                total = self.buf[rows, lanes].astype(F32)
                for q in range(number):
                    new = pl.ds(pl.multiple_of(at + q * part + i * PART, PART), PART)
                    total = total + self.recv[new, lanes].astype(F32)
                target[rows, lanes] = total.astype(BF16)
            return carry

        lax.fori_loop(0, part // PART, body, 0)

    def double(self, sem, k, off, size, at):
        copy = self.copy(sem, self.rows(self.out, off, size), self.recv.at[at : at + size], self.place.device(1 << k))
        copy.start()
        return copy

    def add_double(self, off, size, at):
        rows = pl.ds(pl.multiple_of(off, PART), size)
        self.out[rows] = (self.out[rows].astype(F32) + self.recv[at : at + size].astype(F32)).astype(BF16)

    def gather(self, sem, masks, own, part):
        rows = self.rows(self.out, own, part)
        for mask in masks:
            self.copy(sem, rows, rows, self.place.device(mask)).start()
        return self.all_of(sem, masks, part)

    def advance(self, now):
        if self.pending is not None:
            self.pending.wait()
            if self.after is not None:
                self.after()
            self.pending = None
        if self.steps:
            start, self.after, time = self.steps.pop(0)
            self.pending = start()
            self.due = now + time

    def over(self):
        return self.pending is None and not self.steps


def local_kernel(
    sizes,
    lengths_ref,
    pads_ref,
    spans_ref,
    enc_ref,
    w_in_ref,
    w_rec_ref,
    w_bias_ref,
    w_proj_ref,
    proj_bias_ref,
    gain_ref,
    shift_ref,
    mask_in_ref,
    mask_bias_in_ref,
    dec_in_ref,
    wave_grad_ref,
    wave_out,
    spans_out,
    sums_out,
    stream,
    valid,
    mx,
    xj,
    dz,
    dmj,
    normed,
    inv_all,
    u_a,
    u_e,
    hc_a,
    hc_e,
    sv_a,
    sv_e,
    gd,
    dh,
    dp,
    wcat,
    wit,
    wrt,
    pws,
    vec,
    enc_t,
    pre,
    masked,
    feats,
    dpre,
    mask_ref,
    dec_ref,
    send,
    own,
    got,
    wave_got,
    sems,
    sums,
    recv,
    small,
    sum_sems,
    all_sums,
    grad_spans,
    out_sems,
):
    R, K, C, H, clips, blocks, kp, num_dp = sizes
    rows, rows_e = R * K, R * kp
    hop = K // 2
    frames = R * hop
    half = dec_in_ref.shape[0] // 2
    wr = frames * half // LANES
    group = LANES // half
    cr = rows
    speaker = lax.axis_index("spk")
    partner = {"spk": 1 - speaker}

    barrier = pltpu.get_barrier_semaphore()
    place = Place(num_dp)
    everyone = place.masks(range(1, min(place.bits, 5))) + [1 << k for k in [0, *range(5, place.bits)]]
    for mask in everyone:
        pl.semaphore_signal(barrier, inc=1, device_id=place.device(mask), device_id_type=MESH)

    mask_row = -(-wr // 8) * 8
    for i in range(wr):
        at = pl.multiple_of(speaker * (wr * LANES) + i * LANES, LANES)
        own[i : i + 1] = wave_grad_ref[0:1, pl.ds(at, LANES)].astype(F32)
        at = pl.multiple_of((1 - speaker) * (wr * LANES) + i * LANES, LANES)
        send[i : i + 1] = wave_grad_ref[0:1, pl.ds(at, LANES)].astype(F32)
    mask_f = mask_in_ref[0].astype(F32)
    send[wr:mask_row] = jnp.zeros((mask_row - wr, LANES), F32)
    send[mask_row : mask_row + C] = jnp.concatenate([mask_f, mask_f], axis=1)
    bias_f = mask_bias_in_ref[0:1].astype(F32)
    bias_f = jnp.concatenate([bias_f, bias_f], axis=1)
    send[mask_row + C : mask_row + C + 8] = jnp.broadcast_to(bias_f, (8, LANES))

    jio = lax.broadcasted_iota(jnp.int32, (R, LANES), 0)
    lane = lax.broadcasted_iota(jnp.int32, (1, LANES), 1)
    ones_lanes = jnp.logical_and(lane >= C, lane < C + 3)

    lens = [lengths_ref[0, speaker, c] for c in range(clips)]
    pads = [pads_ref[0, speaker, c] for c in range(clips)]
    starts, ends, at = [], [], 0
    for c in range(clips):
        starts.append(at)
        at = at + lens[c]
        ends.append(at)

    def is_start(j):
        hit = j == starts[0]
        for c in range(1, clips):
            hit = jnp.logical_or(hit, j == starts[c])
        return hit

    def is_end(j):
        hit = j == ends[0] - 1
        for c in range(1, clips):
            hit = jnp.logical_or(hit, j == ends[c] - 1)
        return hit

    members, thr, inv_count = [], jnp.full((R, LANES), K, jnp.int32), jnp.zeros((R, LANES), F32)
    for c in range(clips):
        member = jnp.logical_and(jio >= starts[c], jio < ends[c]).astype(F32)
        members.append(member)
        thr = jnp.where(jio == ends[c] - 1, K - pads[c], thr)
        count = (C * (K * lens[c] - pads[c])).astype(F32)
        inv_count = inv_count + member / jnp.full((R, LANES), count, F32)
    not_first = 1.0 - is_start(jio).astype(F32)
    next_not_first = 1.0 - jnp.logical_or(is_start(jio + 1), jio == R - 1).astype(F32)

    def clip_sum(x):
        out = jnp.zeros((R, 1), F32)
        for member in members:
            out = out + member[:, :1] * jnp.sum(member * x, axis=(0, 1), keepdims=True)
        return out

    def fill_valid(r):
        k = lax.broadcasted_iota(jnp.int32, (cr // R, R, LANES), 0) + r // R
        low = lax.broadcasted_iota(jnp.int32, (cr // R, R, LANES), 2) < C
        ok = jnp.logical_and(k < thr[None], low).astype(F32)
        valid[pl.ds(r, cr)] = ok.reshape(cr, LANES)

    chunks(rows, cr, fill_valid)

    near, far = list(range(1, min(place.bits, 3))), list(range(3, min(place.bits, 5)))
    outer = range(5, place.bits)
    times = {1: 1.7, 2: 4.2, 4: 6.8}

    def reduction(n, stages):
        reduce = Reduction(sums.at[n], recv.at[n], all_sums.at[n], sum_sems.at[n], place, stages, outer, times)
        reduce.number = n
        return reduce

    lay = sum_rows(C, H)
    active = []
    clock = [0.0]

    def point(passed):
        clock[0] += passed
        for reduce in active:
            if not reduce.over() and reduce.due <= clock[0]:
                reduce.advance(clock[0])

    for n in range(2 * blocks):
        for at in (lay["proj"], lay["head"]):
            sums[n, at : at + PAIR] = jnp.zeros((PAIR, 4 * H), BF16)

    pws[...] = jnp.zeros_like(pws)
    wit[...] = jnp.zeros_like(wit)
    vec[...] = jnp.zeros_like(vec)
    for b in range(blocks):
        for s in range(2):
            n = 2 * b + s
            pws[b, s, 0:C] = w_proj_ref[b, s]
            vec[n, 0:1, 0:C] = proj_bias_ref[b, s : s + 1]
            vec[n, 1:2, 0:C] = gain_ref[b, s : s + 1]
            vec[n, 2:3, 0:C] = shift_ref[b, s : s + 1]

    stream[...] = jnp.zeros_like(stream)
    for j in range(R):
        x = spans_ref[j].astype(F32)
        x = jnp.concatenate([x, jnp.zeros_like(x)], axis=0).T
        stream[pl.ds(j, K, stride=R), :] = x

    def start_stream(r):
        x = stream[pl.ds(r, cr)] * valid[pl.ds(r, cr)]
        stream[pl.ds(r, cr)] = jnp.where(ones_lanes, 1.0, x)

    chunks(rows, cr, start_stream)

    gate_scale = jnp.where(
        lax.broadcasted_iota(jnp.int32, (1, 4 * H), 1) // H == 2, 1.0, 0.5
    ).astype(F32)

    def lane_part(x, g):
        return x[:, g * H : (g + 1) * H]

    def gate_step(d, sv, b, r, n, p, c, keep_next):
        acts = [jnp.tanh(p[:, g * H : (g + 1) * H]) for g in range(4)]
        ti, tf, g, to = acts
        i, f, o = 0.5 * ti + 0.5, 0.5 * tf + 0.5, 0.5 * to + 0.5
        cn = f * c + i * g
        tc = jnp.tanh(cn)
        h = o * tc
        parts = [
            g * (0.25 - 0.25 * ti * ti),
            c * (0.25 - 0.25 * tf * tf),
            i * (1.0 - g * g),
            tc * (0.25 - 0.25 * to * to),
            o * (1.0 - tc * tc),
            f,
        ]
        for m, part in enumerate(parts):
            sv[b, d, pl.ds(r, n), m * H : (m + 1) * H] = part.astype(BF16)
        if keep_next is None:
            return h.astype(BF16), h.astype(BF16), cn
        return h.astype(BF16), (h * keep_next).astype(BF16), cn * keep_next

    def run_forward(b, sec, u, hc, sv, n, steps, unroll):
        total = n * steps
        for d in range(2):
            wcat[d, 0:H] = (w_rec_ref[b, sec, d].astype(F32) * gate_scale).astype(BF16)
            wcat[d, H : H + C] = (w_in_ref[b, sec, d].astype(F32) * gate_scale).astype(BF16)
            bias = w_bias_ref[b, sec, d : d + 1] * gate_scale
            terms = []
            for _ in range(3):
                terms.append(bias.astype(BF16).astype(F32))
                bias = bias - terms[-1]
            row = lax.broadcasted_iota(jnp.int32, (H - C, 4 * H), 0)
            block = jnp.zeros((H - C, 4 * H), F32)
            for m, term in enumerate(terms):
                block = jnp.where(row == m, jnp.broadcast_to(term, block.shape), block)
            wcat[d, H + C : 2 * H] = block.astype(BF16)

        def step(t, carry):
            hf, hb, cf, cb = carry
            back = steps - 1 - t
            rf, rb = t * n, back * n
            if sec == 0:
                rf, rb = pl.multiple_of(rf, n), pl.multiple_of(rb, n)
            kf = kb = None
            if sec == 1:
                kf = 1.0 - is_start(t + 1).astype(F32)
                kb = 1.0 - is_end(back - 1).astype(F32)
            if sec == 1 and t < steps // 2:
                uf = stream[pl.ds(t, n, stride=R), :].astype(BF16)
                ub = stream[pl.ds(back, n, stride=R), :].astype(BF16)
                u[b, rf : rf + n] = uf
                u[b, rb : rb + n] = ub
            else:
                uf, ub = u[b, pl.ds(rf, n)], u[b, pl.ds(rb, n)]
            pf = dot(jnp.concatenate([hf, uf], axis=1), wcat[0])
            pb = dot(jnp.concatenate([hb, ub], axis=1), wcat[1])
            out_f, hf, cf = gate_step(0, sv, b, rf, n, pf, cf, kf)
            out_b, hb, cb = gate_step(1, sv, b, rb, n, pb, cb, kb)
            hc[b, pl.ds(rf, n), 0:H] = out_f
            hc[b, pl.ds(rb, n), H : 2 * H] = out_b
            return hf, hb, cf, cb

        zh, zc = jnp.zeros((n, H), BF16), jnp.zeros((n, H), F32)
        carry = (zh, zh, zc, zc)
        if sec == 1:
            for t in range(steps):
                carry = step(t, carry)
        else:
            lax.fori_loop(0, steps, step, carry, unroll=unroll)

    def norm_forward(b, sec):
        n = 2 * b + sec
        gain, shift = vec[n, 1:2], vec[n, 2:3]

        def fold(body):
            def step(i, acc):
                return acc + jnp.sum(body(pl.multiple_of(i * cr, cr)).reshape(cr // R, R, LANES), axis=0)

            return lax.fori_loop(0, rows // cr, step, jnp.zeros((R, LANES), F32))

        mean = clip_sum(fold(lambda r: valid[pl.ds(r, cr)] * mx[pl.ds(r, cr)])) * inv_count

        def spread(r):
            x = mx[pl.ds(r, cr)].reshape(cr // R, R, LANES) - mean[None]
            return valid[pl.ds(r, cr)] * (x * x).reshape(cr, LANES)

        inv = lax.rsqrt(clip_sum(fold(spread)) * inv_count + 1e-08)
        inv_all[n] = inv

        def apply(r):
            x = (mx[pl.ds(r, cr)].reshape(cr // R, R, LANES) - mean[None]) * inv[None]
            x = x.reshape(cr, LANES)
            normed[n, pl.ds(r, cr)] = x
            stream[pl.ds(r, cr)] += valid[pl.ds(r, cr)] * (x * gain + shift)

        chunks(rows, cr, apply)

    swap = pltpu.make_async_remote_copy(
        src_ref=send, dst_ref=got, send_sem=sems.at[0], recv_sem=sems.at[1], device_id=partner, device_id_type=MESH
    )

    def forward_block(b, carry):
        def u_intra(r):
            u_a[b, pl.ds(r, cr)] = stream[pl.ds(r, cr)].astype(BF16)

        chunks(rows, cr, u_intra)
        run_forward(b, 0, u_a, hc_a, sv_a, R, K, 10)

        @pl.when(b == 0)
        def _():
            pl.semaphore_wait(barrier, len(everyone))
            swap.start()


        mx[0:rows] = dot_nt(hc_a[b], pws[b, 0]) + vec[2 * b, 0:1]
        norm_forward(b, 0)

        run_forward(b, 1, u_e, hc_e, sv_e, kp, R, R)

        xj[...] = dot_nt(hc_e[b], pws[b, 1]) + vec[2 * b + 1, 0:1]
        for k in range(K):
            mx[k * R : (k + 1) * R] = xj[pl.ds(k, R, stride=kp), :]
        norm_forward(b, 1)
        return carry

    lax.fori_loop(0, blocks, forward_block, 0)

    e = enc_ref[...].astype(F32)
    xj[0:frames] = jnp.concatenate([e, e], axis=0).T
    for j in range(R):
        enc_t[pl.ds(j, hop, stride=R), :] = xj[j * hop : (j + 1) * hop]

    first_half = lane < half
    second_half = jnp.logical_and(lane >= half, lane < 2 * half)
    d = dec_in_ref[...].astype(F32)
    d = jnp.concatenate([d, jnp.zeros((LANES - 2 * half, C), F32)], axis=0).T
    dec_ref[0:C, 0:LANES] = jnp.where(first_half, d, 0.0).astype(BF16)
    dec_ref[C : 2 * C, 0:LANES] = jnp.where(second_half, pltpu.roll(d, half, 1), 0.0).astype(BF16)
    dec_ref[0:C, LANES : 2 * LANES] = jnp.where(first_half, pltpu.roll(d, LANES - half, 1), 0.0).astype(BF16)
    dec_ref[C : 2 * C, LANES : 2 * LANES] = jnp.where(second_half, d, 0.0).astype(BF16)

    swap.wait()
    mask_ref[...] = jnp.concatenate([mask_f, got[mask_row : mask_row + C, 0:C]], axis=1).astype(BF16)
    mask_bias = jnp.concatenate(
        [mask_bias_in_ref[0:1].astype(F32), got[mask_row + C : mask_row + C + 1, 0:C]], axis=1
    )
    for q in range(group):
        a = pltpu.roll(own[0:mask_row], LANES - q * half, 1) if q else own[0:mask_row]
        b = pltpu.roll(got[0:mask_row], (LANES - (q - 1) * half) % LANES, 1) if q != 1 else got[0:mask_row]
        w = jnp.where(first_half, a, jnp.where(second_half, b, 0.0))
        xj[pl.ds(q, wr, stride=group), :] = w[0:wr]
    for j in range(R):
        gd[1, j * hop : (j + 1) * hop, 0:LANES] = xj[j * hop : (j + 1) * hop]
    for j in range(R):
        xj[pl.ds(j, hop, stride=R), :] = gd[1, j * hop : (j + 1) * hop, 0:LANES]

    def head_pre(r):
        x = stream[pl.ds(r, cr)]
        f = x * (0.5 * jnp.tanh(0.5 * x) + 0.5)
        f = jnp.where(lane == C, 1.0, f).astype(BF16)
        feats[pl.ds(r, cr)] = f
        pre[pl.ds(r, cr)] = dot(f[:, 0:C], mask_ref[...]) + mask_bias

    chunks(rows, cr, head_pre)

    hr = frames // 5

    def tile(v):
        return jnp.broadcast_to(v[None], (hr // R, R, LANES)).reshape(hr, LANES)

    for q in range(5):
        r = q * hr
        fr = pre[r : r + hr] + tile(not_first) * pre[frames + r - 1 : frames + r - 1 + hr]
        e = enc_t[r : r + hr]
        sp = jnp.maximum(fr, 0.0) + jnp.log1p(jnp.exp(-jnp.abs(fr)))
        masked[r : r + hr] = (sp * e).astype(BF16)
        pre[r : r + hr] = e * (0.5 * jnp.tanh(0.5 * fr) + 0.5)
    for q in range(5):
        r = q * hr
        gd[0, r : r + hr, 0 : 2 * LANES] = dot(masked[r : r + hr], dec_ref[...])
    gd[1, 0:R, 0:LANES] = (
        gd[0, 0:R, 0:LANES] + not_first * gd[0, frames - R - 1 : frames - 1, LANES : 2 * LANES]
    )
    gd[1, R:frames, 0:LANES] = gd[0, R:frames, 0:LANES] + gd[0, 0 : frames - R, LANES : 2 * LANES]
    xj[frames : 2 * frames] = gd[1, 0:frames, 0:LANES]
    for j in range(R):
        gd[1, j * hop : (j + 1) * hop, 0:LANES] = xj[pl.ds(frames + j, hop, stride=R), :]
    xj[frames : 2 * frames] = gd[1, 0:frames, 0:LANES]
    zero = jnp.zeros((wr, LANES), F32)
    w_own, w_far = zero, zero
    for q in range(group):
        x = xj[pl.ds(frames + q, wr, stride=group), :]
        a = jnp.where(first_half, x, 0.0)
        b = jnp.where(second_half, x, 0.0)
        w_own = w_own + (pltpu.roll(a, q * half, 1) if q else a)
        w_far = w_far + (pltpu.roll(b, (q - 1) * half % LANES, 1) if q != 1 else b)
    own[0:wr] = w_own
    send[0:wr] = w_far
    wave_swap = pltpu.make_async_remote_copy(
        src_ref=send.at[0:mask_row],
        dst_ref=wave_got,
        send_sem=sems.at[2],
        recv_sem=sems.at[3],
        device_id=partner,
        device_id_type=MESH,
    )
    wave_swap.start()

    gd[0, 0:frames, 0:LANES] = xj[0:frames]
    gd[0, 0 : frames - R, LANES : 2 * LANES] = xj[R:frames]
    gd[0, frames - R : frames, LANES : 2 * LANES] = next_not_first * xj[1 : R + 1]
    dp[0:frames, 0 : 2 * LANES] = gd[0, 0:frames, 0 : 2 * LANES].astype(BF16)
    g = dot_tn(masked[...], dp[0:frames, 0 : 2 * LANES])
    g_lead = g[0:C, 0:LANES] + pltpu.roll(g[C : 2 * C, 0:LANES], LANES - half, 1)
    g_tail = pltpu.roll(g[0:C, LANES : 2 * LANES], half, 1) + g[C : 2 * C, LANES : 2 * LANES]
    g = jnp.where(first_half, g_lead, g_tail)
    g_dec = jnp.concatenate([g, jnp.zeros_like(g)], axis=0).T[0 : 2 * half]
    xj[frames : frames + 8] = jnp.zeros((8, LANES), F32)
    for q in range(5):
        r = q * hr
        dfr = dot_nt(dp[r : r + hr, 0 : 2 * LANES], dec_ref[...]) * pre[r : r + hr]
        xj[r : r + hr] = dfr
        dpre[r : r + hr] = dfr.astype(BF16)
    for q in range(5):
        r = q * hr
        dpre[frames + r : frames + r + hr] = (tile(next_not_first) * xj[r + 1 : r + 1 + hr]).astype(BF16)
    gm = dot_tn(feats[...], dpre[...])
    gm = jnp.where(speaker == 0, gm, pltpu.roll(gm, C, 1))
    n, at = 2 * blocks - 1, lay["head"]
    for q in range(4):
        sums[n, at : at + 16, q * LANES : (q + 1) * LANES] = gm[16 * q : 16 * q + 16].astype(BF16)
    sums[n, at + 16 : at + 32, 0:LANES] = jnp.where(lane < C, g_dec, 0.0).astype(BF16)
    sums[n, at + 16 : at + 32, LANES : 2 * LANES] = jnp.broadcast_to(gm[C : C + 1], (16, LANES)).astype(BF16)
    dz[...] = jnp.zeros_like(dz)

    def head_dz(r):
        x = stream[pl.ds(r, cr)]
        sg = 0.5 * jnp.tanh(0.5 * x) + 0.5
        df = dot_nt(dpre[pl.ds(r, cr)], mask_ref[...])
        df = jnp.concatenate([df, jnp.zeros_like(df)], axis=1)
        dz[pl.ds(r, cr)] = df * sg * (1.0 + x * (1.0 - sg))

    chunks(rows, cr, head_dz)

    def norm_backward(b, sec):
        n = 2 * b + sec
        gain = vec[n, 1:2]

        def sums(i, acc):
            r = pl.multiple_of(i * cr, cr)
            v = valid[pl.ds(r, cr)] * dz[pl.ds(r, cr)]
            w = v * normed[n, pl.ds(r, cr)]
            return (
                acc[0] + jnp.sum(v.reshape(cr // R, R, LANES), axis=0),
                acc[1] + jnp.sum(w.reshape(cr // R, R, LANES), axis=0),
            )

        zero = jnp.zeros((R, LANES), F32)
        s1, s2 = lax.fori_loop(0, rows // cr, sums, (zero, zero))
        small[1:2, LANES : 2 * LANES] = jnp.sum(s2, axis=0, keepdims=True)
        small[1:2, 2 * LANES : 3 * LANES] = jnp.sum(s1, axis=0, keepdims=True)
        m1 = clip_sum(s1 * gain) * inv_count
        m2 = clip_sum(s2 * gain) * inv_count
        inv = inv_all[n]

        def apply(i, acc):
            r = pl.multiple_of(i * cr, cr)
            d = (dz[pl.ds(r, cr)] * gain).reshape(cr // R, R, LANES)
            x = normed[n, pl.ds(r, cr)].reshape(cr // R, R, LANES)
            y = (d - m1[None] - x * m2[None]) * inv[None]
            y = (y.reshape(cr, LANES) * valid[pl.ds(r, cr)]).astype(BF16)
            if sec == 0:
                dmj[pl.ds(r, cr)] = y
            y = y.astype(F32)
            if sec == 1:
                mx[pl.ds(r, cr)] = y
            return acc + jnp.sum(y.reshape(cr // R, R, LANES), axis=0)

        acc = lax.fori_loop(0, rows // cr, apply, zero)
        small[1:2, 0:LANES] = jnp.sum(acc, axis=0, keepdims=True)

    def back_step(d, sv, b, r, n, dhn, dcn, keep):
        a = [sv[b, d, pl.ds(r, n), m * H : (m + 1) * H].astype(F32) for m in range(6)]
        g = dh[pl.ds(r, n), d * H : (d + 1) * H] + dhn
        dc = dcn + g * a[4]
        for m in range(4):
            dp[pl.ds(r, n), (4 * d + m) * H : (4 * d + m + 1) * H] = ((g if m == 3 else dc) * a[m]).astype(BF16)
        dhn = dot(dp[pl.ds(r, n), 4 * d * H : 4 * (d + 1) * H], wrt[d])
        dcn = dc * a[5]
        if keep is not None:
            dhn, dcn = dhn * keep, dcn * keep
        return dhn, dcn

    def run_backward(b, sec, u, hc, sv, n, steps, unroll, parts):
        total = n * steps
        out = sums.at[2 * b + sec]
        g = dot_tn(dmj[0:total], hc[b])[0:C].astype(BF16)
        at = lay["proj"]
        out[at : at + C // 2, 0 : 2 * H] = g[0 : C // 2]
        out[at : at + C // 2, 2 * H : 4 * H] = g[C // 2 : C]

        dh[0:total] = dot(dmj[0:total], pws[b, sec])
        for d in range(2):
            wrt[d] = w_rec_ref[b, sec, d].T
            wit[d * 4 * H : (d + 1) * 4 * H, 0:C] = w_in_ref[b, sec, d].T

        def step(t, carry):
            hf, hb, cf, cb = carry
            back = steps - 1 - t
            rf = pl.multiple_of(back * n, n)
            rb = pl.multiple_of(t * n, n)
            kf = kb = None
            if sec == 1:
                kf = 1.0 - is_start(back).astype(F32)
                kb = 1.0 - is_end(t).astype(F32)
            hf, cf = back_step(0, sv, b, rf, n, hf, cf, kf)
            hb, cb = back_step(1, sv, b, rb, n, hb, cb, kb)
            return hf, hb, cf, cb

        z = jnp.zeros((n, H), F32)
        carry = (z, z, z, z)
        point(2.5)
        for p in range(parts):
            carry = lax.fori_loop(p * steps // parts, (p + 1) * steps // parts, step, carry, unroll=unroll)
            point(steps * 0.125 / parts)
        if sec == 1:
            for j in range(1, steps):
                kf = (1.0 - is_start(j).astype(F32)).astype(BF16)
                at = slice((j - 1) * n, j * n)
                hc[b, at, 0:H] = hc[b, at, 0:H] * kf
                kb = (1.0 - is_end(j - 1).astype(F32)).astype(BF16)
                at = slice(j * n, (j + 1) * n)
                hc[b, at, H : 2 * H] = hc[b, at, H : 2 * H] * kb
        last = (b, sec) == (0, 0)
        core = place.bit(0)
        reduce = reduction(2 * b + sec, [[0], near + far] if b == 0 else [[0], near, far])
        for d in (1 - core, core):
            gates = pl.ds(pl.multiple_of(4 * d * H, H), 4 * H)
            g = dot_tn(u[b], dp[0:total, gates])
            base = d * lay["half"]
            out[pl.ds(pl.multiple_of(base + lay["in"], PART), C)] = g[0:C].astype(BF16)
            small[0:1] = g[C : C + 1]
            out[pl.ds(pl.multiple_of(base + lay["small"], PART), 16)] = small[...].astype(BF16)
            h_prev = hc[b, pl.ds(pl.multiple_of(d * n, n), total - n), pl.ds(pl.multiple_of(d * H, H), H)]
            g = dot_tn(h_prev, dp[pl.ds(pl.multiple_of((1 - d) * n, n), total - n), gates])
            out[pl.ds(pl.multiple_of(base + lay["rec"], PART), H)] = g.astype(BF16)
            if d is core:
                point(0.6)
            else:
                reduce.advance(clock[0] + 0.6)
                active.append(reduce)

    def stream_grad(total):
        return dot(dp[0:total], wit[...])

    small[...] = jnp.zeros_like(small)
    for b in reversed(range(blocks)):
        norm_backward(b, 1)
        mx[rows:rows_e] = jnp.zeros((rows_e - rows, LANES), F32)
        for j in range(R):
            dmj[pl.ds(j * kp, kp)] = mx[pl.ds(j, kp, stride=R), :].astype(BF16)
        run_backward(b, 1, u_e, hc_e, sv_e, kp, R, R, 1)

        xj[...] = stream_grad(rows_e)
        for k in range(K):
            dz[k * R : (k + 1) * R] += xj[pl.ds(k, R, stride=kp), :]
        point(1.5)

        norm_backward(b, 0)
        run_backward(b, 0, u_a, hc_a, sv_a, R, K, 10, 5)

        dz[0:rows] += stream_grad(rows)
        point(1.5)

    def finish(r):
        dz[pl.ds(r, cr)] = dz[pl.ds(r, cr)] * valid[pl.ds(r, cr)]

    chunks(rows, cr, finish)
    for j in range(R):
        grad_spans[j] = dz[pl.ds(j, K, stride=R), :].T[0:C]
    exits = [pltpu.make_async_copy(grad_spans, spans_out, out_sems.at[2 * blocks])]
    exits[0].start()
    wave_swap.wait()
    for i in range(wr):
        at = pl.multiple_of(speaker * (wr * LANES) + i * LANES, LANES)
        wave_out[0:1, pl.ds(at, LANES)] = own[i : i + 1]
        at = pl.multiple_of((1 - speaker) * (wr * LANES) + i * LANES, LANES)
        wave_out[0:1, pl.ds(at, LANES)] = wave_got[i : i + 1]

    left = list(active)
    while left:
        for reduce in [reduce for reduce in left if reduce.over()]:
            n = reduce.number
            exits.append(pltpu.make_async_copy(all_sums.at[n], sums_out.at[n], out_sems.at[n]))
            exits[-1].start()
            left.remove(reduce)
        if left:
            nearest = min(left, key=lambda reduce: reduce.due)
            clock[0] = max(clock[0], nearest.due)
            nearest.advance(clock[0])
    for copy in exits:
        copy.wait()


def unpack_kernel(
    sizes,
    sums,
    wave_in,
    spans_in,
    wave_out,
    spans_out,
    in_out,
    rec_out,
    bias_out,
    proj_out,
    proj_bias_out,
    gain_out,
    shift_out,
    mask_out,
    mask_bias_out,
    dec_out,
):
    C, H = sizes
    lay = sum_rows(C, H)
    n = pl.program_id(0)
    b, sec = n // 2, n % 2
    speaker = lax.axis_index("spk")
    spans_out[...] = spans_in[...]
    for d in range(2):
        base = d * lay["half"]
        in_out[d] = sums[base + lay["in"] : base + lay["in"] + C].astype(F32)
        rec_out[d] = sums[base + lay["rec"] : base + lay["rec"] + H].astype(F32)
        small = sums[base + lay["small"] : base + lay["small"] + 16].astype(F32)
        bias_out[d : d + 1] = small[0:1]
        if d == 0:
            for m, out in enumerate((proj_bias_out, gain_out, shift_out)):
                out[b, pl.ds(sec, 1)] = small[1:2, m * LANES : m * LANES + C]
    at = lay["proj"]
    proj_out[0 : C // 2] = sums[at : at + C // 2, 0 : 2 * H].astype(F32)
    proj_out[C // 2 : C] = sums[at : at + C // 2, 2 * H : 4 * H].astype(F32)

    @pl.when(n == 0)
    def _():
        wave_out[...] = wave_in[...]

    @pl.when(n == pl.num_programs(0) - 1)
    def _():
        at = lay["head"]

        def own(x):
            return jnp.where(speaker == 0, x, pltpu.roll(x, C, 1))[:, 0:C]

        for q in range(4):
            x = sums[at : at + 16, q * LANES : (q + 1) * LANES].astype(F32)
            mask_out[0, 16 * q : 16 * q + 16] = own(x)
        x = sums[at + 16 : at + 32, 0 : 2 * LANES].astype(F32)
        mask_bias_out[...] = own(x[:, LANES : 2 * LANES])[0:1]
        dec_out[...] = x[:, 0:C]


def sum_rows(C, H):
    lay, at = {}, 0
    for name, rows in (("in", C), ("rec", H), ("small", 16), ("proj", C // 2)):
        lay[name] = at
        at += rows
    lay["half"] = -(-at // (16 * PART)) * 16 * PART
    lay["head"] = lay["half"] + lay["proj"]
    lay["total"] = 2 * lay["half"]
    return lay


def shards(
    num_dp,
    spans,
    encoded,
    clip_lengths,
    clip_pads,
    lstm_in,
    lstm_rec,
    lstm_bias,
    proj_weight,
    proj_bias,
    gln_gain,
    gln_shift,
    mask_weight,
    mask_bias,
    dec_weight,
    wave_grad,
):
    R, K, C = spans.shape
    H = lstm_rec.shape[3]
    blocks = lstm_in.shape[0]
    clips = clip_lengths.shape[2]
    frames = encoded.shape[0]
    half = dec_weight.shape[1] // 2
    kp = -(-K // 16) * 16
    rows, rows_e = R * K, R * kp
    wr = frames * half // LANES
    mask_row = -(-wr // 8) * 8

    sizes = (R, K, C, H, clips, blocks, kp, num_dp)
    lay = sum_rows(C, H)
    outer = max(num_dp.bit_length() - 5, 0)
    smem = pl.BlockSpec(memory_space=pltpu.SMEM)
    vmem = pl.BlockSpec(memory_space=pltpu.VMEM)
    shape = jax.ShapeDtypeStruct
    outs = pl.pallas_call(
        functools.partial(local_kernel, sizes),
        out_shape=(
            shape((1, 2 * frames * half), F32),
            shape((R, C, K), F32),
            shape((2 * blocks, lay["total"], 4 * H), BF16),
        ),
        in_specs=[smem, smem] + [vmem] * 13,
        out_specs=(vmem, pl.BlockSpec(memory_space=pl.ANY), pl.BlockSpec(memory_space=pl.ANY)),
        scratch_shapes=[
            pltpu.VMEM((rows_e, LANES), F32),
            pltpu.VMEM((rows, LANES), F32),
            pltpu.VMEM((rows_e, LANES), F32),
            pltpu.VMEM((rows_e, LANES), F32),
            pltpu.VMEM((rows_e, LANES), F32),
            pltpu.VMEM((rows_e, LANES), BF16),
            pltpu.VMEM((2 * blocks, rows, LANES), F32),
            pltpu.VMEM((2 * blocks, R, LANES), F32),
            pltpu.VMEM((blocks, rows, LANES), BF16),
            pltpu.VMEM((blocks, rows_e, LANES), BF16),
            pltpu.VMEM((blocks, rows, 2 * H), BF16),
            pltpu.VMEM((blocks, rows_e, 2 * H), BF16),
            pltpu.VMEM((blocks, 2, rows, 6 * H), BF16),
            pltpu.VMEM((blocks, 2, rows_e, 6 * H), BF16),
            pltpu.VMEM((2, frames, 2 * LANES), F32),
            pltpu.VMEM((rows_e, 2 * H), F32),
            pltpu.VMEM((rows_e, 8 * H), BF16),
            pltpu.VMEM((2, 2 * H, 4 * H), BF16),
            pltpu.VMEM((8 * H, LANES), BF16),
            pltpu.VMEM((2, 4 * H, H), BF16),
            pltpu.VMEM((blocks, 2, LANES, 2 * H), BF16),
            pltpu.VMEM((2 * blocks, 8, LANES), F32),
            pltpu.VMEM((frames, LANES), F32),
            pltpu.VMEM((rows, LANES), F32),
            pltpu.VMEM((frames, LANES), BF16),
            pltpu.VMEM((rows, LANES), BF16),
            pltpu.VMEM((rows, LANES), BF16),
            pltpu.VMEM((C, 2 * C), BF16),
            pltpu.VMEM((2 * C, 2 * LANES), BF16),
            pltpu.VMEM((mask_row + C + 8, LANES), F32),
            pltpu.VMEM((mask_row, LANES), F32),
            pltpu.VMEM((mask_row + C + 8, LANES), F32),
            pltpu.VMEM((mask_row, LANES), F32),
            pltpu.SemaphoreType.DMA((4,)),
            pltpu.VMEM((2 * blocks, lay["total"], 4 * H), BF16),
            pltpu.VMEM((2 * blocks, lay["total"] + PART * outer, 4 * H), BF16),
            pltpu.VMEM((16, 4 * H), F32),
            pltpu.SemaphoreType.DMA((2 * blocks, 6 + outer, 2)),
            pltpu.VMEM((2 * blocks, lay["total"], 4 * H), BF16),
            pltpu.VMEM((R, C, K), F32),
            pltpu.SemaphoreType.DMA((2 * blocks + 1,)),
        ],
        compiler_params=pltpu.CompilerParams(
            vmem_limit_bytes=62 * 1024 * 1024, collective_id=0, has_side_effects=True
        ),
        name="dual_path",
    )(
        clip_lengths,
        clip_pads,
        spans.transpose(0, 2, 1),
        encoded.T,
        lstm_in,
        lstm_rec,
        lstm_bias,
        proj_weight.transpose(0, 1, 3, 2),
        proj_bias,
        gln_gain,
        gln_shift,
        mask_weight,
        mask_bias,
        dec_weight.T,
        wave_grad,
    )
    half = dec_weight.shape[1] // 2
    per_section = pl.BlockSpec((None, lay["total"], 4 * H), lambda n: (n, 0, 0))

    def whole(*dims):
        return pl.BlockSpec(dims, lambda n: (0,) * len(dims))

    def section(*dims):
        return pl.BlockSpec((None, None) + dims, lambda n: (n // 2, n % 2) + (0,) * len(dims))

    finals = pl.pallas_call(
        functools.partial(unpack_kernel, (C, H)),
        grid=(2 * blocks,),
        out_shape=(
            shape((1, 2 * frames * half), F32),
            shape((R, C, K), F32),
            shape((blocks, 2, 2, C, 4 * H), F32),
            shape((blocks, 2, 2, H, 4 * H), F32),
            shape((blocks, 2, 2, 4 * H), F32),
            shape((blocks, 2, C, 2 * H), F32),
            shape((blocks, 2, C), F32),
            shape((blocks, 2, C), F32),
            shape((blocks, 2, C), F32),
            shape((1, C, C), F32),
            shape((1, C), F32),
            shape((2 * half, C), F32),
        ),
        in_specs=[
            per_section,
            whole(1, 2 * frames * half),
            pl.BlockSpec((R // (2 * blocks), C, K), lambda n: (n, 0, 0)),
        ],
        out_specs=(
            whole(1, 2 * frames * half),
            pl.BlockSpec((R // (2 * blocks), C, K), lambda n: (n, 0, 0)),
            section(2, C, 4 * H),
            section(2, H, 4 * H),
            section(2, 4 * H),
            section(C, 2 * H),
            whole(blocks, 2, C),
            whole(blocks, 2, C),
            whole(blocks, 2, C),
            whole(1, C, C),
            whole(1, C),
            whole(2 * half, C),
        ),
        compiler_params=pltpu.CompilerParams(vmem_limit_bytes=60 * 1024 * 1024),
        name="unpack",
    )(outs[2], outs[0], outs[1])
    return (
        finals[0],
        finals[1].transpose(0, 2, 1),
        finals[2],
        finals[3],
        finals[4],
        finals[5].transpose(0, 1, 3, 2),
        finals[6],
        finals[7],
        finals[8],
        finals[9],
        finals[10],
        finals[11].T,
    )


def solution(mesh):
    return jax.shard_map(
        functools.partial(shards, mesh.shape["dp"]),
        mesh=mesh,
        in_specs=(
            P(("dp", "spk"), None, None),
            P(("dp", "spk"), None),
            P("dp", None, None),
            P("dp", None, None),
            P(),
            P(),
            P(),
            P(),
            P(),
            P(),
            P(),
            P("spk", None, None),
            P("spk", None),
            P(),
            P("spk", "dp"),
        ),
        out_specs=(
            P("spk", "dp"),
            P(("dp", "spk"), None, None),
            P(),
            P(),
            P(),
            P(),
            P(),
            P(),
            P(),
            P("spk", None, None),
            P("spk", None),
            P(),
        ),
        check_vma=False,
    )
```

```python
import functools

import jax
import jax.numpy as jnp
from jax import lax
from jax.experimental import pallas as pl
from jax.experimental.pallas import tpu as pltpu
from jax.sharding import PartitionSpec as P

F32 = jnp.float32
BF16 = jnp.bfloat16
LANES = 128
PART = 16
PAIR = 2 * PART
MESH = pl.DeviceIdType.MESH


def dot(a, b):
    return jnp.dot(a, b, preferred_element_type=F32)


def dot_tn(a, b):
    return lax.dot_general(a, b, (((0,), (0,)), ((), ())), preferred_element_type=F32)


def dot_nt(a, b):
    return lax.dot_general(a, b, (((1,), (1,)), ((), ())), preferred_element_type=F32)


def chunks(total, size, body):
    assert total % size == 0

    def step(i, carry):
        body(pl.multiple_of(i * size, size))
        return carry

    lax.fori_loop(0, total // size, step, 0)


class Place:
    def __init__(self, num_dp):
        self.dp, self.spk = lax.axis_index("dp"), lax.axis_index("spk")
        self.bits = num_dp.bit_length()

    def bit(self, k):
        if k == 1:
            return self.spk
        return self.dp // (1 << max(k - 1, 0)) % 2

    def device(self, mask):
        dp, spk = self.dp, self.spk
        for k in range(self.bits):
            if mask >> k & 1:
                if k == 1:
                    spk = 1 - spk
                else:
                    dp = dp + (1 - 2 * self.bit(k)) * (1 << max(k - 1, 0))
        return {"dp": dp, "spk": spk}

    def index(self, bits, mask=0):
        number = 0
        for i, k in enumerate(bits):
            one = 1 - self.bit(k) if mask >> k & 1 else self.bit(k)
            number = number + one * (1 << i)
        return number

    def masks(self, bits):
        found = []
        for m in range((1 << len(bits)) - 1, 0, -1):
            found.append(sum((m >> i & 1) << k for i, k in enumerate(bits)))
        return found


class Reduction:
    def __init__(self, buf, recv, out, sems, place, stages, outer, times):
        self.buf, self.recv, self.out, self.sems, self.place = buf, recv, out, sems, place
        self.steps, back = [], []
        off, size, at, sem = 0, buf.shape[0], 0, 0
        for i, bits in enumerate(stages):
            masks = place.masks(bits)
            part = size // (len(masks) + 1)
            own = off + place.index(bits) * part
            last = i == len(stages) - 1
            self.steps.append(
                (
                    functools.partial(self.scatter, sem, masks, bits, off, part, at),
                    functools.partial(self.add, len(masks), own, part, at, out if last else buf),
                    times[len(bits)],
                )
            )
            back.append((masks, own, part, times[len(bits)]))
            off, size = own, part
            at += len(masks) * part
            sem += 1
        for k in outer:
            self.steps.append(
                (
                    functools.partial(self.double, sem, k, off, size, at),
                    functools.partial(self.add_double, off, size, at),
                    times[1],
                )
            )
            at += size
            sem += 1
        for masks, own, part, time in reversed(back):
            self.steps.append((functools.partial(self.gather, sem, masks, own, part), None, time))
            sem += 1
        self.pending, self.after, self.due = None, None, 0.0

    def copy(self, sem, src, dst, device):
        return pltpu.make_async_remote_copy(
            src_ref=src,
            dst_ref=dst,
            send_sem=self.sems.at[sem, 0],
            recv_sem=self.sems.at[sem, 1],
            device_id=device,
            device_id_type=MESH,
        )

    def rows(self, ref, off, size):
        return ref.at[pl.ds(pl.multiple_of(off, PART), size)]

    def all_of(self, sem, masks, part):
        rows = self.recv.at[0 : len(masks) * part]
        return self.copy(sem, rows, rows, self.place.device(masks[0]))

    def scatter(self, sem, masks, bits, off, part, at):
        for i, mask in enumerate(masks):
            src = self.rows(self.buf, off + self.place.index(bits, mask) * part, part)
            dst = self.recv.at[at + i * part : at + (i + 1) * part]
            self.copy(sem, src, dst, self.place.device(mask)).start()
        return self.all_of(sem, masks, part)

    def add(self, number, own, part, at, target):
        def body(i, carry):
            rows = pl.ds(pl.multiple_of(own + i * PART, PART), PART)
            for lanes in [slice(x, x + LANES) for x in range(0, self.buf.shape[1], LANES)]:
                total = self.buf[rows, lanes].astype(F32)
                for q in range(number):
                    new = pl.ds(pl.multiple_of(at + q * part + i * PART, PART), PART)
                    total = total + self.recv[new, lanes].astype(F32)
                target[rows, lanes] = total.astype(BF16)
            return carry

        lax.fori_loop(0, part // PART, body, 0)

    def double(self, sem, k, off, size, at):
        copy = self.copy(sem, self.rows(self.out, off, size), self.recv.at[at : at + size], self.place.device(1 << k))
        copy.start()
        return copy

    def add_double(self, off, size, at):
        rows = pl.ds(pl.multiple_of(off, PART), size)
        self.out[rows] = (self.out[rows].astype(F32) + self.recv[at : at + size].astype(F32)).astype(BF16)

    def gather(self, sem, masks, own, part):
        rows = self.rows(self.out, own, part)
        for mask in masks:
            self.copy(sem, rows, rows, self.place.device(mask)).start()
        return self.all_of(sem, masks, part)

    def advance(self, now):
        if self.pending is not None:
            self.pending.wait()
            if self.after is not None:
                self.after()
            self.pending = None
        if self.steps:
            start, self.after, time = self.steps.pop(0)
            self.pending = start()
            self.due = now + time

    def over(self):
        return self.pending is None and not self.steps


def local_kernel(
    sizes,
    lengths_ref,
    pads_ref,
    spans_ref,
    enc_ref,
    w_in_ref,
    w_rec_ref,
    w_bias_ref,
    w_proj_ref,
    proj_bias_ref,
    gain_ref,
    shift_ref,
    mask_in_ref,
    mask_bias_in_ref,
    dec_in_ref,
    wave_grad_ref,
    wave_out,
    spans_out,
    sums_out,
    stream,
    valid,
    mx,
    xj,
    dz,
    dmj,
    normed,
    inv_all,
    u_a,
    u_e,
    hc_a,
    hc_e,
    sv_a,
    sv_e,
    gd,
    dh,
    dp,
    wcat,
    wit,
    wrt,
    pws,
    vec,
    enc_t,
    pre,
    masked,
    feats,
    dpre,
    mask_ref,
    dec_ref,
    send,
    own,
    got,
    wave_got,
    sems,
    sums,
    recv,
    small,
    sum_sems,
    all_sums,
    grad_spans,
    out_sems,
):
    R, K, C, H, clips, blocks, kp, num_dp = sizes
    rows, rows_e = R * K, R * kp
    hop = K // 2
    frames = R * hop
    half = dec_in_ref.shape[0] // 2
    wr = frames * half // LANES
    group = LANES // half
    cr = rows
    speaker = lax.axis_index("spk")
    partner = {"spk": 1 - speaker}

    barrier = pltpu.get_barrier_semaphore()
    place = Place(num_dp)
    everyone = place.masks(range(1, min(place.bits, 5))) + [1 << k for k in [0, *range(5, place.bits)]]
    for mask in everyone:
        pl.semaphore_signal(barrier, inc=1, device_id=place.device(mask), device_id_type=MESH)

    mask_row = -(-wr // 8) * 8
    for i in range(wr):
        at = pl.multiple_of(speaker * (wr * LANES) + i * LANES, LANES)
        own[i : i + 1] = wave_grad_ref[0:1, pl.ds(at, LANES)].astype(F32)
        at = pl.multiple_of((1 - speaker) * (wr * LANES) + i * LANES, LANES)
        send[i : i + 1] = wave_grad_ref[0:1, pl.ds(at, LANES)].astype(F32)
    mask_f = mask_in_ref[0].astype(F32)
    send[wr:mask_row] = jnp.zeros((mask_row - wr, LANES), F32)
    send[mask_row : mask_row + C] = jnp.concatenate([mask_f, mask_f], axis=1)
    bias_f = mask_bias_in_ref[0:1].astype(F32)
    bias_f = jnp.concatenate([bias_f, bias_f], axis=1)
    send[mask_row + C : mask_row + C + 8] = jnp.broadcast_to(bias_f, (8, LANES))

    jio = lax.broadcasted_iota(jnp.int32, (R, LANES), 0)
    lane = lax.broadcasted_iota(jnp.int32, (1, LANES), 1)
    ones_lanes = jnp.logical_and(lane >= C, lane < C + 3)

    lens = [lengths_ref[0, speaker, c] for c in range(clips)]
    pads = [pads_ref[0, speaker, c] for c in range(clips)]
    starts, ends, at = [], [], 0
    for c in range(clips):
        starts.append(at)
        at = at + lens[c]
        ends.append(at)

    def is_start(j):
        hit = j == starts[0]
        for c in range(1, clips):
            hit = jnp.logical_or(hit, j == starts[c])
        return hit

    def is_end(j):
        hit = j == ends[0] - 1
        for c in range(1, clips):
            hit = jnp.logical_or(hit, j == ends[c] - 1)
        return hit

    members, thr, inv_count = [], jnp.full((R, LANES), K, jnp.int32), jnp.zeros((R, LANES), F32)
    for c in range(clips):
        member = jnp.logical_and(jio >= starts[c], jio < ends[c]).astype(F32)
        members.append(member)
        thr = jnp.where(jio == ends[c] - 1, K - pads[c], thr)
        count = (C * (K * lens[c] - pads[c])).astype(F32)
        inv_count = inv_count + member / jnp.full((R, LANES), count, F32)
    not_first = 1.0 - is_start(jio).astype(F32)
    next_not_first = 1.0 - jnp.logical_or(is_start(jio + 1), jio == R - 1).astype(F32)

    def clip_sum(x):
        out = jnp.zeros((R, 1), F32)
        for member in members:
            out = out + member[:, :1] * jnp.sum(member * x, axis=(0, 1), keepdims=True)
        return out

    def fill_valid(r):
        k = lax.broadcasted_iota(jnp.int32, (cr // R, R, LANES), 0) + r // R
        low = lax.broadcasted_iota(jnp.int32, (cr // R, R, LANES), 2) < C
        ok = jnp.logical_and(k < thr[None], low).astype(F32)
        valid[pl.ds(r, cr)] = ok.reshape(cr, LANES)

    chunks(rows, cr, fill_valid)

    near, far = list(range(1, min(place.bits, 3))), list(range(3, min(place.bits, 5)))
    outer = range(5, place.bits)
    times = {1: 2.2, 2: 5.0, 4: 8.0}

    def reduction(n, stages):
        reduce = Reduction(sums.at[n], recv.at[n], all_sums.at[n], sum_sems.at[n], place, stages, outer, times)
        reduce.number = n
        return reduce

    lay = sum_rows(C, H)
    active = []
    clock = [0.0]

    def point(passed):
        clock[0] += passed
        for reduce in active:
            if not reduce.over() and reduce.due <= clock[0]:
                reduce.advance(clock[0])

    for n in range(2 * blocks):
        for at in (lay["proj"], lay["head"]):
            sums[n, at : at + PAIR] = jnp.zeros((PAIR, 4 * H), BF16)

    pws[...] = jnp.zeros_like(pws)
    wit[...] = jnp.zeros_like(wit)
    vec[...] = jnp.zeros_like(vec)
    for b in range(blocks):
        for s in range(2):
            n = 2 * b + s
            pws[b, s, 0:C] = w_proj_ref[b, s]
            vec[n, 0:1, 0:C] = proj_bias_ref[b, s : s + 1]
            vec[n, 1:2, 0:C] = gain_ref[b, s : s + 1]
            vec[n, 2:3, 0:C] = shift_ref[b, s : s + 1]

    stream[...] = jnp.zeros_like(stream)
    for j in range(R):
        x = spans_ref[j].astype(F32)
        x = jnp.concatenate([x, jnp.zeros_like(x)], axis=0).T
        stream[pl.ds(j, K, stride=R), :] = x

    def start_stream(r):
        x = stream[pl.ds(r, cr)] * valid[pl.ds(r, cr)]
        stream[pl.ds(r, cr)] = jnp.where(ones_lanes, 1.0, x)

    chunks(rows, cr, start_stream)

    gate_scale = jnp.where(
        lax.broadcasted_iota(jnp.int32, (1, 4 * H), 1) // H == 2, 1.0, 0.5
    ).astype(F32)

    def lane_part(x, g):
        return x[:, g * H : (g + 1) * H]

    def gate_step(d, sv, b, r, n, p, c, keep_next):
        acts = [jnp.tanh(p[:, g * H : (g + 1) * H]) for g in range(4)]
        ti, tf, g, to = acts
        i, f, o = 0.5 * ti + 0.5, 0.5 * tf + 0.5, 0.5 * to + 0.5
        cn = f * c + i * g
        tc = jnp.tanh(cn)
        h = o * tc
        parts = [
            g * (0.25 - 0.25 * ti * ti),
            c * (0.25 - 0.25 * tf * tf),
            i * (1.0 - g * g),
            tc * (0.25 - 0.25 * to * to),
            o * (1.0 - tc * tc),
            f,
        ]
        for m, part in enumerate(parts):
            sv[b, d, pl.ds(r, n), m * H : (m + 1) * H] = part.astype(BF16)
        if keep_next is None:
            return h.astype(BF16), h.astype(BF16), cn
        return h.astype(BF16), (h * keep_next).astype(BF16), cn * keep_next

    def run_forward(b, sec, u, hc, sv, n, steps, unroll):
        total = n * steps
        for d in range(2):
            wcat[d, 0:H] = (w_rec_ref[b, sec, d].astype(F32) * gate_scale).astype(BF16)
            wcat[d, H : H + C] = (w_in_ref[b, sec, d].astype(F32) * gate_scale).astype(BF16)
            bias = w_bias_ref[b, sec, d : d + 1] * gate_scale
            terms = []
            for _ in range(3):
                terms.append(bias.astype(BF16).astype(F32))
                bias = bias - terms[-1]
            row = lax.broadcasted_iota(jnp.int32, (H - C, 4 * H), 0)
            block = jnp.zeros((H - C, 4 * H), F32)
            for m, term in enumerate(terms):
                block = jnp.where(row == m, jnp.broadcast_to(term, block.shape), block)
            wcat[d, H + C : 2 * H] = block.astype(BF16)

        def step(t, carry):
            hf, hb, cf, cb = carry
            back = steps - 1 - t
            rf, rb = t * n, back * n
            if sec == 0:
                rf, rb = pl.multiple_of(rf, n), pl.multiple_of(rb, n)
            kf = kb = None
            if sec == 1:
                kf = 1.0 - is_start(t + 1).astype(F32)
                kb = 1.0 - is_end(back - 1).astype(F32)
            if sec == 1 and t < steps // 2:
                uf = stream[pl.ds(t, n, stride=R), :].astype(BF16)
                ub = stream[pl.ds(back, n, stride=R), :].astype(BF16)
                u[b, rf : rf + n] = uf
                u[b, rb : rb + n] = ub
            else:
                uf, ub = u[b, pl.ds(rf, n)], u[b, pl.ds(rb, n)]
            pf = dot(jnp.concatenate([hf, uf], axis=1), wcat[0])
            pb = dot(jnp.concatenate([hb, ub], axis=1), wcat[1])
            out_f, hf, cf = gate_step(0, sv, b, rf, n, pf, cf, kf)
            out_b, hb, cb = gate_step(1, sv, b, rb, n, pb, cb, kb)
            hc[b, pl.ds(rf, n), 0:H] = out_f
            hc[b, pl.ds(rb, n), H : 2 * H] = out_b
            return hf, hb, cf, cb

        zh, zc = jnp.zeros((n, H), BF16), jnp.zeros((n, H), F32)
        carry = (zh, zh, zc, zc)
        if sec == 1:
            for t in range(steps):
                carry = step(t, carry)
        else:
            lax.fori_loop(0, steps, step, carry, unroll=unroll)

    def norm_forward(b, sec):
        n = 2 * b + sec
        gain, shift = vec[n, 1:2], vec[n, 2:3]

        def fold(body):
            def step(i, acc):
                return acc + jnp.sum(body(pl.multiple_of(i * cr, cr)).reshape(cr // R, R, LANES), axis=0)

            return lax.fori_loop(0, rows // cr, step, jnp.zeros((R, LANES), F32))

        mean = clip_sum(fold(lambda r: valid[pl.ds(r, cr)] * mx[pl.ds(r, cr)])) * inv_count

        def spread(r):
            x = mx[pl.ds(r, cr)].reshape(cr // R, R, LANES) - mean[None]
            return valid[pl.ds(r, cr)] * (x * x).reshape(cr, LANES)

        inv = lax.rsqrt(clip_sum(fold(spread)) * inv_count + 1e-08)
        inv_all[n] = inv

        def apply(r):
            x = (mx[pl.ds(r, cr)].reshape(cr // R, R, LANES) - mean[None]) * inv[None]
            x = x.reshape(cr, LANES)
            normed[n, pl.ds(r, cr)] = x
            stream[pl.ds(r, cr)] += valid[pl.ds(r, cr)] * (x * gain + shift)

        chunks(rows, cr, apply)

    swap = pltpu.make_async_remote_copy(
        src_ref=send, dst_ref=got, send_sem=sems.at[0], recv_sem=sems.at[1], device_id=partner, device_id_type=MESH
    )

    def forward_block(b, carry):
        def u_intra(r):
            u_a[b, pl.ds(r, cr)] = stream[pl.ds(r, cr)].astype(BF16)

        chunks(rows, cr, u_intra)
        run_forward(b, 0, u_a, hc_a, sv_a, R, K, 10)

        @pl.when(b == 0)
        def _():
            pl.semaphore_wait(barrier, len(everyone))
            swap.start()


        mx[0:rows] = dot_nt(hc_a[b], pws[b, 0]) + vec[2 * b, 0:1]
        norm_forward(b, 0)

        run_forward(b, 1, u_e, hc_e, sv_e, kp, R, R)

        xj[...] = dot_nt(hc_e[b], pws[b, 1]) + vec[2 * b + 1, 0:1]
        for k in range(K):
            mx[k * R : (k + 1) * R] = xj[pl.ds(k, R, stride=kp), :]
        norm_forward(b, 1)
        return carry

    lax.fori_loop(0, blocks, forward_block, 0)

    e = enc_ref[...].astype(F32)
    xj[0:frames] = jnp.concatenate([e, e], axis=0).T
    for j in range(R):
        enc_t[pl.ds(j, hop, stride=R), :] = xj[j * hop : (j + 1) * hop]

    first_half = lane < half
    second_half = jnp.logical_and(lane >= half, lane < 2 * half)
    d = dec_in_ref[...].astype(F32)
    d = jnp.concatenate([d, jnp.zeros((LANES - 2 * half, C), F32)], axis=0).T
    dec_ref[0:C, 0:LANES] = jnp.where(first_half, d, 0.0).astype(BF16)
    dec_ref[C : 2 * C, 0:LANES] = jnp.where(second_half, pltpu.roll(d, half, 1), 0.0).astype(BF16)
    dec_ref[0:C, LANES : 2 * LANES] = jnp.where(first_half, pltpu.roll(d, LANES - half, 1), 0.0).astype(BF16)
    dec_ref[C : 2 * C, LANES : 2 * LANES] = jnp.where(second_half, d, 0.0).astype(BF16)

    swap.wait()
    mask_ref[...] = jnp.concatenate([mask_f, got[mask_row : mask_row + C, 0:C]], axis=1).astype(BF16)
    mask_bias = jnp.concatenate(
        [mask_bias_in_ref[0:1].astype(F32), got[mask_row + C : mask_row + C + 1, 0:C]], axis=1
    )
    for q in range(group):
        a = pltpu.roll(own[0:mask_row], LANES - q * half, 1) if q else own[0:mask_row]
        b = pltpu.roll(got[0:mask_row], (LANES - (q - 1) * half) % LANES, 1) if q != 1 else got[0:mask_row]
        w = jnp.where(first_half, a, jnp.where(second_half, b, 0.0))
        xj[pl.ds(q, wr, stride=group), :] = w[0:wr]
    for j in range(R):
        gd[1, j * hop : (j + 1) * hop, 0:LANES] = xj[j * hop : (j + 1) * hop]
    for j in range(R):
        xj[pl.ds(j, hop, stride=R), :] = gd[1, j * hop : (j + 1) * hop, 0:LANES]

    def head_pre(r):
        x = stream[pl.ds(r, cr)]
        f = x * (0.5 * jnp.tanh(0.5 * x) + 0.5)
        f = jnp.where(lane == C, 1.0, f).astype(BF16)
        feats[pl.ds(r, cr)] = f
        pre[pl.ds(r, cr)] = dot(f[:, 0:C], mask_ref[...]) + mask_bias

    chunks(rows, cr, head_pre)

    hr = frames // 5

    def tile(v):
        return jnp.broadcast_to(v[None], (hr // R, R, LANES)).reshape(hr, LANES)

    for q in range(5):
        r = q * hr
        fr = pre[r : r + hr] + tile(not_first) * pre[frames + r - 1 : frames + r - 1 + hr]
        e = enc_t[r : r + hr]
        sp = jnp.maximum(fr, 0.0) + jnp.log1p(jnp.exp(-jnp.abs(fr)))
        masked[r : r + hr] = (sp * e).astype(BF16)
        pre[r : r + hr] = e * (0.5 * jnp.tanh(0.5 * fr) + 0.5)
    for q in range(5):
        r = q * hr
        gd[0, r : r + hr, 0 : 2 * LANES] = dot(masked[r : r + hr], dec_ref[...])
    gd[1, 0:R, 0:LANES] = (
        gd[0, 0:R, 0:LANES] + not_first * gd[0, frames - R - 1 : frames - 1, LANES : 2 * LANES]
    )
    gd[1, R:frames, 0:LANES] = gd[0, R:frames, 0:LANES] + gd[0, 0 : frames - R, LANES : 2 * LANES]
    xj[frames : 2 * frames] = gd[1, 0:frames, 0:LANES]
    for j in range(R):
        gd[1, j * hop : (j + 1) * hop, 0:LANES] = xj[pl.ds(frames + j, hop, stride=R), :]
    xj[frames : 2 * frames] = gd[1, 0:frames, 0:LANES]
    zero = jnp.zeros((wr, LANES), F32)
    w_own, w_far = zero, zero
    for q in range(group):
        x = xj[pl.ds(frames + q, wr, stride=group), :]
        a = jnp.where(first_half, x, 0.0)
        b = jnp.where(second_half, x, 0.0)
        w_own = w_own + (pltpu.roll(a, q * half, 1) if q else a)
        w_far = w_far + (pltpu.roll(b, (q - 1) * half % LANES, 1) if q != 1 else b)
    own[0:wr] = w_own
    send[0:wr] = w_far
    wave_swap = pltpu.make_async_remote_copy(
        src_ref=send.at[0:mask_row],
        dst_ref=wave_got,
        send_sem=sems.at[2],
        recv_sem=sems.at[3],
        device_id=partner,
        device_id_type=MESH,
    )
    wave_swap.start()

    gd[0, 0:frames, 0:LANES] = xj[0:frames]
    gd[0, 0 : frames - R, LANES : 2 * LANES] = xj[R:frames]
    gd[0, frames - R : frames, LANES : 2 * LANES] = next_not_first * xj[1 : R + 1]
    dp[0:frames, 0 : 2 * LANES] = gd[0, 0:frames, 0 : 2 * LANES].astype(BF16)
    g = dot_tn(masked[...], dp[0:frames, 0 : 2 * LANES])
    g_lead = g[0:C, 0:LANES] + pltpu.roll(g[C : 2 * C, 0:LANES], LANES - half, 1)
    g_tail = pltpu.roll(g[0:C, LANES : 2 * LANES], half, 1) + g[C : 2 * C, LANES : 2 * LANES]
    g = jnp.where(first_half, g_lead, g_tail)
    g_dec = jnp.concatenate([g, jnp.zeros_like(g)], axis=0).T[0 : 2 * half]
    xj[frames : frames + 8] = jnp.zeros((8, LANES), F32)
    for q in range(5):
        r = q * hr
        dfr = dot_nt(dp[r : r + hr, 0 : 2 * LANES], dec_ref[...]) * pre[r : r + hr]
        xj[r : r + hr] = dfr
        dpre[r : r + hr] = dfr.astype(BF16)
    for q in range(5):
        r = q * hr
        dpre[frames + r : frames + r + hr] = (tile(next_not_first) * xj[r + 1 : r + 1 + hr]).astype(BF16)
    gm = dot_tn(feats[...], dpre[...])
    gm = jnp.where(speaker == 0, gm, pltpu.roll(gm, C, 1))
    n, at = 2 * blocks - 1, lay["head"]
    for q in range(4):
        sums[n, at : at + 16, q * LANES : (q + 1) * LANES] = gm[16 * q : 16 * q + 16].astype(BF16)
    sums[n, at + 16 : at + 32, 0:LANES] = jnp.where(lane < C, g_dec, 0.0).astype(BF16)
    sums[n, at + 16 : at + 32, LANES : 2 * LANES] = jnp.broadcast_to(gm[C : C + 1], (16, LANES)).astype(BF16)
    dz[...] = jnp.zeros_like(dz)

    def head_dz(r):
        x = stream[pl.ds(r, cr)]
        sg = 0.5 * jnp.tanh(0.5 * x) + 0.5
        df = dot_nt(dpre[pl.ds(r, cr)], mask_ref[...])
        df = jnp.concatenate([df, jnp.zeros_like(df)], axis=1)
        dz[pl.ds(r, cr)] = df * sg * (1.0 + x * (1.0 - sg))

    chunks(rows, cr, head_dz)

    def norm_backward(b, sec):
        n = 2 * b + sec
        gain = vec[n, 1:2]

        def sums(i, acc):
            r = pl.multiple_of(i * cr, cr)
            v = valid[pl.ds(r, cr)] * dz[pl.ds(r, cr)]
            w = v * normed[n, pl.ds(r, cr)]
            return (
                acc[0] + jnp.sum(v.reshape(cr // R, R, LANES), axis=0),
                acc[1] + jnp.sum(w.reshape(cr // R, R, LANES), axis=0),
            )

        zero = jnp.zeros((R, LANES), F32)
        s1, s2 = lax.fori_loop(0, rows // cr, sums, (zero, zero))
        small[1:2, LANES : 2 * LANES] = jnp.sum(s2, axis=0, keepdims=True)
        small[1:2, 2 * LANES : 3 * LANES] = jnp.sum(s1, axis=0, keepdims=True)
        m1 = clip_sum(s1 * gain) * inv_count
        m2 = clip_sum(s2 * gain) * inv_count
        inv = inv_all[n]

        def apply(i, acc):
            r = pl.multiple_of(i * cr, cr)
            d = (dz[pl.ds(r, cr)] * gain).reshape(cr // R, R, LANES)
            x = normed[n, pl.ds(r, cr)].reshape(cr // R, R, LANES)
            y = (d - m1[None] - x * m2[None]) * inv[None]
            y = (y.reshape(cr, LANES) * valid[pl.ds(r, cr)]).astype(BF16)
            if sec == 0:
                dmj[pl.ds(r, cr)] = y
            y = y.astype(F32)
            if sec == 1:
                mx[pl.ds(r, cr)] = y
            return acc + jnp.sum(y.reshape(cr // R, R, LANES), axis=0)

        acc = lax.fori_loop(0, rows // cr, apply, zero)
        small[1:2, 0:LANES] = jnp.sum(acc, axis=0, keepdims=True)

    def back_step(d, sv, b, r, n, dhn, dcn, keep):
        a = [sv[b, d, pl.ds(r, n), m * H : (m + 1) * H].astype(F32) for m in range(6)]
        g = dh[pl.ds(r, n), d * H : (d + 1) * H] + dhn
        dc = dcn + g * a[4]
        for m in range(4):
            dp[pl.ds(r, n), (4 * d + m) * H : (4 * d + m + 1) * H] = ((g if m == 3 else dc) * a[m]).astype(BF16)
        dhn = dot(dp[pl.ds(r, n), 4 * d * H : 4 * (d + 1) * H], wrt[d])
        dcn = dc * a[5]
        if keep is not None:
            dhn, dcn = dhn * keep, dcn * keep
        return dhn, dcn

    def run_backward(b, sec, u, hc, sv, n, steps, unroll, parts):
        total = n * steps
        out = sums.at[2 * b + sec]
        g = dot_tn(dmj[0:total], hc[b])[0:C].astype(BF16)
        at = lay["proj"]
        out[at : at + C // 2, 0 : 2 * H] = g[0 : C // 2]
        out[at : at + C // 2, 2 * H : 4 * H] = g[C // 2 : C]

        dh[0:total] = dot(dmj[0:total], pws[b, sec])
        for d in range(2):
            wrt[d] = w_rec_ref[b, sec, d].T
            wit[d * 4 * H : (d + 1) * 4 * H, 0:C] = w_in_ref[b, sec, d].T

        def step(t, carry):
            hf, hb, cf, cb = carry
            back = steps - 1 - t
            rf = pl.multiple_of(back * n, n)
            rb = pl.multiple_of(t * n, n)
            kf = kb = None
            if sec == 1:
                kf = 1.0 - is_start(back).astype(F32)
                kb = 1.0 - is_end(t).astype(F32)
            hf, cf = back_step(0, sv, b, rf, n, hf, cf, kf)
            hb, cb = back_step(1, sv, b, rb, n, hb, cb, kb)
            return hf, hb, cf, cb

        z = jnp.zeros((n, H), F32)
        carry = (z, z, z, z)
        point(2.5)
        for p in range(parts):
            carry = lax.fori_loop(p * steps // parts, (p + 1) * steps // parts, step, carry, unroll=unroll)
            point(steps * 0.125 / parts)
        if sec == 1:
            for j in range(1, steps):
                kf = (1.0 - is_start(j).astype(F32)).astype(BF16)
                at = slice((j - 1) * n, j * n)
                hc[b, at, 0:H] = hc[b, at, 0:H] * kf
                kb = (1.0 - is_end(j - 1).astype(F32)).astype(BF16)
                at = slice(j * n, (j + 1) * n)
                hc[b, at, H : 2 * H] = hc[b, at, H : 2 * H] * kb
        last = (b, sec) == (0, 0)
        core = place.bit(0)
        reduce = reduction(2 * b + sec, [[0], near + far] if b == 0 else [[0], near, far])
        for d in (1 - core, core):
            gates = pl.ds(pl.multiple_of(4 * d * H, H), 4 * H)
            g = dot_tn(u[b], dp[0:total, gates])
            base = d * lay["half"]
            out[pl.ds(pl.multiple_of(base + lay["in"], PART), C)] = g[0:C].astype(BF16)
            small[0:1] = g[C : C + 1]
            out[pl.ds(pl.multiple_of(base + lay["small"], PART), 16)] = small[...].astype(BF16)
            h_prev = hc[b, pl.ds(pl.multiple_of(d * n, n), total - n), pl.ds(pl.multiple_of(d * H, H), H)]
            g = dot_tn(h_prev, dp[pl.ds(pl.multiple_of((1 - d) * n, n), total - n), gates])
            out[pl.ds(pl.multiple_of(base + lay["rec"], PART), H)] = g.astype(BF16)
            if d is core:
                point(0.6)
            else:
                reduce.advance(clock[0] + 0.6)
                active.append(reduce)

    def stream_grad(total):
        return dot(dp[0:total], wit[...])

    small[...] = jnp.zeros_like(small)
    for b in reversed(range(blocks)):
        norm_backward(b, 1)
        mx[rows:rows_e] = jnp.zeros((rows_e - rows, LANES), F32)
        for j in range(R):
            dmj[pl.ds(j * kp, kp)] = mx[pl.ds(j, kp, stride=R), :].astype(BF16)
        run_backward(b, 1, u_e, hc_e, sv_e, kp, R, R, 1)

        xj[...] = stream_grad(rows_e)
        for k in range(K):
            dz[k * R : (k + 1) * R] += xj[pl.ds(k, R, stride=kp), :]
        point(1.5)

        norm_backward(b, 0)
        run_backward(b, 0, u_a, hc_a, sv_a, R, K, 10, 5)

        dz[0:rows] += stream_grad(rows)
        point(1.5)

    def finish(r):
        dz[pl.ds(r, cr)] = dz[pl.ds(r, cr)] * valid[pl.ds(r, cr)]

    chunks(rows, cr, finish)
    for j in range(R):
        grad_spans[j] = dz[pl.ds(j, K, stride=R), :].T[0:C]
    exits = [pltpu.make_async_copy(grad_spans, spans_out, out_sems.at[2 * blocks])]
    exits[0].start()
    wave_swap.wait()
    for i in range(wr):
        at = pl.multiple_of(speaker * (wr * LANES) + i * LANES, LANES)
        wave_out[0:1, pl.ds(at, LANES)] = own[i : i + 1]
        at = pl.multiple_of((1 - speaker) * (wr * LANES) + i * LANES, LANES)
        wave_out[0:1, pl.ds(at, LANES)] = wave_got[i : i + 1]

    left = list(active)
    while left:
        for reduce in [reduce for reduce in left if reduce.over()]:
            n = reduce.number
            exits.append(pltpu.make_async_copy(all_sums.at[n], sums_out.at[n], out_sems.at[n]))
            exits[-1].start()
            left.remove(reduce)
        if left:
            nearest = min(left, key=lambda reduce: reduce.due)
            clock[0] = max(clock[0], nearest.due)
            nearest.advance(clock[0])
    for copy in exits:
        copy.wait()


def unpack_kernel(
    sizes,
    sums,
    wave_in,
    spans_in,
    wave_out,
    spans_out,
    in_out,
    rec_out,
    bias_out,
    proj_out,
    proj_bias_out,
    gain_out,
    shift_out,
    mask_out,
    mask_bias_out,
    dec_out,
):
    C, H = sizes
    lay = sum_rows(C, H)
    n = pl.program_id(0)
    b, sec = n // 2, n % 2
    speaker = lax.axis_index("spk")
    spans_out[...] = spans_in[...]
    for d in range(2):
        base = d * lay["half"]
        in_out[d] = sums[base + lay["in"] : base + lay["in"] + C].astype(F32)
        rec_out[d] = sums[base + lay["rec"] : base + lay["rec"] + H].astype(F32)
        small = sums[base + lay["small"] : base + lay["small"] + 16].astype(F32)
        bias_out[d : d + 1] = small[0:1]
        if d == 0:
            for m, out in enumerate((proj_bias_out, gain_out, shift_out)):
                out[b, pl.ds(sec, 1)] = small[1:2, m * LANES : m * LANES + C]
    at = lay["proj"]
    proj_out[0 : C // 2] = sums[at : at + C // 2, 0 : 2 * H].astype(F32)
    proj_out[C // 2 : C] = sums[at : at + C // 2, 2 * H : 4 * H].astype(F32)

    @pl.when(n == 0)
    def _():
        wave_out[...] = wave_in[...]

    @pl.when(n == pl.num_programs(0) - 1)
    def _():
        at = lay["head"]

        def own(x):
            return jnp.where(speaker == 0, x, pltpu.roll(x, C, 1))[:, 0:C]

        for q in range(4):
            x = sums[at : at + 16, q * LANES : (q + 1) * LANES].astype(F32)
            mask_out[0, 16 * q : 16 * q + 16] = own(x)
        x = sums[at + 16 : at + 32, 0 : 2 * LANES].astype(F32)
        mask_bias_out[...] = own(x[:, LANES : 2 * LANES])[0:1]
        dec_out[...] = x[:, 0:C]


def sum_rows(C, H):
    lay, at = {}, 0
    for name, rows in (("in", C), ("rec", H), ("small", 16), ("proj", C // 2)):
        lay[name] = at
        at += rows
    lay["half"] = -(-at // (16 * PART)) * 16 * PART
    lay["head"] = lay["half"] + lay["proj"]
    lay["total"] = 2 * lay["half"]
    return lay


def shards(
    num_dp,
    spans,
    encoded,
    clip_lengths,
    clip_pads,
    lstm_in,
    lstm_rec,
    lstm_bias,
    proj_weight,
    proj_bias,
    gln_gain,
    gln_shift,
    mask_weight,
    mask_bias,
    dec_weight,
    wave_grad,
):
    R, K, C = spans.shape
    H = lstm_rec.shape[3]
    blocks = lstm_in.shape[0]
    clips = clip_lengths.shape[2]
    frames = encoded.shape[0]
    half = dec_weight.shape[1] // 2
    kp = -(-K // 16) * 16
    rows, rows_e = R * K, R * kp
    wr = frames * half // LANES
    mask_row = -(-wr // 8) * 8

    sizes = (R, K, C, H, clips, blocks, kp, num_dp)
    lay = sum_rows(C, H)
    outer = max(num_dp.bit_length() - 5, 0)
    smem = pl.BlockSpec(memory_space=pltpu.SMEM)
    vmem = pl.BlockSpec(memory_space=pltpu.VMEM)
    shape = jax.ShapeDtypeStruct
    outs = pl.pallas_call(
        functools.partial(local_kernel, sizes),
        out_shape=(
            shape((1, 2 * frames * half), F32),
            shape((R, C, K), F32),
            shape((2 * blocks, lay["total"], 4 * H), BF16),
        ),
        in_specs=[smem, smem] + [vmem] * 13,
        out_specs=(vmem, pl.BlockSpec(memory_space=pl.ANY), pl.BlockSpec(memory_space=pl.ANY)),
        scratch_shapes=[
            pltpu.VMEM((rows_e, LANES), F32),
            pltpu.VMEM((rows, LANES), F32),
            pltpu.VMEM((rows_e, LANES), F32),
            pltpu.VMEM((rows_e, LANES), F32),
            pltpu.VMEM((rows_e, LANES), F32),
            pltpu.VMEM((rows_e, LANES), BF16),
            pltpu.VMEM((2 * blocks, rows, LANES), F32),
            pltpu.VMEM((2 * blocks, R, LANES), F32),
            pltpu.VMEM((blocks, rows, LANES), BF16),
            pltpu.VMEM((blocks, rows_e, LANES), BF16),
            pltpu.VMEM((blocks, rows, 2 * H), BF16),
            pltpu.VMEM((blocks, rows_e, 2 * H), BF16),
            pltpu.VMEM((blocks, 2, rows, 6 * H), BF16),
            pltpu.VMEM((blocks, 2, rows_e, 6 * H), BF16),
            pltpu.VMEM((2, frames, 2 * LANES), F32),
            pltpu.VMEM((rows_e, 2 * H), F32),
            pltpu.VMEM((rows_e, 8 * H), BF16),
            pltpu.VMEM((2, 2 * H, 4 * H), BF16),
            pltpu.VMEM((8 * H, LANES), BF16),
            pltpu.VMEM((2, 4 * H, H), BF16),
            pltpu.VMEM((blocks, 2, LANES, 2 * H), BF16),
            pltpu.VMEM((2 * blocks, 8, LANES), F32),
            pltpu.VMEM((frames, LANES), F32),
            pltpu.VMEM((rows, LANES), F32),
            pltpu.VMEM((frames, LANES), BF16),
            pltpu.VMEM((rows, LANES), BF16),
            pltpu.VMEM((rows, LANES), BF16),
            pltpu.VMEM((C, 2 * C), BF16),
            pltpu.VMEM((2 * C, 2 * LANES), BF16),
            pltpu.VMEM((mask_row + C + 8, LANES), F32),
            pltpu.VMEM((mask_row, LANES), F32),
            pltpu.VMEM((mask_row + C + 8, LANES), F32),
            pltpu.VMEM((mask_row, LANES), F32),
            pltpu.SemaphoreType.DMA((4,)),
            pltpu.VMEM((2 * blocks, lay["total"], 4 * H), BF16),
            pltpu.VMEM((2 * blocks, lay["total"] + PART * outer, 4 * H), BF16),
            pltpu.VMEM((16, 4 * H), F32),
            pltpu.SemaphoreType.DMA((2 * blocks, 6 + outer, 2)),
            pltpu.VMEM((2 * blocks, lay["total"], 4 * H), BF16),
            pltpu.VMEM((R, C, K), F32),
            pltpu.SemaphoreType.DMA((2 * blocks + 1,)),
        ],
        compiler_params=pltpu.CompilerParams(
            vmem_limit_bytes=62 * 1024 * 1024, collective_id=0, has_side_effects=True
        ),
        name="dual_path",
    )(
        clip_lengths,
        clip_pads,
        spans.transpose(0, 2, 1),
        encoded.T,
        lstm_in,
        lstm_rec,
        lstm_bias,
        proj_weight.transpose(0, 1, 3, 2),
        proj_bias,
        gln_gain,
        gln_shift,
        mask_weight,
        mask_bias,
        dec_weight.T,
        wave_grad,
    )
    half = dec_weight.shape[1] // 2
    per_section = pl.BlockSpec((None, lay["total"], 4 * H), lambda n: (n, 0, 0))

    def whole(*dims):
        return pl.BlockSpec(dims, lambda n: (0,) * len(dims))

    def section(*dims):
        return pl.BlockSpec((None, None) + dims, lambda n: (n // 2, n % 2) + (0,) * len(dims))

    finals = pl.pallas_call(
        functools.partial(unpack_kernel, (C, H)),
        grid=(2 * blocks,),
        out_shape=(
            shape((1, 2 * frames * half), F32),
            shape((R, C, K), F32),
            shape((blocks, 2, 2, C, 4 * H), F32),
            shape((blocks, 2, 2, H, 4 * H), F32),
            shape((blocks, 2, 2, 4 * H), F32),
            shape((blocks, 2, C, 2 * H), F32),
            shape((blocks, 2, C), F32),
            shape((blocks, 2, C), F32),
            shape((blocks, 2, C), F32),
            shape((1, C, C), F32),
            shape((1, C), F32),
            shape((2 * half, C), F32),
        ),
        in_specs=[
            per_section,
            whole(1, 2 * frames * half),
            pl.BlockSpec((R // (2 * blocks), C, K), lambda n: (n, 0, 0)),
        ],
        out_specs=(
            whole(1, 2 * frames * half),
            pl.BlockSpec((R // (2 * blocks), C, K), lambda n: (n, 0, 0)),
            section(2, C, 4 * H),
            section(2, H, 4 * H),
            section(2, 4 * H),
            section(C, 2 * H),
            whole(blocks, 2, C),
            whole(blocks, 2, C),
            whole(blocks, 2, C),
            whole(1, C, C),
            whole(1, C),
            whole(2 * half, C),
        ),
        compiler_params=pltpu.CompilerParams(vmem_limit_bytes=60 * 1024 * 1024),
        name="unpack",
    )(outs[2], outs[0], outs[1])
    return (
        finals[0],
        finals[1].transpose(0, 2, 1),
        finals[2],
        finals[3],
        finals[4],
        finals[5].transpose(0, 1, 3, 2),
        finals[6],
        finals[7],
        finals[8],
        finals[9],
        finals[10],
        finals[11].T,
    )


def solution(mesh):
    return jax.shard_map(
        functools.partial(shards, mesh.shape["dp"]),
        mesh=mesh,
        in_specs=(
            P(("dp", "spk"), None, None),
            P(("dp", "spk"), None),
            P("dp", None, None),
            P("dp", None, None),
            P(),
            P(),
            P(),
            P(),
            P(),
            P(),
            P(),
            P("spk", None, None),
            P("spk", None),
            P(),
            P("spk", "dp"),
        ),
        out_specs=(
            P("spk", "dp"),
            P(("dp", "spk"), None, None),
            P(),
            P(),
            P(),
            P(),
            P(),
            P(),
            P(),
            P("spk", None, None),
            P("spk", None),
            P(),
        ),
        check_vma=False,
    )
```
